32 devices in a mesh: expert: 8 (over y, x, core), hidden: 4 (over z).
Axes of the slice: x: 2, y: 2, z: 4, core: 2. Of those that a mesh axis runs over, the one named last changes fastest.
Arguments:
- tokens: bfloat16 [32768, 512], P(('expert', 'hidden')), may hold values from -6 to 6
- cotangent: bfloat16 [32768, 512], P(('expert', 'hidden')), may hold values from -6 to 6
- w_qkv: bfloat16 [512, 1536], replicated, may hold values from -0.25 to 0.25
- bias_qv: float32 [2, 512], replicated, may hold values from -1.5 to 1.5
- w_out: bfloat16 [512, 512], replicated, may hold values from -0.75 to 0.75
- out_bias: float32 [512], replicated, may hold values from -1.5 to 1.5
- norm_gains: float32 [2, 512], replicated, may hold values from 0.25 to 1.75
- norm_shifts: float32 [2, 512], replicated, may hold values from -1.5 to 1.5
- gate_table: float32 [30, 2], replicated, may hold values from -3 to 3
- w_in: bfloat16 [8, 512, 2048], P('expert', None, 'hidden'), may hold values from -0.25 to 0.25
- w_down: bfloat16 [8, 2048, 512], P('expert', 'hidden'), may hold values from -0.125 to 0.125
- lengths: int32 [32, 32], P(('expert', 'hidden')), may hold values from 1 to 64, 1024 in all within a row
- seg_task: int32 [32, 32], P(('expert', 'hidden')), may hold values from 0 to 29
- routes: int32 [30, 2], replicated, may hold values from 0 to 7, all different within a row
Outputs:
- layer_out: bfloat16 [32768, 512], P(('expert', 'hidden'))
- input_grad: bfloat16 [32768, 512], P(('expert', 'hidden'))
- grad_qkv: float32 [512, 1536], replicated
- grad_bias_qv: float32 [2, 512], replicated
- grad_out: float32 [512, 512], replicated
- grad_out_bias: float32 [512], replicated
- grad_gains: float32 [2, 512], replicated
- grad_shifts: float32 [2, 512], replicated
- grad_gate: float32 [30, 2], replicated
- grad_w_in: float32 [8, 512, 2048], P('expert', None, 'hidden')
- grad_w_down: float32 [8, 2048, 512], P('expert', 'hidden')
The draws below stay inside these ranges and needn't reach their ends.
Inputs may be any that keep to these rules, and one draw needn't show every extreme that they name: Each pack's 32 sentence lengths sum to 1024; every pack has one sentence of exactly 64 tokens. `routes`: each task names 2 different experts; every expert is named by some task.
All inputs are finite; a program needn't handle non-finite values.
Results may differ from the reference program's by a relative error of at most 0.017.
Values may be sent and summed in bfloat16 or wider, within the bound.
No kernel may reach another device: no remote copies, remote signals or barrier semaphores. Data moves between devices by JAX's collectives and lax.ppermute only.
A program may use at most 384 MiB of HBM per device.

```python
import math
import jax
import jax.numpy as jnp
import numpy as np
from jax import lax

D = 512
HEADS = 8
HD = 64
FF = 2048
TASKS = 30
TOP = 2
PACK = 1024
SEGS = 32
MOST = 64
EXPERTS = 8
PACKS = 32
TOKENS = 32768
CAP = 384
N_EXPERT = 8
N_HIDDEN = 4


def place_ends(values, rng, low, high):
    spot = [jax.random.randint(jax.random.fold_in(rng, axis), (), 0, length) for axis, length in enumerate(values.shape)]
    widest = values.shape.index(max(values.shape))
    neighbour = spot[:widest] + [(spot[widest] + 1) % values.shape[widest]] + spot[widest + 1:]
    return values.at[tuple(spot)].set(low).at[tuple(neighbour)].set(high)


def block_scale(key, extent, cuts, least, largest):
    level = 1.0
    for dim, shards_of in cuts:
        steps = jax.random.uniform(jax.random.fold_in(jax.random.fold_in(key, 6), dim), (shards_of,), jnp.float32, least / len(cuts), largest / len(cuts))
        level = level * jnp.repeat(jnp.exp(steps), extent[dim] // shards_of).reshape((-1,) + (1,) * (len(extent) - 1 - dim))
    return level


def cumulative_ranks(amount, skew):
    loads = [(1 << 20) // math.isqrt(standing ** skew) + 1 for standing in range(1, amount + 1)]
    width = 1 + sum(loads) // (1 << 30)
    return np.cumsum(np.array([max(1, weight // width) for weight in loads]))


def ranked(key, dims, count, skew):
    table = cumulative_ranks(count, skew)
    lot = jax.random.randint(jax.random.fold_in(key, 1), dims, 0, int(table[count - 1]))
    rank = jnp.searchsorted(jnp.asarray(table, jnp.int32), lot, side="right")
    return jax.random.permutation(jax.random.fold_in(key, 2), count)[rank].astype(jnp.int32)


def distinct(own_key, rows, amount, top, lift):
    sequence = jax.random.permutation(jax.random.fold_in(own_key, 1), amount)
    favour = sequence
    for power in range(3):
        favour = favour * favour // amount
    favour = favour * lift // amount
    tickets = jax.random.randint(jax.random.fold_in(own_key, 2), (rows, amount), 0, 4096) + favour
    sure = jax.random.permutation(jax.random.fold_in(own_key, 3), rows)[jnp.arange(amount) % rows]
    tickets = jnp.where(jnp.arange(rows)[:, None] == sure[None, :], 1 << 14, tickets)
    merit = tickets * amount + jnp.arange(amount)
    return lax.top_k(merit.astype(jnp.int32), top)[1].astype(jnp.int32)


def profile(number_of, total, most, skew):
    portions = [(1 << 20) // math.isqrt(standing ** skew) + 1 for standing in range(2, number_of + 1)]
    surplus, given = total - most - (number_of - 1), [1] * (number_of - 1)
    while surplus > 0:
        candidates = [i for i in range(number_of - 1) if given[i] < most]
        pool, budget = sum([portions[i] for i in candidates]), surplus
        for i in candidates:
            more = min(most - given[i], max(1, budget * portions[i] // pool), surplus)
            given[i] = given[i] + more
            surplus = surplus - more
    return np.array([most] + given)


def ragged(key, count, total, reach, slope):
    if count == 2:
        one = jax.random.randint(key, (), max(1, total - reach), min(reach, total - 1) + 1)
        return jnp.stack([one, total - one])
    tallies = jnp.asarray(profile(count, total, reach, slope), jnp.int32)
    twos = (count - 1) // 2
    source_of, taker = tallies[1:1 + 2 * twos:2], tallies[2:2 + 2 * twos:2]
    margin = jnp.minimum(source_of - 1, reach - taker)
    passed = jax.random.randint(jax.random.fold_in(key, 1), (twos,), 0, 1 << 20) % (margin + 1)
    tallies = tallies.at[1:1 + 2 * twos:2].set(source_of - passed).at[2:2 + 2 * twos:2].set(taker + passed)
    return tallies[jax.random.permutation(jax.random.fold_in(key, 2), count)]


def normal_values(stream_key, shape, scale, most, split=(), kind=jnp.bfloat16):
    array = jax.random.normal(stream_key, shape, jnp.float32) * scale
    if len(split) > 0:
        array = block_scale(stream_key, shape, split, -0.22, 0.18) * array
    return jnp.clip(array, min=-most, max=most).astype(kind)


def setup_inputs(seed: int = 0) -> dict:
    arg_keys = jax.random.split(jax.random.key(seed), 15)
    tokens = normal_values(arg_keys[0], (TOKENS, D), 1.0, 6.0, ((0, 32),))
    cotangent = normal_values(arg_keys[1], (TOKENS, D), 1.0, 6.0, ((0, 32),))
    w_qkv = normal_values(arg_keys[2], (D, 3 * D), D ** -0.5, 0.25)
    bias_qv = normal_values(arg_keys[3], (2, D), 0.3, 1.5, (), jnp.float32)
    w_out = normal_values(arg_keys[4], (D, D), (D // 8) ** -0.5, 0.75)
    out_bias = normal_values(arg_keys[5], (D,), 0.3, 1.5, (), jnp.float32)
    norm_gains = jnp.clip(1.0 + 0.15 * jax.random.normal(arg_keys[6], (2, D), jnp.float32), 0.25, 1.75)
    norm_shifts = normal_values(arg_keys[7], (2, D), 0.3, 1.5, (), jnp.float32)
    gate_table = normal_values(arg_keys[8], (TASKS, TOP), 0.7, 3.0, (), jnp.float32)
    w_in = normal_values(arg_keys[9], (EXPERTS, D, FF), D ** -0.5, 0.25, ((0, 8), (2, 4)))
    w_down = normal_values(arg_keys[10], (EXPERTS, FF, D), FF ** -0.5, 0.125, ((0, 8), (1, 4)))
    lengths = jax.vmap(lambda own: ragged(own, SEGS, PACK, MOST, 1))(jax.random.split(arg_keys[11], PACKS)).reshape((PACKS, SEGS)).astype(jnp.int32)
    seg_task = place_ends(ranked(arg_keys[12], (PACKS, SEGS), TASKS, 2), jax.random.fold_in(arg_keys[12], 3), 0, TASKS - 1).astype(jnp.int32)
    routes = distinct(arg_keys[13], TASKS, EXPERTS, TOP, 0)
    return {"tokens": tokens, "cotangent": cotangent, "w_qkv": w_qkv, "bias_qv": bias_qv, "w_out": w_out, "out_bias": out_bias, "norm_gains": norm_gains, "norm_shifts": norm_shifts, "gate_table": gate_table, "w_in": w_in, "w_down": w_down, "lengths": lengths, "seg_task": seg_task, "routes": routes}


@jax.custom_vjp
def low(v):
    return lax.optimization_barrier(v.astype(jnp.bfloat16)).astype(jnp.float32)

@jax.custom_vjp
def low_back(v):
    return v

def low_keep(v):
    return (low(v), None)

def low_pass(kept, grad):
    return (grad,)

def back_keep(v):
    return (v, None)

def back_low(kept, grad):
    return (low(grad),)
low.defvjp(low_keep, low_pass)
low_back.defvjp(back_keep, back_low)
NORM_EPS = 1e-05
MASK_FILL = -1000000000.0

def norm_rows(values, gain, shift):
    center = lax.optimization_barrier(jnp.mean(values, axis=-1, keepdims=True))
    centred = values - center
    spread = lax.optimization_barrier(jnp.mean(centred * centred, axis=-1, keepdims=True))
    return centred * lax.rsqrt(spread + NORM_EPS) * gain + shift

def matmul(left, right):
    return jnp.dot(left, right, precision=lax.Precision.HIGHEST)

def attend(packed, w_qkv, bias_qv):
    block, seg_pack = packed
    qkv = matmul(block, w_qkv)
    queries = low_back(low(qkv[:, :D] + bias_qv[0])).reshape(PACK, HEADS, HD)
    keyset = low_back(low(qkv[:, D:2 * D])).reshape(PACK, HEADS, HD)
    values = low_back(low(qkv[:, 2 * D:] + bias_qv[1])).reshape(PACK, HEADS, HD)
    raw_scores = jnp.einsum('qhc,khc->hqk', queries, keyset, precision=lax.Precision.HIGHEST) * HD ** (-0.5)
    same_seg = seg_pack[:, None] == seg_pack[None, :]
    scores = low_back(jnp.where(same_seg[None], raw_scores, MASK_FILL))
    soft_probs = low(jax.nn.softmax(scores, axis=-1))
    attended = jnp.einsum('hqk,khc->qhc', soft_probs, values, precision=lax.Precision.HIGHEST)
    return low_back(low(attended.reshape(PACK, D)))

def expert_rows(packed):
    rows_in, weight_in, weight_down = packed
    pre_act = low_back(matmul(rows_in, weight_in))
    active = low(jax.nn.gelu(pre_act, approximate=True))
    return matmul(active, weight_down)

def reference(tokens, cotangent, w_qkv, bias_qv, w_out, out_bias, norm_gains, norm_shifts, gate_table, w_in, w_down, lengths, seg_task, routes):
    devices_all = N_EXPERT * N_HIDDEN
    bounds = jnp.cumsum(lengths, axis=1, dtype=jnp.int32)
    places = jnp.arange(PACK, dtype=jnp.int32)
    segment = lax.optimization_barrier(jnp.sum((places[None, :, None] >= bounds[:, None, :]).astype(jnp.int32), axis=2, dtype=jnp.int32))
    task_tok = jnp.take_along_axis(seg_task, segment, axis=1).reshape(-1)
    chosen = routes[task_tok]
    flat_route = chosen.reshape(devices_all, -1)
    route_hits = (flat_route[:, :, None] == jnp.arange(EXPERTS, dtype=jnp.int32)[None, None, :]).astype(jnp.int32)
    before = jnp.cumsum(route_hits, axis=1, dtype=jnp.int32) - route_hits
    position = lax.optimization_barrier(jnp.sum(before * route_hits, axis=2, dtype=jnp.int32))
    row_width = EXPERTS * CAP + 1
    slot_index = jnp.where(position < CAP, flat_route * CAP + position, EXPERTS * CAP)
    global_index = (slot_index + jnp.arange(devices_all, dtype=jnp.int32)[:, None] * row_width).reshape(-1)

    def layer(inputs, wq, bq, wo, bo, gains, shifts, table, wa, wb):
        normed_one = low(norm_rows(inputs, gains[0], shifts[0]))

        def attend_one(packed):
            return attend(packed, wq, bq)
        attended = lax.map(jax.checkpoint(attend_one), (normed_one.reshape(PACKS, PACK, D), segment))
        attended = attended.reshape(TOKENS, D)
        hidden_state = inputs + low_back(matmul(attended, wo)) + bo
        normed_two = low(norm_rows(hidden_state, gains[1], shifts[1]))
        spread_rows = jnp.repeat(normed_two, TOP, axis=0)
        buffer = jnp.zeros((devices_all * row_width, D), jnp.float32).at[global_index].add(spread_rows)
        buffer = buffer.reshape(devices_all, row_width, D)[:, :EXPERTS * CAP].reshape(devices_all, EXPERTS, CAP, D)
        buffer = low_back(buffer)
        grouped = jnp.transpose(buffer, (1, 0, 2, 3)).reshape(EXPERTS, devices_all * CAP, D)
        results = lax.map(jax.checkpoint(expert_rows), (grouped, wa, wb))
        results = low_back(low(results))
        returned = jnp.transpose(results.reshape(EXPERTS, devices_all, CAP, D), (1, 0, 2, 3)).reshape(devices_all, EXPERTS * CAP, D)
        returned = jnp.concatenate([returned, jnp.zeros((devices_all, 1, D), jnp.float32)], axis=1).reshape(devices_all * row_width, D)
        picked = returned[global_index].reshape(TOKENS, TOP, D)
        gate_probs = jax.nn.softmax(table[task_tok], axis=-1)
        return hidden_state + lax.optimization_barrier(jnp.sum(gate_probs[:, :, None] * picked, axis=1))
    primals = (tokens.astype(jnp.float32), w_qkv.astype(jnp.float32), bias_qv, w_out.astype(jnp.float32), out_bias, norm_gains, norm_shifts, gate_table, w_in.astype(jnp.float32), w_down.astype(jnp.float32))
    result, pullback = jax.vjp(layer, *primals)
    grads = pullback(cotangent.astype(jnp.float32))
    return (result.astype(jnp.bfloat16), grads[0].astype(jnp.bfloat16), grads[1], grads[2], grads[3], grads[4], grads[5], grads[6], grads[7], grads[8], grads[9])
```

```python
import jax
import jax.numpy as jnp
from jax import lax
from jax.sharding import PartitionSpec as P

HEADS = 8
HD = 64


NORM_EPS = 1e-05
MASK_FILL = -1000000000.0


def norm_rows(values, gain, shift):
    center = jnp.mean(values, axis=-1, keepdims=True)
    centred = values - center
    spread = jnp.mean(centred * centred, axis=-1, keepdims=True)
    return centred * lax.rsqrt(spread + NORM_EPS) * gain + shift


def soft_gelu(values):
    return jax.nn.gelu(values, approximate=True)


def expert_back(inputs, grad_slots, weight_in, weight_down):
    pre_act = jnp.einsum("red,edf->ref", inputs, weight_in, preferred_element_type=jnp.float32)
    active, gelu_back = jax.vjp(soft_gelu, pre_act)
    active_low = active.astype(jnp.bfloat16)
    grad_active = jnp.einsum(
        "red,efd->ref", grad_slots, weight_down, preferred_element_type=jnp.float32
    )
    grad_pre = gelu_back(grad_active)[0].astype(jnp.bfloat16)
    grad_down = jnp.einsum(
        "ref,red->efd", active_low, grad_slots, preferred_element_type=jnp.float32
    )
    grad_in = jnp.einsum("red,ref->edf", inputs, grad_pre, preferred_element_type=jnp.float32)
    return (grad_pre, grad_in, grad_down)


def shards(
    tokens,
    cotangent,
    w_qkv,
    bias_qv,
    w_out,
    out_bias,
    norm_gains,
    norm_shifts,
    gate_table,
    w_in,
    w_down,
    lengths,
    seg_task,
    routes,
):
    packs_here, seg_count = lengths.shape
    tok_count, width_model = tokens.shape
    pack_len = tok_count // packs_here
    local_experts = w_in.shape[0]
    groups = lax.axis_size("expert")
    experts_all = local_experts * groups
    top_count = routes.shape[1]
    task_total = gate_table.shape[0]
    capacity = 3 * top_count * tok_count // (2 * experts_all)
    rows_here = groups * capacity
    score_scale = HD ** (-0.5)
    planes = lax.axis_size("hidden")
    down_shape = w_down.shape
    in_shape = w_in.shape
    w_in = lax.all_gather(w_in, "hidden", axis=2, tiled=True)
    w_down = lax.all_gather(w_down, "hidden", axis=1, tiled=True)
    places = jnp.arange(pack_len, dtype=jnp.int32)
    bounds = jnp.cumsum(lengths, axis=1, dtype=jnp.int32)
    segment = jnp.sum(
        (places[None, :, None] >= bounds[:, None, :]).astype(jnp.int32), axis=2, dtype=jnp.int32
    )
    seg_match = segment[:, :, None] == jnp.arange(seg_count, dtype=jnp.int32)[None, None, :]
    task_tok = jnp.sum(
        jnp.where(seg_match, seg_task[:, None, :], 0), axis=2, dtype=jnp.int32
    ).reshape(-1)
    task_onehot = task_tok[:, None] == jnp.arange(task_total, dtype=jnp.int32)[None, :]
    chosen = jnp.sum(
        jnp.where(task_onehot[:, :, None], routes[None, :, :], 0), axis=1, dtype=jnp.int32
    )
    task_float = task_onehot.astype(jnp.float32)
    logits = jnp.dot(task_float, gate_table, precision=lax.Precision.HIGHEST)
    gate_probs = jax.nn.softmax(logits, axis=-1)
    flat_route = chosen.reshape(-1)
    route_hits = (flat_route[:, None] == jnp.arange(experts_all, dtype=jnp.int32)[None, :]).astype(
        jnp.int32
    )
    before = jnp.cumsum(route_hits, axis=0, dtype=jnp.int32) - route_hits
    position = jnp.sum(before * route_hits, axis=1, dtype=jnp.int32)
    slot_index = jnp.where(
        position < capacity, flat_route * capacity + position, experts_all * capacity
    )
    token_float = tokens.astype(jnp.float32)
    normed_one = norm_rows(token_float, norm_gains[0], norm_shifts[0]).astype(jnp.bfloat16)
    qkv = jnp.dot(normed_one, w_qkv, preferred_element_type=jnp.float32)
    queries = (qkv[:, :width_model] + bias_qv[0]).astype(jnp.bfloat16)
    keyset = qkv[:, width_model : 2 * width_model].astype(jnp.bfloat16)
    values = (qkv[:, 2 * width_model :] + bias_qv[1]).astype(jnp.bfloat16)

    def by_pack(array):
        return array.reshape(packs_here, pack_len, HEADS, HD)

    def scores_of(query_pack, key_pack, seg_pack):
        raw_scores = (
            jnp.einsum("qhc,khc->hqk", query_pack, key_pack, preferred_element_type=jnp.float32)
            * score_scale
        )
        same_seg = seg_pack[:, None] == seg_pack[None, :]
        return jnp.where(same_seg[None], raw_scores, MASK_FILL)

    def forward_pack(packed):
        query_pack, key_pack, value_pack, seg_pack = packed
        scores = scores_of(query_pack, key_pack, seg_pack)
        row_peak = jnp.max(scores, axis=-1, keepdims=True)
        exp_total = jnp.sum(jnp.exp(scores - row_peak), axis=-1, keepdims=True)
        log_total = row_peak + jnp.log(exp_total)
        soft_probs = jnp.exp(scores - log_total).astype(jnp.bfloat16)
        attended = jnp.einsum(
            "hqk,khc->qhc", soft_probs, value_pack, preferred_element_type=jnp.float32
        )
        return (attended.astype(jnp.bfloat16), log_total)

    attended, log_totals = lax.map(
        forward_pack, (by_pack(queries), by_pack(keyset), by_pack(values), segment)
    )
    attended_flat = attended.reshape(tok_count, width_model)
    hidden_state = (
        token_float + jnp.dot(attended_flat, w_out, preferred_element_type=jnp.float32) + out_bias
    )
    normed_two, norm_back_two = jax.vjp(norm_rows, hidden_state, norm_gains[1], norm_shifts[1])
    normed_low = normed_two.astype(jnp.bfloat16)
    spread_rows = jnp.repeat(normed_low, top_count, axis=0)
    outgoing = (
        jnp.zeros((experts_all * capacity + 1, width_model), jnp.bfloat16)
        .at[slot_index]
        .set(spread_rows)
    )
    outgoing = outgoing[:-1].reshape(experts_all, capacity, width_model)
    arrived = lax.all_to_all(outgoing, "expert", split_axis=0, concat_axis=0, tiled=True)

    def to_rows(expert_block):
        return (
            expert_block.reshape(groups, local_experts, capacity, width_model)
            .transpose(0, 2, 1, 3)
            .reshape(rows_here, local_experts, width_model)
        )

    def from_rows(row_block):
        return (
            row_block.reshape(groups, capacity, local_experts, width_model)
            .transpose(0, 2, 1, 3)
            .reshape(experts_all, capacity, width_model)
        )

    expert_in = to_rows(arrived)
    pre_piece = jnp.einsum(
        "red,edf->ref",
        expert_in,
        w_in,
        preferred_element_type=jnp.float32,
    )
    active = soft_gelu(pre_piece).astype(jnp.bfloat16)
    row_piece = active
    expert_out = jnp.einsum(
        "ref,efd->red", row_piece, w_down, preferred_element_type=jnp.float32
    ).astype(jnp.bfloat16)
    returned = lax.all_to_all(
        from_rows(expert_out), "expert", split_axis=0, concat_axis=0, tiled=True
    )
    padded_back = jnp.concatenate(
        [returned.reshape(-1, width_model), jnp.zeros((1, width_model), jnp.bfloat16)], axis=0
    )
    picked = padded_back[slot_index].reshape(tok_count, top_count, width_model).astype(jnp.float32)
    layer_out = (hidden_state + jnp.sum(gate_probs[:, :, None] * picked, axis=1)).astype(
        jnp.bfloat16
    )
    grad_final = cotangent.astype(jnp.float32)
    gate_grad = jnp.sum(grad_final[:, None, :] * picked, axis=2)
    slot_grad = (
        (gate_probs[:, :, None] * grad_final[:, None, :])
        .astype(jnp.bfloat16)
        .reshape(-1, width_model)
    )
    grad_outgoing = (
        jnp.zeros((experts_all * capacity + 1, width_model), jnp.bfloat16)
        .at[slot_index]
        .set(slot_grad)
    )
    grad_outgoing = grad_outgoing[:-1].reshape(experts_all, capacity, width_model)
    grad_arrived = lax.all_to_all(grad_outgoing, "expert", split_axis=0, concat_axis=0, tiled=True)
    grad_rows = to_rows(grad_arrived)
    grad_pre, grad_w_in, grad_w_down = expert_back(expert_in, grad_rows, w_in, w_down)

    def over_planes(pieces):
        moved = lax.all_to_all(
            pieces.astype(jnp.bfloat16), "hidden", split_axis=0, concat_axis=0, tiled=True
        )
        return jnp.sum(moved.astype(jnp.float32), axis=0)

    grad_w_in = over_planes(
        grad_w_in.reshape(in_shape[:2] + (planes, in_shape[2])).transpose(2, 0, 1, 3)
    )
    grad_w_down = over_planes(
        grad_w_down.reshape((down_shape[0], planes) + down_shape[1:]).transpose(1, 0, 2, 3)
    )
    row_piece = grad_pre
    slot_input_grad = jnp.einsum(
        "ref,edf->red", row_piece, w_in, preferred_element_type=jnp.float32
    ).astype(jnp.bfloat16)
    grad_back = lax.all_to_all(
        from_rows(slot_input_grad), "expert", split_axis=0, concat_axis=0, tiled=True
    )
    grad_padded = jnp.concatenate(
        [grad_back.reshape(-1, width_model), jnp.zeros((1, width_model), jnp.bfloat16)], axis=0
    )
    grad_picked = (
        grad_padded[slot_index].reshape(tok_count, top_count, width_model).astype(jnp.float32)
    )
    grad_normed_two = jnp.sum(grad_picked, axis=1)
    grad_hidden_part, grad_gain_two, grad_shift_two = norm_back_two(grad_normed_two)
    grad_hidden = grad_final + grad_hidden_part
    gate_inner = jnp.sum(gate_probs * gate_grad, axis=-1, keepdims=True)
    grad_logits = gate_probs * (gate_grad - gate_inner)
    grad_table = jnp.einsum("tk,tr->kr", task_float, grad_logits, precision=lax.Precision.HIGHEST)
    grad_attn = grad_hidden.astype(jnp.bfloat16)
    grad_out_bias = jnp.sum(grad_hidden, axis=0)
    grad_w_out = jnp.einsum(
        "td,te->de", attended_flat, grad_attn, preferred_element_type=jnp.float32
    )
    grad_attended = jnp.einsum(
        "te,de->td", grad_attn, w_out, preferred_element_type=jnp.float32
    ).astype(jnp.bfloat16)

    def backward_pack(packed):
        query_pack, key_pack, value_pack, seg_pack, log_total, grad_pack = packed
        scores = scores_of(query_pack, key_pack, seg_pack)
        soft_probs = jnp.exp(scores - log_total)
        grad_probs = jnp.einsum(
            "qhc,khc->hqk", grad_pack, value_pack, preferred_element_type=jnp.float32
        )
        grad_values = jnp.einsum(
            "hqk,qhc->khc",
            soft_probs.astype(jnp.bfloat16),
            grad_pack,
            preferred_element_type=jnp.float32,
        )
        inner_sum = jnp.sum(soft_probs * grad_probs, axis=-1, keepdims=True)
        grad_scores = (soft_probs * (grad_probs - inner_sum)).astype(jnp.bfloat16)
        grad_queries = (
            jnp.einsum("hqk,khc->qhc", grad_scores, key_pack, preferred_element_type=jnp.float32)
            * score_scale
        )
        grad_keys = (
            jnp.einsum("hqk,qhc->khc", grad_scores, query_pack, preferred_element_type=jnp.float32)
            * score_scale
        )
        return (
            grad_queries.astype(jnp.bfloat16),
            grad_keys.astype(jnp.bfloat16),
            grad_values.astype(jnp.bfloat16),
        )

    grad_queries, grad_keys, grad_values = lax.map(
        backward_pack,
        (
            by_pack(queries),
            by_pack(keyset),
            by_pack(values),
            segment,
            log_totals,
            by_pack(grad_attended),
        ),
    )
    grad_queries = grad_queries.reshape(tok_count, width_model)
    grad_keys = grad_keys.reshape(tok_count, width_model)
    grad_values = grad_values.reshape(tok_count, width_model)
    grad_joined = jnp.concatenate([grad_queries, grad_keys, grad_values], axis=1)
    grad_qkv = jnp.einsum("td,te->de", normed_one, grad_joined, preferred_element_type=jnp.float32)
    grad_bias_qv = jnp.stack(
        [
            jnp.sum(grad_queries.astype(jnp.float32), axis=0),
            jnp.sum(grad_values.astype(jnp.float32), axis=0),
        ]
    )
    grad_normed_one = jnp.einsum(
        "te,de->td", grad_joined, w_qkv, preferred_element_type=jnp.float32
    )
    primal_one, norm_back_one = jax.vjp(norm_rows, token_float, norm_gains[0], norm_shifts[0])
    grad_token_part, grad_gain_one, grad_shift_one = norm_back_one(grad_normed_one)
    input_grad = (grad_hidden + grad_token_part).astype(jnp.bfloat16)
    grad_gains = jnp.stack([grad_gain_one, grad_gain_two])
    grad_shifts = jnp.stack([grad_shift_one, grad_shift_two])
    summed = lax.psum(
        (grad_qkv, grad_bias_qv, grad_w_out, grad_out_bias, grad_gains, grad_shifts, grad_table),
        ("expert", "hidden"),
    )
    return (
        layer_out,
        input_grad,
        summed[0],
        summed[1],
        summed[2],
        summed[3],
        summed[4],
        summed[5],
        summed[6],
        grad_w_in,
        grad_w_down,
    )


def solution(mesh):
    return jax.shard_map(
        shards,
        mesh=mesh,
        in_specs=(
            P(("expert", "hidden"), None),
            P(("expert", "hidden"), None),
            P(),
            P(),
            P(),
            P(),
            P(),
            P(),
            P(),
            P("expert", None, "hidden"),
            P("expert", "hidden", None),
            P(("expert", "hidden"), None),
            P(("expert", "hidden"), None),
            P(),
        ),
        out_specs=(
            P(("expert", "hidden"), None),
            P(("expert", "hidden"), None),
            P(),
            P(),
            P(),
            P(),
            P(),
            P(),
            P(),
            P("expert", None, "hidden"),
            P("expert", "hidden", None),
        ),
        check_vma=False,
    )
```

```python
import functools

import jax
import jax.numpy as jnp
from jax import lax
from jax.experimental import pallas as pl
from jax.experimental.pallas import tpu as pltpu
from jax.sharding import PartitionSpec as P

HEADS = 8
HD = 64
NORM_EPS = 1e-05
MASK_FILL = -1000000000.0

BF = jnp.bfloat16
F32 = jnp.float32
MIB = 1 << 20

ROWS = 256
QROWS = 128
REACH = 64
KROWS = QROWS + 2 * REACH
PAIR = 2 * HD


def iota(shape, dim):
    return lax.broadcasted_iota(jnp.int32, shape, dim)


def dot(left, right):
    return jnp.dot(left, right, preferred_element_type=F32)


def dot_nt(left, right):
    return lax.dot_general(left, right, (((1,), (1,)), ((), ())), preferred_element_type=F32)


def dot_tn(left, right):
    return lax.dot_general(left, right, (((0,), (0,)), ((), ())), preferred_element_type=F32)


def over_lanes(mask, values):
    return jnp.sum(jnp.where(mask, values, 0.0), axis=1, keepdims=True)


def over_rows(mask, values):
    return jnp.sum(jnp.where(mask, values, 0.0), axis=0, keepdims=True)


def to_column(row):
    count = row.shape[1]
    return over_lanes(iota((count, count), 0) == iota((count, count), 1), row)


def centred_of(values):
    centred = values - jnp.mean(values, axis=-1, keepdims=True)
    spread = jnp.mean(centred * centred, axis=-1, keepdims=True)
    return centred * lax.rsqrt(spread + NORM_EPS), lax.rsqrt(spread + NORM_EPS)


def norm_back(grad, hat, scale, gain):
    scaled = grad * gain
    return scale * (
        scaled
        - jnp.mean(scaled, axis=-1, keepdims=True)
        - hat * jnp.mean(scaled * hat, axis=-1, keepdims=True)
    )


def sentence_bounds(lengths_ref):
    len_row = lengths_ref[...].astype(F32)
    count = len_row.shape[1]
    len_col = to_column(len_row)
    below = iota((count, count), 1) < iota((count, count), 0)
    above = iota((count, count), 0) < iota((count, count), 1)
    start_col = over_lanes(below, len_row)
    start_row = over_rows(above, len_col)
    return (len_row, len_col, start_row, start_col)


def routing(lengths_ref, task_ref, routes_ref, table_ref, me, capacity):
    len_row, len_col, start_row, start_col = sentence_bounds(lengths_ref)
    count = len_row.shape[1]
    tasks = routes_ref.shape[0]
    hit = iota((tasks, count), 0) == task_ref[...]
    expert_rows = [over_rows(hit, routes_ref[:, r : r + 1].astype(F32)) for r in range(2)]
    logit_rows = [over_rows(hit, table_ref[:, r : r + 1]) for r in range(2)]
    peak = jnp.maximum(logit_rows[0], logit_rows[1])
    raised = [jnp.exp(row - peak) for row in logit_rows]
    gate_rows = [row / (raised[0] + raised[1]) for row in raised]
    expert_cols = [to_column(row) for row in expert_rows]
    earlier = iota((count, count), 0) < iota((count, count), 1)
    add_rows, far_rows = [], []
    for row in expert_rows:
        same = (expert_cols[0] == row) | (expert_cols[1] == row)
        add_rows.append(over_rows(earlier & same, len_col) - start_row)
        far_rows.append((row.astype(jnp.int32) ^ me).astype(F32))
    return (len_row, len_col, start_row, start_col, far_rows, gate_rows, add_rows)


def dispatch_body(
    weighted, capacity, me_ref, len_ref, task_ref, routes_ref, table_ref, data_ref, *out_refs
):
    me = me_ref[0]
    tables = routing(len_ref, task_ref, routes_ref, table_ref, me, capacity)
    len_row, len_col, start_row, start_col, far_rows, gate_rows, add_rows = tables
    tok_count = data_ref.shape[0]
    count = len_row.shape[1]
    place = iota((count, tok_count), 1).astype(F32)
    inside = (place >= start_col) & (place < start_col + len_col)
    token_place = iota((1, tok_count), 1).astype(F32)

    def per_token(row):
        return over_rows(inside, to_column(row))

    far = [per_token(row) for row in far_rows]
    position = [token_place + per_token(row) for row in add_rows]
    gates = [per_token(row) for row in gate_rows]
    data = data_ref[...]
    slots = iota((capacity, tok_count), 0)
    for k, out_ref in enumerate(out_refs):
        first = far[0] == k
        slot = jnp.where(first, position[0], jnp.where(far[1] == k, position[1], -1.0))
        hit = slots == slot.astype(jnp.int32)
        picked = dot(hit.astype(F32).astype(BF), data)
        if weighted:
            picked = picked * over_lanes(hit, jnp.where(first, gates[0], gates[1]))
        out_ref[...] = picked.astype(BF)


def dispatch(weighted, capacity, groups, me, lengths, seg_task, routes, gate_table, data):
    tok_count, width = data.shape
    whole = pl.BlockSpec(memory_space=pltpu.VMEM)
    return pl.pallas_call(
        functools.partial(dispatch_body, weighted, capacity),
        out_shape=[jax.ShapeDtypeStruct((capacity, width), BF)] * groups,
        in_specs=[pl.BlockSpec(memory_space=pltpu.SMEM)] + [whole] * 5,
        out_specs=[whole] * groups,
        compiler_params=pltpu.CompilerParams(vmem_limit_bytes=40 * MIB),
        cost_estimate=pl.CostEstimate(
            flops=2 * groups * capacity * tok_count * width,
            bytes_accessed=2 * width * (tok_count + groups * capacity),
            transcendentals=0,
        ),
        name="dispatch_grads" if weighted else "dispatch_rows",
    )(me, lengths, seg_task, routes, gate_table, data)


def window_start(block, tok_count):
    start = jnp.clip(block * QROWS - REACH, 0, tok_count - KROWS)
    return pl.multiple_of(start, REACH)


def split_heads(block):
    low = iota(block.shape, 1) < HD
    zero = jnp.zeros_like(block)
    return jnp.concatenate([jnp.where(low, block, zero), jnp.where(low, zero, block)], axis=0)


def join_heads(stacked):
    half = stacked.shape[0] // 2
    low = iota((half, stacked.shape[1]), 1) < HD
    return jnp.where(low, stacked[:half], stacked[half:])


def attend_body(
    len_ref,
    tok_ref,
    wqkv_ref,
    bias_ref,
    wout_ref,
    obias_ref,
    gains_ref,
    shifts_ref,
    qkv_ref,
    att_ref,
    hid_ref,
    one_ref,
    two_ref,
):
    tok_count, width = tok_ref.shape
    len_row, len_col, start_row, start_col = sentence_bounds(len_ref)
    end_row, end_col = start_row + len_row, start_col + len_col
    count = len_row.shape[1]

    def project(step, carry):
        rows = pl.ds(pl.multiple_of(step * ROWS, ROWS), ROWS)
        hat, _ = centred_of(tok_ref[rows, :].astype(F32))
        one = (hat * gains_ref[0:1, :] + shifts_ref[0:1, :]).astype(BF)
        one_ref[rows, :] = one
        qkv = dot(one, wqkv_ref[...])
        queries = (qkv[:, :width] + bias_ref[0:1, :]).astype(BF)
        qkv_ref[rows, :width] = queries * jnp.asarray(HD**-0.5, BF)
        qkv_ref[rows, width : 2 * width] = qkv[:, width : 2 * width].astype(BF)
        qkv_ref[rows, 2 * width :] = (qkv[:, 2 * width :] + bias_ref[1:2, :]).astype(BF)
        return carry

    lax.fori_loop(0, tok_count // ROWS, project, 0)

    def attend(block, carry):
        rows = pl.ds(pl.multiple_of(block * QROWS, QROWS), QROWS)
        start = window_start(block, tok_count)
        keys = pl.ds(start, KROWS)
        key_place = (iota((count, KROWS), 1) + start).astype(F32)
        key_seg = jnp.sum((key_place >= end_col).astype(F32), axis=0, keepdims=True)
        query_place = (iota((QROWS, count), 0) + block * QROWS).astype(F32)
        query_seg = jnp.sum((query_place >= end_row).astype(F32), axis=1, keepdims=True)
        same = key_seg == query_seg
        same = jnp.concatenate([same, same], axis=0)
        for pair in range(width // PAIR):
            lanes = slice(pair * PAIR, (pair + 1) * PAIR)
            stacked = split_heads(qkv_ref[rows, lanes])
            key_rows = qkv_ref[keys, slice(width + lanes.start, width + lanes.stop)]
            value_rows = qkv_ref[keys, slice(2 * width + lanes.start, 2 * width + lanes.stop)]
            scores = jnp.where(same, dot_nt(stacked, key_rows), MASK_FILL)
            raised = jnp.exp(scores - jnp.max(scores, axis=1, keepdims=True))
            total = jnp.sum(raised, axis=1, keepdims=True)
            probs = (raised * (1.0 / total)).astype(BF)
            att_ref[rows, lanes] = join_heads(dot(probs, value_rows)).astype(BF)
        return carry

    lax.fori_loop(0, tok_count // QROWS, attend, 0)

    def finish(step, carry):
        rows = pl.ds(pl.multiple_of(step * ROWS, ROWS), ROWS)
        hidden = tok_ref[rows, :].astype(F32) + dot(att_ref[rows, :], wout_ref[...]) + obias_ref[...]
        hid_ref[rows, :] = hidden
        hat, _ = centred_of(hidden)
        two_ref[rows, :] = (hat * gains_ref[1:2, :] + shifts_ref[1:2, :]).astype(BF)
        return carry

    lax.fori_loop(0, tok_count // ROWS, finish, 0)


def attend_forward(lengths, tokens, w_qkv, bias_qv, w_out, out_bias, gains, shifts):
    tok_count, width = tokens.shape
    whole = pl.BlockSpec(memory_space=pltpu.VMEM)
    return pl.pallas_call(
        attend_body,
        out_shape=[
            jax.ShapeDtypeStruct((tok_count, 3 * width), BF),
            jax.ShapeDtypeStruct((tok_count, width), BF),
            jax.ShapeDtypeStruct((tok_count, width), F32),
            jax.ShapeDtypeStruct((tok_count, width), BF),
            jax.ShapeDtypeStruct((tok_count, width), BF),
        ],
        in_specs=[whole] * 8,
        out_specs=[whole] * 5,
        compiler_params=pltpu.CompilerParams(vmem_limit_bytes=40 * MIB),
        cost_estimate=pl.CostEstimate(
            flops=8 * tok_count * width * width + 16 * tok_count * KROWS * width,
            bytes_accessed=20 * tok_count * width,
            transcendentals=tok_count * KROWS * HEADS,
        ),
        name="attend_forward",
    )(lengths, tokens, w_qkv, bias_qv, w_out, out_bias.reshape(1, width), gains, shifts)


GELU_A = 0.7978845608028654
GELU_B = 0.044715


def gelu_both(values):
    square = values * values
    inner = values * (GELU_A + (GELU_A * GELU_B) * square)
    half = 0.5 * jnp.tanh(inner) + 0.5
    active = values * half
    slope = half + active * (1.0 - half) * (2.0 * GELU_A + (6.0 * GELU_A * GELU_B) * square)
    return active, slope


def load_all(pairs, sem):
    copies = [pltpu.make_async_copy(source, target, sem.at[i]) for i, (source, target) in enumerate(pairs)]
    for copy in copies:
        copy.start()
    for copy in copies:
        copy.wait()


def expert_body(blocks, planes, *refs):
    refs = list(refs)
    take = lambda count: [refs.pop(0) for _ in range(count)]
    x_in, g_in = take(blocks), take(blocks)
    w_in, w_down = take(planes), take(planes)
    out_refs, dx_refs = take(blocks), take(blocks)
    act_ref, pre_ref, xt_ref, gt_ref = take(4)
    xs, gs, sem = take(3)
    cap = x_in[0].shape[0]
    hid = w_in[0].shape[1]
    spots = [pl.ds(i * cap, cap) for i in range(blocks)]
    load_all(
        [(ref, xs.at[spot]) for ref, spot in zip(x_in, spots)]
        + [(ref, gs.at[spot]) for ref, spot in zip(g_in, spots)],
        sem,
    )
    x, g = xs[...], gs[...]
    out = dx = None
    for c in range(planes):
        lanes = slice(c * hid, (c + 1) * hid)
        active, slope = gelu_both(dot(x, w_in[c][...]))
        active = active.astype(BF)
        grad_pre = (dot_nt(g, w_down[c][...]) * slope).astype(BF)
        act_ref[:, lanes] = active
        pre_ref[:, lanes] = grad_pre
        new_out = dot(active, w_down[c][...])
        new_dx = dot_nt(grad_pre, w_in[c][...])
        out = new_out if out is None else out + new_out
        dx = new_dx if dx is None else dx + new_dx
    for i, spot in enumerate(spots):
        dx_refs[i][...] = dx[i * cap : (i + 1) * cap].astype(BF)
        out_refs[i][...] = out[i * cap : (i + 1) * cap].astype(BF)
    xt_ref[...] = x.T
    gt_ref[...] = g.T


def expert_rows(x_blocks, g_blocks, w_in, w_down):
    blocks, planes = len(x_blocks), len(w_in)
    cap, width = x_blocks[0].shape
    hid = w_in[0].shape[1]
    rows = blocks * cap
    whole = pl.BlockSpec(memory_space=pltpu.VMEM)
    anywhere = pl.BlockSpec(memory_space=pl.ANY)
    slot = jax.ShapeDtypeStruct((cap, width), BF)
    units = jax.ShapeDtypeStruct((rows, planes * hid), BF)
    turned = jax.ShapeDtypeStruct((width, rows), BF)
    result = pl.pallas_call(
        functools.partial(expert_body, blocks, planes),
        out_shape=[slot] * (2 * blocks) + [units] * 2 + [turned] * 2,
        in_specs=[anywhere] * (2 * blocks) + [whole] * (2 * planes),
        out_specs=[whole] * (2 * blocks + 4),
        scratch_shapes=[
            pltpu.VMEM((rows, width), BF),
            pltpu.VMEM((rows, width), BF),
            pltpu.SemaphoreType.DMA((2 * blocks,)),
        ],
        compiler_params=pltpu.CompilerParams(vmem_limit_bytes=56 * MIB),
        cost_estimate=pl.CostEstimate(
            flops=8 * rows * width * planes * hid,
            bytes_accessed=4 * rows * planes * hid + 12 * rows * width,
            transcendentals=rows * planes * hid,
        ),
        name="expert_rows",
    )(*x_blocks, *g_blocks, *w_in, *w_down)
    return (
        result[:blocks],
        result[blocks : 2 * blocks],
        result[2 * blocks],
        result[2 * blocks + 1],
        result[2 * blocks + 2],
        result[2 * blocks + 3],
    )


def weight_body(calls, *refs):
    act, pre, xt, gt = (refs[i * calls : (i + 1) * calls] for i in range(4))
    out_ref = refs[4 * calls]
    width = xt[0].shape[0]
    grad_in = grad_down = None
    for i in range(calls):
        new_in = dot(xt[i][...], pre[i][...])
        new_down = dot(gt[i][...], act[i][...])
        grad_in = new_in if grad_in is None else grad_in + new_in
        grad_down = new_down if grad_down is None else grad_down + new_down
    out_ref[0, :width, :] = grad_in.astype(out_ref.dtype)
    out_ref[0, width:, :] = grad_down.astype(out_ref.dtype)


def weight_grads(first, count, planes, dtype, act, pre, xt, gt):
    calls = len(act)
    width, rows = xt[0].shape
    hid = act[0].shape[1] // planes
    units = pl.BlockSpec((rows, hid), lambda i: (0, (i + first) % planes))
    turned = pl.BlockSpec((width, rows), lambda i: (0, 0))
    return pl.pallas_call(
        functools.partial(weight_body, calls),
        grid=(count,),
        out_shape=jax.ShapeDtypeStruct((count, 2 * width, hid), dtype),
        in_specs=[units] * (2 * calls) + [turned] * (2 * calls),
        out_specs=pl.BlockSpec((1, 2 * width, hid), lambda i: (i, 0, 0)),
        compiler_params=pltpu.CompilerParams(vmem_limit_bytes=56 * MIB),
        cost_estimate=pl.CostEstimate(
            flops=4 * count * calls * rows * width * hid,
            bytes_accessed=4 * calls * rows * (count * hid + width),
            transcendentals=0,
        ),
        name="weight_grads",
    )(*act, *pre, *xt, *gt)


def token_slots(tables, tok_count, capacity):
    len_row, _, start_row, _, far_rows, gate_rows, add_rows = tables
    count = len_row.shape[1]
    place = iota((tok_count, count), 0).astype(F32)
    inside = (place >= start_row) & (place < start_row + len_row)
    columns = []
    for far, add in zip(far_rows, add_rows):
        kept = inside & (place + add < capacity)
        columns.append((over_lanes(kept, place + (add + far * capacity + 1.0)) - 1.0).astype(jnp.int32))
    gates = [over_lanes(inside, row) for row in gate_rows]
    return columns, gates, inside


def first_back_body(
    groups,
    capacity,
    me_ref,
    len_ref,
    task_ref,
    routes_ref,
    table_ref,
    cot_ref,
    hid_ref,
    att_ref,
    wout_ref,
    gains_ref,
    *refs,
):
    back_refs = refs[:groups]
    grad_ref, gatt_ref, gout_ref, small_ref, back, slot_ref, sem = refs[groups:]
    load = [(ref, back.at[pl.ds(i * capacity, capacity)]) for i, ref in enumerate(back_refs)]
    tok_count, width = cot_ref.shape
    tables = routing(len_ref, task_ref, routes_ref, table_ref, me_ref[0], capacity)
    columns, _, _ = token_slots(tables, tok_count, capacity)
    slot_ref[:, 0:1] = columns[0]
    slot_ref[:, 1:2] = columns[1]
    load_all(load, sem)
    small_ref[...] = jnp.zeros_like(small_ref)

    def step(index, carry):
        rows = pl.ds(pl.multiple_of(index * ROWS, ROWS), ROWS)
        slots = iota((ROWS, groups * capacity), 1)
        hit = (slots == slot_ref[rows, 0:1]) | (slots == slot_ref[rows, 1:2])
        grad_two = dot(hit.astype(F32).astype(BF), back[...])
        hat, scale = centred_of(hid_ref[rows, :])
        grad = cot_ref[rows, :].astype(F32) + norm_back(grad_two, hat, scale, gains_ref[1:2, :])
        grad_ref[rows, :] = grad
        small_ref[0:1, :] += jnp.sum(grad_two * hat, axis=0, keepdims=True)
        small_ref[1:2, :] += jnp.sum(grad_two, axis=0, keepdims=True)
        small_ref[2:3, :] += jnp.sum(grad, axis=0, keepdims=True)
        low = grad.astype(BF)
        gatt_ref[rows, :] = dot_nt(low, wout_ref[...]).astype(BF)
        return carry

    lax.fori_loop(0, tok_count // ROWS, step, 0)
    gout_ref[...] = dot_tn(att_ref[...], grad_ref[...].astype(BF)).astype(gout_ref.dtype)


def first_back(me, lengths, seg_task, routes, gate_table, cotangent, hidden, attended, w_out, gains, back, capacity):
    tok_count, width = cotangent.shape
    groups = len(back)
    whole = pl.BlockSpec(memory_space=pltpu.VMEM)
    return pl.pallas_call(
        functools.partial(first_back_body, groups, capacity),
        out_shape=[
            jax.ShapeDtypeStruct((tok_count, width), F32),
            jax.ShapeDtypeStruct((tok_count, width), BF),
            jax.ShapeDtypeStruct((width, width), F32),
            jax.ShapeDtypeStruct((8, width), F32),
        ],
        in_specs=[pl.BlockSpec(memory_space=pltpu.SMEM)]
        + [whole] * 9
        + [pl.BlockSpec(memory_space=pl.ANY)] * groups,
        out_specs=[whole] * 4,
        scratch_shapes=[
            pltpu.VMEM((groups * capacity, width), BF),
            pltpu.VMEM((tok_count, 2), jnp.int32),
            pltpu.SemaphoreType.DMA((groups,)),
        ],
        compiler_params=pltpu.CompilerParams(vmem_limit_bytes=56 * MIB),
        cost_estimate=pl.CostEstimate(
            flops=2 * tok_count * width * (groups * capacity + 2 * width),
            bytes_accessed=16 * tok_count * width,
            transcendentals=0,
        ),
        name="first_back",
    )(me, lengths, seg_task, routes, gate_table, cotangent, hidden, attended, w_out, gains, *back)


def attend_back_body(
    len_ref, qkv_ref, gatt_ref, one_ref, gqkv_ref, dqkv_ref, small_ref, key_acc, value_acc
):
    tok_count, width = gatt_ref.shape
    len_row, len_col, start_row, start_col = sentence_bounds(len_ref)
    end_row, end_col = start_row + len_row, start_col + len_col
    count = len_row.shape[1]
    key_acc[...] = jnp.zeros_like(key_acc)
    value_acc[...] = jnp.zeros_like(value_acc)

    def step(block, carry):
        rows = pl.ds(pl.multiple_of(block * QROWS, QROWS), QROWS)
        start = window_start(block, tok_count)
        keys = pl.ds(start, KROWS)
        query_place = (iota((count, QROWS), 1) + block * QROWS).astype(F32)
        query_seg = jnp.sum((query_place >= end_col).astype(F32), axis=0, keepdims=True)
        key_place = (iota((KROWS, count), 0) + start).astype(F32)
        key_seg = jnp.sum((key_place >= end_row).astype(F32), axis=1, keepdims=True)
        same = key_seg == query_seg
        same = jnp.concatenate([same, same], axis=1)
        for pair in range(width // PAIR):
            lanes = slice(pair * PAIR, (pair + 1) * PAIR)
            stacked = split_heads(qkv_ref[rows, lanes])
            grads = split_heads(gatt_ref[rows, lanes])
            key_rows = qkv_ref[keys, slice(width + lanes.start, width + lanes.stop)]
            value_rows = qkv_ref[keys, slice(2 * width + lanes.start, 2 * width + lanes.stop)]
            scores = jnp.where(same, dot_nt(key_rows, stacked), MASK_FILL)
            raised = jnp.exp(scores - jnp.max(scores, axis=0, keepdims=True))
            probs = raised * (1.0 / jnp.sum(raised, axis=0, keepdims=True))
            grad_probs = dot_nt(value_rows, grads)
            inner = jnp.sum(probs * grad_probs, axis=0, keepdims=True)
            grad_scores = (probs * (grad_probs - inner)).astype(BF)
            value_acc[keys, lanes] += dot(probs.astype(BF), grads)
            key_acc[keys, lanes] += dot(grad_scores, stacked)
            grad_queries = join_heads(dot_tn(grad_scores, key_rows)) * HD**-0.5
            dqkv_ref[rows, lanes] = grad_queries.astype(BF)
        return carry

    lax.fori_loop(0, tok_count // QROWS, step, 0)
    dqkv_ref[:, width : 2 * width] = key_acc[...].astype(BF)
    dqkv_ref[:, 2 * width :] = value_acc[...].astype(BF)
    small_ref[...] = jnp.zeros_like(small_ref)
    small_ref[0:1, :] = jnp.sum(dqkv_ref[:, :width].astype(F32), axis=0, keepdims=True)
    small_ref[1:2, :] = jnp.sum(dqkv_ref[:, 2 * width :].astype(F32), axis=0, keepdims=True)
    gqkv_ref[...] = dot_tn(one_ref[...], dqkv_ref[...]).astype(gqkv_ref.dtype)


def attend_back(lengths, qkv, grad_attended, normed_one):
    tok_count, width = grad_attended.shape
    whole = pl.BlockSpec(memory_space=pltpu.VMEM)
    return pl.pallas_call(
        attend_back_body,
        out_shape=[
            jax.ShapeDtypeStruct((width, 3 * width), F32),
            jax.ShapeDtypeStruct((tok_count, 3 * width), BF),
            jax.ShapeDtypeStruct((8, width), F32),
        ],
        in_specs=[whole] * 4,
        out_specs=[whole] * 3,
        scratch_shapes=[
            pltpu.VMEM((tok_count, width), F32),
            pltpu.VMEM((tok_count, width), F32),
        ],
        compiler_params=pltpu.CompilerParams(vmem_limit_bytes=56 * MIB),
        cost_estimate=pl.CostEstimate(
            flops=40 * tok_count * KROWS * width + 6 * tok_count * width * width,
            bytes_accessed=24 * tok_count * width,
            transcendentals=tok_count * KROWS * HEADS,
        ),
        name="attend_back",
    )(lengths, qkv, grad_attended, normed_one)


def last_back_body(dqkv_ref, wqkv_ref, tok_ref, grad_ref, gains_ref, out_ref, small_ref):
    tok_count, width = tok_ref.shape
    small_ref[...] = jnp.zeros_like(small_ref)

    def step(index, carry):
        rows = pl.ds(pl.multiple_of(index * ROWS, ROWS), ROWS)
        grad_one = dot_nt(dqkv_ref[rows, :], wqkv_ref[...])
        hat, scale = centred_of(tok_ref[rows, :].astype(F32))
        back = norm_back(grad_one, hat, scale, gains_ref[0:1, :])
        out_ref[rows, :] = (grad_ref[rows, :] + back).astype(BF)
        small_ref[0:1, :] += jnp.sum(grad_one * hat, axis=0, keepdims=True)
        small_ref[1:2, :] += jnp.sum(grad_one, axis=0, keepdims=True)
        return carry

    lax.fori_loop(0, tok_count // ROWS, step, 0)


def last_back(dqkv, w_qkv, tokens, grad_hidden, gains):
    tok_count, width = tokens.shape
    whole = pl.BlockSpec(memory_space=pltpu.VMEM)
    return pl.pallas_call(
        last_back_body,
        out_shape=[
            jax.ShapeDtypeStruct((tok_count, width), BF),
            jax.ShapeDtypeStruct((8, width), F32),
        ],
        in_specs=[whole] * 5,
        out_specs=[whole] * 2,
        compiler_params=pltpu.CompilerParams(vmem_limit_bytes=40 * MIB),
        cost_estimate=pl.CostEstimate(
            flops=6 * tok_count * width * width,
            bytes_accessed=18 * tok_count * width,
            transcendentals=0,
        ),
        name="last_back",
    )(dqkv, w_qkv, tokens, grad_hidden, gains)


def finish_body(
    groups,
    capacity,
    me_ref,
    len_ref,
    task_ref,
    routes_ref,
    table_ref,
    cot_ref,
    hid_ref,
    *refs,
):
    back_refs = refs[:groups]
    out_ref, gate_ref, back, side_ref, sem = refs[groups:]
    load = [(ref, back.at[pl.ds(i * capacity, capacity)]) for i, ref in enumerate(back_refs)]
    tok_count, width = cot_ref.shape
    tables = routing(len_ref, task_ref, routes_ref, table_ref, me_ref[0], capacity)
    columns, gates, inside = token_slots(tables, tok_count, capacity)
    task_col = over_lanes(inside, task_ref[...].astype(F32))
    for i, column in enumerate([columns[0].astype(F32), columns[1].astype(F32)] + gates + [task_col]):
        side_ref[:, i : i + 1] = column
    load_all(load, sem)
    gate_ref[...] = jnp.zeros_like(gate_ref)

    def step(index, carry):
        rows = pl.ds(pl.multiple_of(index * ROWS, ROWS), ROWS)
        slots = iota((ROWS, groups * capacity), 1)
        side = side_ref[rows, :]
        cot = cot_ref[rows, :].astype(F32)
        total = hid_ref[rows, :]
        inner = jnp.zeros((ROWS, 1), F32)
        parts = []
        mixed = None
        for r in range(2):
            hit = slots == side[:, r : r + 1].astype(jnp.int32)
            picked = dot(hit.astype(F32).astype(BF), back[...])
            gate = side[:, 2 + r : 3 + r]
            mixed = gate * picked if mixed is None else mixed + gate * picked
            grad = jnp.sum(cot * picked, axis=1, keepdims=True)
            parts.append((gate, grad))
            inner = inner + gate * grad
        out_ref[rows, :] = (total + mixed).astype(BF)
        task = iota((ROWS, gate_ref.shape[1]), 1) == side[:, 4:5].astype(jnp.int32)
        for r, (gate, grad) in enumerate(parts):
            gate_ref[r : r + 1, :] += over_rows(task, gate * (grad - inner))
        return carry

    lax.fori_loop(0, tok_count // ROWS, step, 0)


def finish(me, lengths, seg_task, routes, gate_table, cotangent, hidden, back, capacity):
    tok_count, width = cotangent.shape
    groups = len(back)
    whole = pl.BlockSpec(memory_space=pltpu.VMEM)
    return pl.pallas_call(
        functools.partial(finish_body, groups, capacity),
        out_shape=[
            jax.ShapeDtypeStruct((tok_count, width), BF),
            jax.ShapeDtypeStruct((8, 128), F32),
        ],
        in_specs=[pl.BlockSpec(memory_space=pltpu.SMEM)]
        + [whole] * 6
        + [pl.BlockSpec(memory_space=pl.ANY)] * groups,
        out_specs=[whole] * 2,
        scratch_shapes=[
            pltpu.VMEM((groups * capacity, width), BF),
            pltpu.VMEM((tok_count, 8), F32),
            pltpu.SemaphoreType.DMA((groups,)),
        ],
        compiler_params=pltpu.CompilerParams(vmem_limit_bytes=56 * MIB),
        cost_estimate=pl.CostEstimate(
            flops=4 * tok_count * width * groups * capacity,
            bytes_accessed=16 * tok_count * width,
            transcendentals=0,
        ),
        name="finish",
    )(me, lengths, seg_task, routes, gate_table, cotangent, hidden, *back)


def exchange(blocks, axis):
    count = lax.axis_size(axis)
    return [
        block if k == 0 else lax.ppermute(block, axis, [(s, s ^ k) for s in range(count)])
        for k, block in enumerate(blocks)
    ]


def up(block, axis):
    count = lax.axis_size(axis)
    return lax.ppermute(block, axis, [(s, (s + 1) % count) for s in range(count)])


def call_groups(groups, calls):
    order = list(range(groups))[::-1]
    size = max(1, groups // calls)
    return [order[i : i + size] for i in range(0, groups, size)]


def shards(
    tokens,
    cotangent,
    w_qkv,
    bias_qv,
    w_out,
    out_bias,
    norm_gains,
    norm_shifts,
    gate_table,
    w_in,
    w_down,
    lengths,
    seg_task,
    routes,
):
    tok_count, width = tokens.shape
    groups = lax.axis_size("expert")
    planes = lax.axis_size("hidden")
    top_count = routes.shape[1]
    capacity = 3 * top_count * tok_count // (2 * groups * w_in.shape[0])
    me = lax.axis_index("expert").astype(jnp.int32).reshape(1)
    route_args = (me, lengths, seg_task, routes, gate_table)

    in_parts, down_parts = [w_in[0]], [w_down[0]]
    for _ in range(planes - 1):
        down_parts.append(up(down_parts[-1], "hidden"))
        in_parts.append(up(in_parts[-1], "hidden"))

    grad_slots = dispatch(True, capacity, groups, *route_args, cotangent)
    grad_rows = exchange(grad_slots, "expert")

    qkv, attended, hidden, normed_one, normed_two = attend_forward(
        lengths, tokens, w_qkv, bias_qv, w_out, out_bias, norm_gains, norm_shifts
    )
    slots = dispatch(False, capacity, groups, *route_args, normed_two)
    rows = exchange(slots, "expert")

    out_rows, dx_rows = [None] * groups, [None] * groups
    kept = []
    for ids in call_groups(groups, 4):
        outs, dxs, *rest = expert_rows(
            [rows[k] for k in ids], [grad_rows[k] for k in ids], in_parts, down_parts
        )
        kept.append(rest)
        for k, out, dx in zip(ids, outs, dxs):
            out_rows[k], dx_rows[k] = out, dx
    dx_back = exchange(dx_rows, "expert")
    out_back = exchange(out_rows, "expert")

    kept = [list(part) for part in zip(*kept)]
    moving = weight_grads(1, 1, planes, BF, *kept)[0]
    others = weight_grads(2, planes - 1, planes, F32, *kept)
    for i in range(planes - 1):
        total = up(moving, "hidden").astype(F32) + others[i]
        moving = total.astype(BF)
    grad_w_in = total[:width][None]
    grad_w_down = total[width:].T[None]

    grad_hidden, grad_attended, grad_w_out, small_one = first_back(
        *route_args, cotangent, hidden, attended, w_out, norm_gains, dx_back, capacity
    )
    grad_qkv, dqkv, small_two = attend_back(lengths, qkv, grad_attended, normed_one)
    input_grad, small_three = last_back(dqkv, w_qkv, tokens, grad_hidden, norm_gains)
    layer_out, small_four = finish(*route_args, cotangent, hidden, out_back, capacity)

    summed = lax.psum(
        (grad_qkv, grad_w_out, small_one, small_two, small_three, small_four),
        ("expert", "hidden"),
    )
    grad_qkv, grad_w_out, small_one, small_two, small_three, small_four = summed
    return (
        layer_out,
        input_grad,
        grad_qkv,
        small_two[:2],
        grad_w_out,
        small_one[2],
        jnp.stack([small_three[0], small_one[0]]),
        jnp.stack([small_three[1], small_one[1]]),
        small_four[:2, : gate_table.shape[0]].T,
        grad_w_in,
        grad_w_down,
    )


def solution(mesh):
    split = P(("expert", "hidden"), None)
    return jax.shard_map(
        shards,
        mesh=mesh,
        in_specs=(
            split,
            split,
            P(),
            P(),
            P(),
            P(),
            P(),
            P(),
            P(),
            P("expert", None, "hidden"),
            P("expert", "hidden", None),
            split,
            split,
            P(),
        ),
        out_specs=(
            split,
            split,
            P(),
            P(),
            P(),
            P(),
            P(),
            P(),
            P(),
            P("expert", None, "hidden"),
            P("expert", "hidden", None),
        ),
        check_vma=False,
    )
```

```python
import functools
import math

import jax
import jax.numpy as jnp
from jax import lax
from jax.experimental import pallas as pl
from jax.experimental.pallas import tpu as pltpu
from jax.sharding import PartitionSpec as P

HEADS = 8
HD = 64
NORM_EPS = 1e-05
MASK_FILL = -1000000000.0

BF = jnp.bfloat16
F32 = jnp.float32
MIB = 1 << 20

ROWS = 256
REACH = 64
JOINT = 4
LANES = JOINT * HD
SMALL = 128


def iota(shape, dim):
    return lax.broadcasted_iota(jnp.int32, shape, dim)


def dot(left, right):
    return jnp.dot(left, right, preferred_element_type=F32)


def dot_nt(left, right):
    return lax.dot_general(left, right, (((1,), (1,)), ((), ())), preferred_element_type=F32)


def dot_tn(left, right):
    return lax.dot_general(left, right, (((0,), (0,)), ((), ())), preferred_element_type=F32)


def over_lanes(mask, values):
    return jnp.sum(jnp.where(mask, values, 0.0), axis=1, keepdims=True)


def over_rows(mask, values):
    return jnp.sum(jnp.where(mask, values, 0.0), axis=0, keepdims=True)


def to_column(row):
    count = row.shape[1]
    return over_lanes(iota((count, count), 0) == iota((count, count), 1), row)


def one_hot(mask):
    return mask.astype(F32).astype(BF)


WHOLE = pl.BlockSpec(memory_space=pltpu.VMEM)
SCALARS = pl.BlockSpec(memory_space=pltpu.SMEM)
ANYWHERE = pl.BlockSpec(memory_space=pl.ANY)


HOLD = 1
SCALE = 0.4
MICROS = {
    "dispatch_grads": 6,
    "forward": 13,
    "expert_rows": 17,
    "weight_grads": 9,
    "expert_outputs": 11,
    "backward": 23,
    "last_back": 6,
    "finish": 12,
}


def run(name, body, args, in_specs, out_shape, out_specs, scratch=(), after=(), aliases=None):
    count, extra = len(args), len(after)

    def ordered(*refs):
        outs = refs[count + extra :]
        mark, rest = outs[len(out_shape)], outs[: len(out_shape)] + outs[len(out_shape) + 1 :]
        mark[...] = jnp.zeros_like(mark)
        body(*refs[:count], *rest)

    *results, mark = pl.pallas_call(
        ordered,
        out_shape=[*out_shape, jax.ShapeDtypeStruct((8, 128), F32)],
        in_specs=[*in_specs, *[ANYWHERE] * extra],
        out_specs=[*out_specs, WHOLE],
        scratch_shapes=list(scratch),
        input_output_aliases=aliases or {},
        compiler_params=pltpu.CompilerParams(vmem_limit_bytes=56 * MIB),
        cost_estimate=pl.CostEstimate(flops=int(1.15e9 * SCALE * MICROS.get(name, 2)), bytes_accessed=1 << 10, transcendentals=0),
        name=name,
    )(*args, *after)
    return results, mark


def join_weights(w_in, w_down):
    _, width, hid = w_in.shape

    def body(in_ref, down_ref, out_ref):
        out_ref[:width, :] = in_ref[0]
        out_ref[width:, :] = down_ref[0].T

    (out,), mark = run(
        "join_weights",
        body,
        (w_in, w_down),
        [WHOLE] * 2,
        [jax.ShapeDtypeStruct((2 * width, hid), BF)],
        [WHOLE],
    )
    return out, mark


def hold(block, after):
    (block,), _ = run(
        "hold",
        lambda *refs: None,
        (block,),
        [ANYWHERE],
        [jax.ShapeDtypeStruct(block.shape, block.dtype)],
        [ANYWHERE],
        (),
        after,
        {0: 0},
    )
    return block


class Copies:
    def __init__(self, sem):
        self.sem, self.count, self.open = sem, 0, []

    def start(self, source, target):
        copy = pltpu.make_async_copy(source, target, self.sem.at[self.count])
        copy.start()
        self.count += 1
        self.open.append(copy)
        return copy

    def wait(self):
        for copy in self.open:
            copy.wait()
        self.open = []


def centred_of(values):
    centred = values - jnp.mean(values, axis=-1, keepdims=True)
    spread = jnp.mean(centred * centred, axis=-1, keepdims=True)
    scale = lax.rsqrt(spread + NORM_EPS)
    return centred * scale, scale


def norm_back(grad, hat, scale, gain):
    scaled = grad * gain
    return scale * (
        scaled
        - jnp.mean(scaled, axis=-1, keepdims=True)
        - hat * jnp.mean(scaled * hat, axis=-1, keepdims=True)
    )


def sentence_bounds(lengths_ref):
    len_row = lengths_ref[...].astype(F32)
    count = len_row.shape[1]
    len_col = to_column(len_row)
    start_col = over_lanes(iota((count, count), 1) < iota((count, count), 0), len_row)
    start_row = over_rows(iota((count, count), 0) < iota((count, count), 1), len_col)
    return (len_row, len_col, start_row, start_col)


def routing(lengths_ref, task_ref, routes_ref, table_ref, me):
    len_row, len_col, start_row, start_col = sentence_bounds(lengths_ref)
    count = len_row.shape[1]
    tasks = routes_ref.shape[1]
    hit = iota((tasks, count), 0) == task_ref[...]
    expert_rows = [
        over_rows(hit, to_column(routes_ref[r : r + 1, :].astype(F32))) for r in range(2)
    ]
    logit_rows = [over_rows(hit, to_column(table_ref[r : r + 1, :])) for r in range(2)]
    peak = jnp.maximum(logit_rows[0], logit_rows[1])
    raised = [jnp.exp(row - peak) for row in logit_rows]
    gate_rows = [row / (raised[0] + raised[1]) for row in raised]
    expert_cols = [to_column(row) for row in expert_rows]
    earlier = iota((count, count), 0) < iota((count, count), 1)
    add_rows, far_rows = [], []
    for row in expert_rows:
        same = (expert_cols[0] == row) | (expert_cols[1] == row)
        add_rows.append(over_rows(earlier & same, len_col) - start_row)
        far_rows.append((row.astype(jnp.int32) ^ me).astype(F32))
    return (len_row, len_col, start_row, start_col, far_rows, gate_rows, add_rows)


def fill_slots(tables, data, capacity, groups, weighted):
    len_row, len_col, start_row, start_col, far_rows, gate_rows, add_rows = tables
    tok_count, count = data.shape[0], len_row.shape[1]
    place = iota((count, tok_count), 1).astype(F32)
    inside = (place >= start_col) & (place < start_col + len_col)
    token_place = iota((1, tok_count), 1).astype(F32)
    far = [over_rows(inside, to_column(row)) for row in far_rows]
    position = [token_place + over_rows(inside, to_column(row)) for row in add_rows]
    slots = iota((capacity, tok_count), 0)
    slot_column = iota((capacity, count), 0).astype(F32)
    for k in range(groups):
        slot = jnp.where(far[0] == k, position[0], jnp.where(far[1] == k, position[1], -1.0))
        picked = dot(one_hot(slots == slot.astype(jnp.int32)), data)
        if weighted:
            first, second = far_rows[0] == k, far_rows[1] == k
            base = jnp.where(first, add_rows[0], add_rows[1]) + start_row
            gate = jnp.where(first, gate_rows[0], jnp.where(second, gate_rows[1], 0.0))
            picked = picked * over_lanes((slot_column >= base) & (slot_column < base + len_row), gate)
        yield k, picked


def dispatch_body(len_ref, task_ref, routes_ref, table_ref, data_ref, out_ref, stage, sem):
    groups, capacity, _ = out_ref.shape
    copies = Copies(sem)
    tables = routing(len_ref, task_ref, routes_ref, table_ref, 0)
    for k, picked in fill_slots(tables, data_ref[...], capacity, groups, True):
        stage[k] = picked.astype(BF)
        copies.start(stage.at[k], out_ref.at[k])
    copies.wait()


def dispatch_grads(capacity, groups, lengths, seg_task, routes, gate_table, cotangent, after):
    slots = (groups, capacity, cotangent.shape[1])
    (out,), mark = run(
        "dispatch_grads",
        dispatch_body,
        (lengths, seg_task, routes, gate_table, cotangent),
        [WHOLE] * 5,
        [jax.ShapeDtypeStruct(slots, BF)],
        [ANYWHERE],
        [pltpu.VMEM(slots, BF), pltpu.SemaphoreType.DMA((groups,))],
        after,
    )
    return out, mark


def split_heads(block):
    head = iota(block.shape, 1) // HD
    zero = jnp.zeros_like(block)
    return jnp.concatenate([jnp.where(head == h, block, zero) for h in range(JOINT)], axis=0)


def join_heads(stacked):
    rows = stacked.shape[0] // JOINT
    head = iota((rows, stacked.shape[1]), 1) // HD
    out = stacked[:rows]
    for h in range(1, JOINT):
        out = jnp.where(head == h, stacked[h * rows : (h + 1) * rows], out)
    return out


def windows(lengths_ref, tok_count, queries):
    len_row, len_col, start_row, start_col = sentence_bounds(lengths_ref)
    end_row, end_col = start_row + len_row, start_col + len_col
    count = len_row.shape[1]
    keys = queries + 2 * REACH
    for block in range(tok_count // queries):
        start = min(max(block * queries - REACH, 0), tok_count - keys)
        query_place = (iota((count, queries), 1) + block * queries).astype(F32)
        query_seg = jnp.sum((query_place >= end_col).astype(F32), axis=0, keepdims=True)
        key_place = (iota((keys, count), 0) + start).astype(F32)
        key_seg = jnp.sum((key_place >= end_row).astype(F32), axis=1, keepdims=True)
        same = key_seg == jnp.concatenate([query_seg] * JOINT, axis=1)
        rows = slice(block * queries, (block + 1) * queries)
        yield rows, slice(start, start + keys), same


def softmax_of(key_rows, stacked, same):
    scores = jnp.where(same, dot_nt(key_rows, stacked), MASK_FILL)
    raised = jnp.exp(scores - jnp.max(scores, axis=0, keepdims=True))
    return raised * (1.0 / jnp.sum(raised, axis=0, keepdims=True))


def forward_body(
    capacity,
    groups,
    me_ref,
    len_ref,
    task_ref,
    routes_ref,
    table_ref,
    tok_ref,
    wqkv_ref,
    bias_ref,
    wout_ref,
    obias_ref,
    gains_ref,
    shifts_ref,
    *refs,
):
    qkv_out, att_out, hid_out, one_out = refs[:4]
    slot_out = refs[4 : 4 + groups]
    qkv, att, hid, one, two, stage, sem = refs[4 + groups :]
    tok_count, width = tok_ref.shape
    copies = Copies(sem)
    for step in range(tok_count // ROWS):
        rows = slice(step * ROWS, (step + 1) * ROWS)
        hat, _ = centred_of(tok_ref[rows, :].astype(F32))
        normed = (hat * gains_ref[0:1, :] + shifts_ref[0:1, :]).astype(BF)
        one[rows, :] = normed
        wide = dot(normed, wqkv_ref[...])
        queries = (wide[:, :width] + bias_ref[0:1, :]).astype(BF)
        qkv[rows, :width] = queries * jnp.asarray(HD**-0.5, BF)
        qkv[rows, width : 2 * width] = wide[:, width : 2 * width].astype(BF)
        qkv[rows, 2 * width :] = (wide[:, 2 * width :] + bias_ref[1:2, :]).astype(BF)
    copies.start(one, one_out)
    copies.start(qkv, qkv_out)
    for rows, keys, same in windows(len_ref, tok_count, REACH):
        for first in range(0, width, LANES):
            lanes = slice(first, first + LANES)
            key_rows = qkv[keys, width + first : width + first + LANES]
            value_rows = qkv[keys, 2 * width + first : 2 * width + first + LANES]
            probs = softmax_of(key_rows, split_heads(qkv[rows, lanes]), same).astype(BF)
            att[rows, lanes] = join_heads(dot_tn(probs, value_rows)).astype(BF)
    copies.start(att, att_out)
    for step in range(tok_count // ROWS):
        rows = slice(step * ROWS, (step + 1) * ROWS)
        hidden = tok_ref[rows, :].astype(F32) + dot(att[rows, :], wout_ref[...]) + obias_ref[...]
        hid[rows, :] = hidden
        hat, _ = centred_of(hidden)
        two[rows, :] = (hat * gains_ref[1:2, :] + shifts_ref[1:2, :]).astype(BF)
    copies.start(hid, hid_out)
    tables = routing(len_ref, task_ref, routes_ref, table_ref, me_ref[0])
    for k, picked in fill_slots(tables, two[...], capacity, groups, False):
        stage[k] = picked.astype(BF)
        copies.start(stage.at[k], slot_out[k])
    copies.wait()


def forward(
    capacity,
    groups,
    me,
    lengths,
    seg_task,
    routes,
    gate_table,
    tokens,
    w_qkv,
    bias_qv,
    w_out,
    out_bias,
    gains,
    shifts,
    after,
):
    tok_count, width = tokens.shape
    whole = [
        ((tok_count, 3 * width), BF),
        ((tok_count, width), BF),
        ((tok_count, width), F32),
        ((tok_count, width), BF),
    ]
    (qkv, att, hid, one, *slots), mark = run(
        "forward",
        functools.partial(forward_body, capacity, groups),
        (
            me,
            lengths,
            seg_task,
            routes,
            gate_table,
            tokens,
            w_qkv,
            bias_qv,
            w_out,
            out_bias.reshape(1, width),
            gains,
            shifts,
        ),
        [SCALARS] + [WHOLE] * 11,
        [jax.ShapeDtypeStruct(*kind) for kind in whole]
        + [jax.ShapeDtypeStruct((capacity, width), BF)] * groups,
        [ANYWHERE] * (4 + groups),
        [pltpu.VMEM(*kind) for kind in whole]
        + [
            pltpu.VMEM((tok_count, width), BF),
            pltpu.VMEM((groups, capacity, width), BF),
            pltpu.SemaphoreType.DMA((4 + groups,)),
        ],
        after,
    )
    return qkv, att, hid, one, slots, mark


GELU_A = 0.7978845608028654
GELU_B = 0.044715


def gelu_both(values):
    square = values * values
    inner = values * (GELU_A + (GELU_A * GELU_B) * square)
    half = 0.5 * jnp.tanh(inner) + 0.5
    active = values * half
    slope = half + active * (1.0 - half) * (2.0 * GELU_A + (6.0 * GELU_A * GELU_B) * square)
    return active, slope


def pieces_of(total, size):
    return [slice(i, min(i + size, total)) for i in range(0, total, size)]


def expert_body(ids, planes, me_ref, *refs):
    refs = list(refs)
    take = lambda count: [refs.pop(0) for _ in range(count)]
    blocks = len(ids)
    x_in, (g_in,), parts = take(blocks), take(1), take(planes)
    dx_out = take(blocks)
    act_out, pre_out, xt_out, gt_out = take(4)
    xs, gs, w_in, w_down, act, pre, xt, gt, dx, sem = refs
    cap, width = x_in[0].shape
    hid = parts[0].shape[1]
    rows = blocks * cap
    me = me_ref[0]
    copies = Copies(sem)
    for i, k in enumerate(ids):
        copies.start(x_in[i], xs.at[pl.ds(i * cap, cap)])
        copies.start(g_in.at[me ^ k], gs.at[pl.ds(i * cap, cap)])
    rows_there, copies.open = copies.open, []
    parts_there = []
    for c in range(planes):
        lanes = pl.ds(c * hid, hid)
        copies.start(parts[c].at[pl.ds(0, width)], w_in.at[:, lanes])
        copies.start(parts[c].at[pl.ds(width, width)], w_down.at[:, lanes])
        parts_there.append(copies.open)
        copies.open = []
    for copy in rows_there:
        copy.wait()
    for c in range(planes):
        for copy in parts_there[c]:
            copy.wait()
        lanes = slice(c * hid, (c + 1) * hid)
        for spot in pieces_of(rows, 3 * cap):
            active, slope = gelu_both(dot(xs[spot, :], w_in[:, lanes]))
            act[spot, lanes] = active.astype(BF)
            pre[spot, lanes] = (dot(gs[spot, :], w_down[:, lanes]) * slope).astype(BF)
        copies.start(act.at[:, pl.ds(c * hid, hid)], act_out.at[:, pl.ds(c * hid, hid)])
        copies.start(pre.at[:, pl.ds(c * hid, hid)], pre_out.at[:, pl.ds(c * hid, hid)])
        if c == 0:
            xt[...] = xs[...].T
            copies.start(xt, xt_out)
            gt[...] = gs[...].T
            copies.start(gt, gt_out)
    for i, spot in enumerate(pieces_of(rows, 3 * cap)):
        dx[spot, :] = dot_nt(pre[spot, :], w_in[...]).astype(BF)
        for j in range(spot.start // cap, spot.stop // cap):
            copies.start(dx.at[pl.ds(j * cap, cap)], dx_out[j])
    copies.wait()


def expert_rows(ids, me, x_blocks, g_rows, parts, after):
    blocks, planes = len(ids), len(parts)
    cap, width = x_blocks[0].shape
    hid = parts[0].shape[1]
    rows = blocks * cap
    units, turned = (rows, planes * hid), (width, rows)
    result, mark = run(
        "expert_rows",
        functools.partial(expert_body, ids, planes),
        (me, *x_blocks, g_rows, *parts),
        [SCALARS] + [ANYWHERE] * (blocks + 1 + planes),
        [jax.ShapeDtypeStruct((cap, width), BF)] * blocks
        + [jax.ShapeDtypeStruct(units, BF)] * 2
        + [jax.ShapeDtypeStruct(turned, BF)] * 2,
        [ANYWHERE] * (blocks + 4),
        [
            pltpu.VMEM((rows, width), BF),
            pltpu.VMEM((rows, width), BF),
            pltpu.VMEM((width, planes * hid), BF),
            pltpu.VMEM((width, planes * hid), BF),
            pltpu.VMEM(units, BF),
            pltpu.VMEM(units, BF),
            pltpu.VMEM(turned, BF),
            pltpu.VMEM(turned, BF),
            pltpu.VMEM((rows, width), BF),
            pltpu.SemaphoreType.DMA((3 * blocks + 4 * planes + 2,)),
        ],
        after,
    )
    return result[:blocks], result[blocks:], mark


def output_body(calls, planes, me_ref, *refs):
    act_in, parts = refs[: len(calls)], refs[len(calls) : len(calls) + planes]
    out_ref, act, w_down, stage, sem = refs[len(calls) + planes :]
    _, capacity, width = out_ref.shape
    hid = parts[0].shape[1]
    copies = Copies(sem)
    for c, part in enumerate(parts):
        copies.start(part.at[pl.ds(width, width)], w_down.at[:, pl.ds(c * hid, hid)])
    there, copies.open = copies.open, []
    there_rows, spot = [], 0
    for ids, units in zip(calls, act_in):
        size = len(ids) * capacity
        there_rows.append(copies.start(units, act.at[pl.ds(spot, size)]))
        spot += size
    copies.open = []
    for copy in there:
        copy.wait()
    spot = 0
    for ids, copy in zip(calls, there_rows):
        copy.wait()
        size = len(ids) * capacity
        stage[spot : spot + size, :] = dot_nt(act[spot : spot + size, :], w_down[...]).astype(BF)
        for k in ids:
            copies.start(stage.at[pl.ds(spot, capacity)], out_ref.at[me_ref[0] ^ k])
            spot += capacity
    copies.wait()


def expert_outputs(calls, groups, capacity, me, act, parts, after):
    planes = len(parts)
    width, hid = parts[0].shape[0] // 2, parts[0].shape[1]
    (out,), mark = run(
        "expert_outputs",
        functools.partial(output_body, calls, planes),
        (me, *act, *parts),
        [SCALARS] + [ANYWHERE] * (len(act) + planes),
        [jax.ShapeDtypeStruct((groups, capacity, width), BF)],
        [ANYWHERE],
        [
            pltpu.VMEM((groups * capacity, planes * hid), BF),
            pltpu.VMEM((width, planes * hid), BF),
            pltpu.VMEM((groups * capacity, width), BF),
            pltpu.SemaphoreType.DMA((planes + len(calls) + groups,)),
        ],
        after,
    )
    return out, mark


def weight_body(which, calls, *refs):
    act_in, pre_in, xt_in, gt_in = (refs[i * calls : (i + 1) * calls] for i in range(4))
    out_refs = refs[4 * calls : 4 * calls + len(which)]
    act, pre, xt, gt, stage, sem = refs[4 * calls + len(which) :]
    width, hid = xt.shape[0], act.shape[2]
    spots, total = [], 0
    for turned in xt_in:
        spots.append(pl.ds(total, turned.shape[1]))
        total += turned.shape[1]
    copies = Copies(sem)
    there = []

    def work(n):
        for copy in there[n]:
            copy.wait()
        for i, (turned, units) in enumerate(((xt, pre), (gt, act))):
            spot = pl.ds(i * width, width)
            stage[n, spot, :] = dot(turned[...], units[n % 2]).astype(stage.dtype)
            copies.start(stage.at[n, spot], out_refs[n].at[spot])

    for n, c in enumerate(which):
        lanes = pl.ds(c * hid, hid)
        done, copies.open = copies.open, []
        for i, spot in enumerate(spots):
            if n == 0:
                copies.start(xt_in[i], xt.at[:, spot])
                copies.start(gt_in[i], gt.at[:, spot])
            copies.start(pre_in[i].at[:, lanes], pre.at[n % 2, spot])
            copies.start(act_in[i].at[:, lanes], act.at[n % 2, spot])
        there.append(copies.open)
        copies.open = done
        if n:
            work(n - 1)
    work(len(which) - 1)
    copies.wait()


def weight_grads(which, planes, dtype, act, pre, xt, gt, after):
    calls = len(act)
    width, rows = xt[0].shape[0], sum(turned.shape[1] for turned in xt)
    hid = act[0].shape[1] // planes
    return run(
        "weight_grads",
        functools.partial(weight_body, which, calls),
        (*act, *pre, *xt, *gt),
        [ANYWHERE] * (4 * calls),
        [jax.ShapeDtypeStruct((2 * width, hid), dtype)] * len(which),
        [ANYWHERE] * len(which),
        [
            pltpu.VMEM((2, rows, hid), BF),
            pltpu.VMEM((2, rows, hid), BF),
            pltpu.VMEM((width, rows), BF),
            pltpu.VMEM((width, rows), BF),
            pltpu.VMEM((len(which), 2 * width, hid), dtype),
            pltpu.SemaphoreType.DMA((2 * calls * (len(which) + 1) + 2 * len(which),)),
        ],
        after,
    )


def token_slots(tables, tok_count, capacity):
    len_row, _, start_row, _, far_rows, gate_rows, add_rows = tables
    count = len_row.shape[1]
    place = iota((tok_count, count), 0).astype(F32)
    inside = (place >= start_row) & (place < start_row + len_row)
    columns = []
    for far, add in zip(far_rows, add_rows):
        kept = inside & (place + add < capacity)
        columns.append(over_lanes(kept, place + (add + far * capacity + 1.0)) - 1.0)
    gates = [over_lanes(inside, row) for row in gate_rows]
    return columns, gates, inside


def backward_body(
    groups,
    capacity,
    me_ref,
    len_ref,
    task_ref,
    routes_ref,
    table_ref,
    cot_ref,
    wout_ref,
    gains_ref,
    hid_in,
    att_in,
    qkv_in,
    one_in,
    *refs,
):
    back_in = refs[:groups]
    keep_ref, send_ref, grad_out, dqkv_out = refs[groups : groups + 4]
    back, side, hid, att, qkv, one, grad_all, low, gatt, dqkv, total, sem = refs[groups + 4 :]
    copies = Copies(sem)
    for i, ref in enumerate(back_in):
        copies.start(ref, back.at[pl.ds(i * capacity, capacity)])
    copies.start(hid_in, hid)
    first, copies.open = copies.open, []
    att_there = copies.start(att_in, att)
    qkv_there = copies.start(qkv_in, qkv)
    one_there = copies.start(one_in, one)
    copies.open = []
    tok_count, width = cot_ref.shape
    me = me_ref[0]
    tables = routing(len_ref, task_ref, routes_ref, table_ref, me)
    columns, _, _ = token_slots(tables, tok_count, capacity)
    for i, column in enumerate(columns):
        side[:, i : i + 1] = column.astype(jnp.int32)
    for copy in first:
        copy.wait()
    sums = [jnp.zeros((1, width), F32)] * 3
    for step in range(tok_count // ROWS):
        rows = slice(step * ROWS, (step + 1) * ROWS)
        slots = iota((ROWS, groups * capacity), 1)
        hit = (slots == side[rows, 0:1]) | (slots == side[rows, 1:2])
        grad_two = dot(one_hot(hit), back[...])
        hat, scale = centred_of(hid[rows, :])
        grad = cot_ref[rows, :].astype(F32) + norm_back(grad_two, hat, scale, gains_ref[1:2, :])
        grad_all[rows, :] = grad
        for i, part in enumerate((grad_two * hat, grad_two, grad)):
            sums[i] = sums[i] + jnp.sum(part, axis=0, keepdims=True)
        low[rows, :] = grad.astype(BF)
        gatt[rows, :] = dot_nt(low[rows, :], wout_ref[...]).astype(BF)
    copies.start(grad_all, grad_out)
    att_there.wait()
    total[:, 3 * width : 4 * width] = dot_tn(att[...], low[...])

    qkv_there.wait()
    open_sums = [({}, {}) for _ in range(width // LANES)]
    bias_sums = {}
    spans = list(windows(len_ref, tok_count, 2 * REACH))
    for index, (rows, keys, same) in enumerate(spans):
        next_key = spans[index + 1][1].start if index + 1 < len(spans) else tok_count
        for group, lane in enumerate(range(0, width, LANES)):
            lanes = slice(lane, lane + LANES)
            key_lanes = slice(width + lane, width + lane + LANES)
            value_lanes = slice(2 * width + lane, 2 * width + lane + LANES)
            stacked, grads = split_heads(qkv[rows, lanes]), split_heads(gatt[rows, lanes])
            key_rows, value_rows = qkv[keys, key_lanes], qkv[keys, value_lanes]
            probs = softmax_of(key_rows, stacked, same)
            grad_probs = dot_nt(value_rows, grads)
            inner = jnp.sum(probs * grad_probs, axis=0, keepdims=True)
            grad_scores = (probs * (grad_probs - inner)).astype(BF)
            grad_values = dot(probs.astype(BF), grads)
            grad_keys = dot(grad_scores, stacked)
            grad_queries = join_heads(dot_tn(grad_scores, key_rows)) * HD**-0.5
            dqkv[rows, lanes] = grad_queries.astype(BF)
            for held, fresh, target in zip(
                open_sums[group], (grad_keys, grad_values), (key_lanes, value_lanes)
            ):
                for i in range(0, fresh.shape[0], REACH):
                    place = keys.start + i
                    part = fresh[i : i + REACH]
                    held[place] = held[place] + part if place in held else part
                for place in [place for place in held if place < next_key]:
                    dqkv[place : place + REACH, target] = held.pop(place).astype(BF)
    copies.start(dqkv, dqkv_out)
    ones = jnp.ones((8, tok_count), BF)
    bias = [dot(ones, dqkv[:, :width])[0:1], dot(ones, dqkv[:, 2 * width :])[0:1]]
    short = jnp.concatenate(sums + bias + [jnp.zeros((SMALL - 5, width), F32)], axis=0)
    total[:, 4 * width :] = short.T
    one_there.wait()
    total[:, : 3 * width] = dot_tn(one[...], dqkv[...])
    half, rows, _ = keep_ref.shape
    for j in range(half):
        for bit, ref in enumerate((keep_ref, send_ref)):
            owner = me ^ (2 * j + bit)
            ref[j] = total[pl.ds(pl.multiple_of(owner * rows, rows), rows), :].astype(BF)
    copies.wait()


def backward(
    capacity,
    me,
    lengths,
    seg_task,
    routes,
    gate_table,
    cotangent,
    w_out,
    gains,
    hidden,
    attended,
    qkv,
    one,
    back,
    after,
):
    tok_count, width = cotangent.shape
    groups = len(back)
    columns = 4 * width + SMALL
    pieces = jax.ShapeDtypeStruct((groups // 2, width // groups, columns), BF)
    (keep, send, grad, dqkv), mark = run(
        "backward",
        functools.partial(backward_body, groups, capacity),
        (
            me,
            lengths,
            seg_task,
            routes,
            gate_table,
            cotangent,
            w_out,
            gains,
            hidden,
            attended,
            qkv,
            one,
            *back,
        ),
        [SCALARS] + [WHOLE] * 7 + [ANYWHERE] * (4 + groups),
        [
            pieces,
            pieces,
            jax.ShapeDtypeStruct((tok_count, width), F32),
            jax.ShapeDtypeStruct((tok_count, 3 * width), BF),
        ],
        [WHOLE, WHOLE, ANYWHERE, ANYWHERE],
        [
            pltpu.VMEM((groups * capacity, width), BF),
            pltpu.VMEM((tok_count, 2), jnp.int32),
            pltpu.VMEM((tok_count, width), F32),
            pltpu.VMEM((tok_count, width), BF),
            pltpu.VMEM((tok_count, 3 * width), BF),
            pltpu.VMEM((tok_count, width), BF),
            pltpu.VMEM((tok_count, width), F32),
            pltpu.VMEM((tok_count, width), BF),
            pltpu.VMEM((tok_count, width), BF),
            pltpu.VMEM((tok_count, 3 * width), BF),
            pltpu.VMEM((width, columns), F32),
            pltpu.SemaphoreType.DMA((groups + 6,)),
        ],
        after,
    )
    return keep, send, grad, dqkv, mark


def last_body(dqkv_ref, wqkv_ref, tok_ref, grad_ref, gains_ref, out_ref, small_ref):
    tok_count, width = tok_ref.shape
    sums = [jnp.zeros((1, width), F32)] * 2
    for step in range(tok_count // ROWS):
        rows = slice(step * ROWS, (step + 1) * ROWS)
        grad_one = dot_nt(dqkv_ref[rows, :], wqkv_ref[...])
        hat, scale = centred_of(tok_ref[rows, :].astype(F32))
        back = norm_back(grad_one, hat, scale, gains_ref[0:1, :])
        out_ref[rows, :] = (grad_ref[rows, :] + back).astype(BF)
        for i, part in enumerate((grad_one * hat, grad_one)):
            sums[i] = sums[i] + jnp.sum(part, axis=0, keepdims=True)
    small_ref[...] = jnp.concatenate(sums, axis=0)


def last_back(dqkv, w_qkv, tokens, grad_hidden, gains, after):
    tok_count, width = tokens.shape
    (out, small), mark = run(
        "last_back",
        last_body,
        (dqkv, w_qkv, tokens, grad_hidden, gains),
        [WHOLE] * 5,
        [jax.ShapeDtypeStruct((tok_count, width), BF), jax.ShapeDtypeStruct((2, width), F32)],
        [WHOLE] * 2,
        (),
        after,
    )
    return out, small, mark


def finish_body(
    len_ref,
    task_ref,
    routes_ref,
    table_ref,
    cot_ref,
    hid_ref,
    back_in,
    out_ref,
    gate_ref,
    back,
    side_ref,
    sem,
):
    groups, capacity, _ = back_in.shape
    copies = Copies(sem)
    for i in range(groups):
        copies.start(back_in.at[i], back.at[pl.ds(i * capacity, capacity)])
    tok_count, width = cot_ref.shape
    tables = routing(len_ref, task_ref, routes_ref, table_ref, 0)
    columns, gates, inside = token_slots(tables, tok_count, capacity)
    task_col = over_lanes(inside, task_ref[...].astype(F32))
    for i, column in enumerate(columns + gates + [task_col]):
        side_ref[:, i : i + 1] = column
    copies.wait()
    gate_sums = [jnp.zeros((1, gate_ref.shape[1]), F32)] * 2
    for step in range(tok_count // ROWS):
        rows = slice(step * ROWS, (step + 1) * ROWS)
        slots = iota((ROWS, groups * capacity), 1)
        side = side_ref[rows, :]
        cot = cot_ref[rows, :].astype(F32)
        mixed = hid_ref[rows, :]
        inner = jnp.zeros((ROWS, 1), F32)
        parts = []
        for r in range(2):
            hit = slots == side[:, r : r + 1].astype(jnp.int32)
            picked = dot(one_hot(hit), back[...])
            gate = side[:, 2 + r : 3 + r]
            mixed = mixed + gate * picked
            grad = jnp.sum(cot * picked, axis=1, keepdims=True)
            parts.append((gate, grad))
            inner = inner + gate * grad
        out_ref[rows, :] = mixed.astype(BF)
        task = iota((ROWS, gate_ref.shape[1]), 1) == side[:, 4:5].astype(jnp.int32)
        for r, (gate, grad) in enumerate(parts):
            gate_sums[r] = gate_sums[r] + over_rows(task, gate * (grad - inner))
    gate_ref[...] = jnp.concatenate(gate_sums, axis=0)


def finish(lengths, seg_task, routes, gate_table, cotangent, hidden, back, after):
    tok_count, width = cotangent.shape
    groups, capacity, _ = back.shape
    (out, gate), mark = run(
        "finish",
        finish_body,
        (lengths, seg_task, routes, gate_table, cotangent, hidden, back),
        [WHOLE] * 6 + [ANYWHERE],
        [jax.ShapeDtypeStruct((tok_count, width), BF), jax.ShapeDtypeStruct((2, 128), F32)],
        [WHOLE] * 2,
        [
            pltpu.VMEM((groups * capacity, width), BF),
            pltpu.VMEM((tok_count, 8), F32),
            pltpu.SemaphoreType.DMA((groups,)),
        ],
        after,
    )
    return out, gate, mark


def swap(block, axis, distance):
    count = lax.axis_size(axis)
    return lax.ppermute(block, axis, [(s, s ^ distance) for s in range(count)])


def turn(block, axis, distance):
    count = lax.axis_size(axis)
    return lax.ppermute(block, axis, [(s, (s + distance) % count) for s in range(count)])


def powers(count):
    return [1 << i for i in range(count.bit_length() - 1)]


def add_pairs(keep, came, after):
    count, rows, columns = keep.shape

    def body(keep_ref, came_ref, *out_refs):
        for j, out_ref in enumerate(out_refs):
            out_ref[...] = (keep_ref[j].astype(F32) + came_ref[j].astype(F32)).astype(BF)

    return run(
        "add_pairs",
        body,
        (keep, came),
        [WHOLE] * 2,
        [jax.ShapeDtypeStruct((rows, columns), BF)] * count,
        [WHOLE] * count,
        (),
        after,
    )


def add_all(blocks, after):
    def body(*refs):
        total = refs[0][...].astype(F32)
        for ref in refs[1:-1]:
            total = total + ref[...].astype(F32)
        refs[-1][...] = total.astype(BF)

    (out,), mark = run(
        "add_all",
        body,
        blocks,
        [WHOLE] * len(blocks),
        [jax.ShapeDtypeStruct(blocks[0].shape, BF)],
        [WHOLE],
        (),
        after,
    )
    return out, mark


def add_part(came, own, after):
    def body(came_ref, own_ref, out_ref):
        out_ref[...] = (came_ref[...].astype(F32) + own_ref[...]).astype(BF)

    size = came.shape
    (out,), mark = run(
        "add_part",
        body,
        (came, own),
        [WHOLE] * 2,
        [jax.ShapeDtypeStruct(size, BF)],
        [WHOLE],
        (),
        after,
    )
    return out, mark


def last_part(came, own, after):
    width, hid = came.shape[0] // 2, came.shape[1]

    def body(came_ref, own_ref, in_ref, down_ref):
        in_ref[0] = came_ref[:width, :].astype(F32) + own_ref[:width, :]
        down_ref[0] = (came_ref[width:, :].astype(F32) + own_ref[width:, :]).T

    return run(
        "last_part",
        body,
        (came, own),
        [WHOLE] * 2,
        [jax.ShapeDtypeStruct((1, width, hid), F32), jax.ShapeDtypeStruct((1, hid, width), F32)],
        [WHOLE] * 2,
        (),
        after,
    )


def assemble(me, pieces, after):
    rows, columns = pieces[0].shape
    count = len(pieces)
    width = count * rows

    def body(me_ref, *refs):
        qkv_ref, out_ref, small_ref, small = refs[count:]
        for k, piece in enumerate(refs[:count]):
            owner = me_ref[0] ^ k
            spot = pl.ds(pl.multiple_of(owner * rows, rows), rows)
            qkv_ref[spot, :] = piece[:, : 3 * width].astype(F32)
            out_ref[spot, :] = piece[:, 3 * width : 4 * width].astype(F32)
            small[spot, :] = piece[:, 4 * width :].astype(F32)
        small_ref[...] = small[...].T[:8]

    return run(
        "assemble",
        body,
        (me, *pieces),
        [SCALARS] + [WHOLE] * count,
        [
            jax.ShapeDtypeStruct((width, 3 * width), F32),
            jax.ShapeDtypeStruct((width, width), F32),
            jax.ShapeDtypeStruct((8, width), F32),
        ],
        [WHOLE] * 3,
        [pltpu.VMEM((width, columns - 4 * width), F32)],
        after,
    )


def sum_small(block, axis, after):
    def body(block_ref, sent_ref, out_ref):
        out_ref[...] = block_ref[...] + sent_ref[...]

    for distance in powers(lax.axis_size(axis)):
        (block,), mark = run(
            "add_small",
            body,
            (block, swap(block, axis, distance)),
            [WHOLE] * 2,
            [jax.ShapeDtypeStruct(block.shape, F32)],
            [WHOLE],
            (),
            after,
        )
        after = (mark,)
    return block, mark


def working_order(groups, capacity):
    unit = 128 // math.gcd(128, capacity)
    near = max(2, unit)
    order = sorted(range(near, groups), key=lambda k: (-k.bit_count(), k))
    half = (groups - near) // 2 // unit * unit
    return [list(range(near))[::-1], order[:half], order[half:]]


def shards(
    tokens,
    cotangent,
    w_qkv,
    bias_qv,
    w_out,
    out_bias,
    norm_gains,
    norm_shifts,
    gate_table,
    w_in,
    w_down,
    lengths,
    seg_task,
    routes,
):
    tok_count, width = tokens.shape
    groups = lax.axis_size("expert")
    planes = lax.axis_size("hidden")
    top_count = routes.shape[1]
    capacity = 3 * top_count * tok_count // (2 * groups * w_in.shape[0])
    me = lax.axis_index("expert").astype(jnp.int32).reshape(1)
    route_args = (lengths, seg_task, routes.T, gate_table.T)

    own, mark = join_weights(w_in, w_down)
    above = [own]
    above.append(turn(above[0], "hidden", 1))
    below = above[:1]
    for _ in range((planes - 1) // 2):
        below.append(turn(below[-1], "hidden", -1))

    grad_slots, mark = dispatch_grads(capacity, groups, *route_args, cotangent, (mark,))
    grad_rows = lax.all_to_all(grad_slots, "expert", split_axis=0, concat_axis=0, tiled=True)

    qkv, attended, hidden, one, slots, mark = forward(
        capacity,
        groups,
        me,
        *route_args,
        tokens,
        w_qkv,
        bias_qv,
        w_out,
        out_bias,
        norm_gains,
        norm_shifts,
        (mark,),
    )

    calls = working_order(groups, capacity)
    rows, dx_back, kept = {0: slots[0]}, {}, []
    for ids in calls:
        for k in ids:
            if k:
                rows[k] = swap(slots[k], "expert", k)
    above[1] = hold(above[1], (mark, *[rows[k] for k in calls[1][:HOLD]]))
    for _ in range(planes // 2 - 1):
        above.append(turn(above[-1], "hidden", 1))
    parts = above + below[:0:-1]

    for ids in calls:
        dxs, rest, mark = expert_rows(ids, me, [rows[k] for k in ids], grad_rows, parts, (mark,))
        kept.append(rest)
        for k, dx in zip(ids, dxs):
            dx_back[k] = swap(dx, "expert", k) if k else dx
    kept = [list(part) for part in zip(*kept)]

    (moving, *others), mark = weight_grads(
        [i % planes for i in range(1, 1 + planes // 2)], planes, BF, *kept, (mark,)
    )
    came = turn(moving, "hidden", 1)
    out_rows, mark = expert_outputs(calls, groups, capacity, me, kept[0], parts, (mark,))
    out_back = lax.all_to_all(out_rows, "expert", split_axis=0, concat_axis=0, tiled=True)

    keep, send, grad_hidden, dqkv, mark = backward(
        capacity,
        me,
        *route_args,
        cotangent,
        w_out,
        norm_gains,
        hidden,
        attended,
        qkv,
        one,
        [dx_back[k] for k in range(groups)],
        (mark,),
    )
    sent = swap(send, "expert", 1)
    part, mark = add_part(came, others.pop(0), (mark,))
    came = turn(part, "hidden", 1)
    input_grad, small_one, mark = last_back(dqkv, w_qkv, tokens, grad_hidden, norm_gains, (mark,))
    mine, mark = add_pairs(keep, sent, (mark,))
    sent = [swap(mine[j], "expert", 2 * j) for j in range(1, groups // 2)]
    fresh, mark = weight_grads(
        [i % planes for i in range(1 + planes // 2, planes + 1)], planes, F32, *kept, (mark,)
    )
    others += fresh
    total, mark = add_all([mine[0], *sent], (mark,))
    for step, distance in enumerate(powers(planes)):
        sent = swap(total, "hidden", distance)
        if step == 0:
            layer_out, small_two, mark = finish(
                *route_args, cotangent, hidden, out_back, (mark,)
            )
        total, mark = add_all([total, sent], (mark,))
    even = [total] + [swap(total, "expert", 2 * j) for j in range(1, groups // 2)]
    own = jnp.concatenate([small_one.reshape(-1, 128), small_two], axis=0)
    own, mark = sum_small(own, "hidden", (mark,))
    for other in others[:-1]:
        part, mark = add_part(came, other, (mark,))
        came = turn(part, "hidden", 1)
    odd = [swap(piece, "expert", 1) for piece in even]
    own, mark = sum_small(own, "expert", (mark, *even[1:]))
    (grad_qkv, grad_w_out, small), mark = assemble(
        me, [piece for pair in zip(even, odd) for piece in pair], (mark,)
    )
    (grad_w_in, grad_w_down), _ = last_part(came, others[-1], (mark,))

    first = own[:-2].reshape(2, width)
    return (
        layer_out,
        input_grad,
        grad_qkv,
        small[3:5],
        grad_w_out,
        small[2],
        jnp.stack([first[0], small[0]]),
        jnp.stack([first[1], small[1]]),
        own[-2:, : gate_table.shape[0]].T,
        grad_w_in,
        grad_w_down,
    )


def solution(mesh):
    split = P(("expert", "hidden"), None)
    return jax.shard_map(
        shards,
        mesh=mesh,
        in_specs=(
            split,
            split,
            P(),
            P(),
            P(),
            P(),
            P(),
            P(),
            P(),
            P("expert", None, "hidden"),
            P("expert", "hidden", None),
            split,
            split,
            P(),
        ),
        out_specs=(
            split,
            split,
            P(),
            P(),
            P(),
            P(),
            P(),
            P(),
            P(),
            P("expert", None, "hidden"),
            P("expert", "hidden", None),
        ),
        check_vma=False,
    )
```

```python
import functools
import math

import jax
import jax.numpy as jnp
from jax import lax
from jax.experimental import pallas as pl
from jax.experimental.pallas import tpu as pltpu
from jax.sharding import PartitionSpec as P

HEADS = 8
HD = 64
NORM_EPS = 1e-05
MASK_FILL = -1000000000.0

BF = jnp.bfloat16
F32 = jnp.float32
MIB = 1 << 20

ROWS = 256
REACH = 64
JOINT = 4
LANES = JOINT * HD
SMALL = 128


def iota(shape, dim):
    return lax.broadcasted_iota(jnp.int32, shape, dim)


def dot(left, right):
    return jnp.dot(left, right, preferred_element_type=F32)


def dot_nt(left, right):
    return lax.dot_general(left, right, (((1,), (1,)), ((), ())), preferred_element_type=F32)


def dot_tn(left, right):
    return lax.dot_general(left, right, (((0,), (0,)), ((), ())), preferred_element_type=F32)


def over_lanes(mask, values):
    return jnp.sum(jnp.where(mask, values, 0.0), axis=1, keepdims=True)


def over_rows(mask, values):
    return jnp.sum(jnp.where(mask, values, 0.0), axis=0, keepdims=True)


def to_column(row):
    count = row.shape[1]
    return over_lanes(iota((count, count), 0) == iota((count, count), 1), row)


def one_hot(mask):
    return mask.astype(F32).astype(BF)


WHOLE = pl.BlockSpec(memory_space=pltpu.VMEM)
SCALARS = pl.BlockSpec(memory_space=pltpu.SMEM)
ANYWHERE = pl.BlockSpec(memory_space=pl.ANY)


SCALE = 0.4
MICROS = {
    "dispatch_grads": 1,
    "forward": 1,
    "hold": 50,
    "expert_rows": 17,
    "weight_grads": 9,
    "expert_outputs": 11,
    "backward": 23,
    "last_back": 6,
    "finish": 12,
}
OTHER = 2


def run(name, body, args, in_specs, out_shape, out_specs, scratch=(), after=(), aliases=None):
    count, extra = len(args), len(after)

    def ordered(*refs):
        outs = refs[count + extra :]
        mark, rest = outs[len(out_shape)], outs[: len(out_shape)] + outs[len(out_shape) + 1 :]
        mark[...] = jnp.zeros_like(mark)
        body(*refs[:count], *rest)

    *results, mark = pl.pallas_call(
        ordered,
        out_shape=[*out_shape, jax.ShapeDtypeStruct((8, 128), F32)],
        in_specs=[*in_specs, *[ANYWHERE] * extra],
        out_specs=[*out_specs, WHOLE],
        scratch_shapes=list(scratch),
        input_output_aliases=aliases or {},
        compiler_params=pltpu.CompilerParams(vmem_limit_bytes=56 * MIB),
        cost_estimate=pl.CostEstimate(flops=int(1.15e9 * SCALE * MICROS.get(name, OTHER)), bytes_accessed=1 << 10, transcendentals=0),
        name=name,
    )(*args, *after)
    return results, mark


def join_weights(w_in, w_down):
    _, width, hid = w_in.shape

    def body(in_ref, down_ref, out_ref):
        out_ref[:width, :] = in_ref[0]
        out_ref[width:, :] = down_ref[0].T

    (out,), mark = run(
        "join_weights",
        body,
        (w_in, w_down),
        [WHOLE] * 2,
        [jax.ShapeDtypeStruct((2 * width, hid), BF)],
        [WHOLE],
    )
    return out, mark


def hold(block, after):
    (block,), _ = run(
        "hold",
        lambda *refs: None,
        (block,),
        [ANYWHERE],
        [jax.ShapeDtypeStruct(block.shape, block.dtype)],
        [ANYWHERE],
        (),
        after,
        {0: 0},
    )
    return block


class Copies:
    def __init__(self, sem):
        self.sem, self.count, self.open = sem, 0, []

    def start(self, source, target):
        copy = pltpu.make_async_copy(source, target, self.sem.at[self.count])
        copy.start()
        self.count += 1
        self.open.append(copy)
        return copy

    def wait(self):
        for copy in self.open:
            copy.wait()
        self.open = []


def centred_of(values):
    centred = values - jnp.mean(values, axis=-1, keepdims=True)
    spread = jnp.mean(centred * centred, axis=-1, keepdims=True)
    scale = lax.rsqrt(spread + NORM_EPS)
    return centred * scale, scale


def norm_back(grad, hat, scale, gain):
    scaled = grad * gain
    return scale * (
        scaled
        - jnp.mean(scaled, axis=-1, keepdims=True)
        - hat * jnp.mean(scaled * hat, axis=-1, keepdims=True)
    )


def sentence_bounds(lengths_ref):
    len_row = lengths_ref[...].astype(F32)
    count = len_row.shape[1]
    len_col = to_column(len_row)
    start_col = over_lanes(iota((count, count), 1) < iota((count, count), 0), len_row)
    start_row = over_rows(iota((count, count), 0) < iota((count, count), 1), len_col)
    return (len_row, len_col, start_row, start_col)


def routing(lengths_ref, task_ref, routes_ref, table_ref, me):
    len_row, len_col, start_row, start_col = sentence_bounds(lengths_ref)
    count = len_row.shape[1]
    tasks = routes_ref.shape[1]
    hit = iota((tasks, count), 0) == task_ref[...]
    expert_rows = [
        over_rows(hit, to_column(routes_ref[r : r + 1, :].astype(F32))) for r in range(2)
    ]
    logit_rows = [over_rows(hit, to_column(table_ref[r : r + 1, :])) for r in range(2)]
    peak = jnp.maximum(logit_rows[0], logit_rows[1])
    raised = [jnp.exp(row - peak) for row in logit_rows]
    gate_rows = [row / (raised[0] + raised[1]) for row in raised]
    expert_cols = [to_column(row) for row in expert_rows]
    earlier = iota((count, count), 0) < iota((count, count), 1)
    add_rows, far_rows = [], []
    for row in expert_rows:
        same = (expert_cols[0] == row) | (expert_cols[1] == row)
        add_rows.append(over_rows(earlier & same, len_col) - start_row)
        far_rows.append((row.astype(jnp.int32) ^ me).astype(F32))
    return (len_row, len_col, start_row, start_col, far_rows, gate_rows, add_rows)


def fill_slots(tables, data, capacity, groups, weighted):
    len_row, len_col, start_row, start_col, far_rows, gate_rows, add_rows = tables
    tok_count, count = data.shape[0], len_row.shape[1]
    place = iota((count, tok_count), 1).astype(F32)
    inside = (place >= start_col) & (place < start_col + len_col)
    token_place = iota((1, tok_count), 1).astype(F32)
    far = [over_rows(inside, to_column(row)) for row in far_rows]
    position = [token_place + over_rows(inside, to_column(row)) for row in add_rows]
    slots = iota((capacity, tok_count), 0)
    slot_column = iota((capacity, count), 0).astype(F32)
    for k in range(groups):
        slot = jnp.where(far[0] == k, position[0], jnp.where(far[1] == k, position[1], -1.0))
        picked = dot(one_hot(slots == slot.astype(jnp.int32)), data)
        if weighted:
            first, second = far_rows[0] == k, far_rows[1] == k
            base = jnp.where(first, add_rows[0], add_rows[1]) + start_row
            gate = jnp.where(first, gate_rows[0], jnp.where(second, gate_rows[1], 0.0))
            picked = picked * over_lanes((slot_column >= base) & (slot_column < base + len_row), gate)
        yield k, picked


def dispatch_body(len_ref, task_ref, routes_ref, table_ref, data_ref, out_ref, stage, sem):
    groups, capacity, _ = out_ref.shape
    copies = Copies(sem)
    tables = routing(len_ref, task_ref, routes_ref, table_ref, 0)
    for k, picked in fill_slots(tables, data_ref[...], capacity, groups, True):
        stage[k] = picked.astype(BF)
        copies.start(stage.at[k], out_ref.at[k])
    copies.wait()


def dispatch_grads(capacity, groups, lengths, seg_task, routes, gate_table, cotangent, after):
    slots = (groups, capacity, cotangent.shape[1])
    (out,), mark = run(
        "dispatch_grads",
        dispatch_body,
        (lengths, seg_task, routes, gate_table, cotangent),
        [WHOLE] * 5,
        [jax.ShapeDtypeStruct(slots, BF)],
        [ANYWHERE],
        [pltpu.VMEM(slots, BF), pltpu.SemaphoreType.DMA((groups,))],
        after,
    )
    return out, mark


def split_heads(block):
    head = iota(block.shape, 1) // HD
    zero = jnp.zeros_like(block)
    return jnp.concatenate([jnp.where(head == h, block, zero) for h in range(JOINT)], axis=0)


def join_heads(stacked):
    rows = stacked.shape[0] // JOINT
    head = iota((rows, stacked.shape[1]), 1) // HD
    out = stacked[:rows]
    for h in range(1, JOINT):
        out = jnp.where(head == h, stacked[h * rows : (h + 1) * rows], out)
    return out


def windows(lengths_ref, tok_count, queries):
    len_row, len_col, start_row, start_col = sentence_bounds(lengths_ref)
    end_row, end_col = start_row + len_row, start_col + len_col
    count = len_row.shape[1]
    keys = queries + 2 * REACH
    for block in range(tok_count // queries):
        start = min(max(block * queries - REACH, 0), tok_count - keys)
        query_place = (iota((count, queries), 1) + block * queries).astype(F32)
        query_seg = jnp.sum((query_place >= end_col).astype(F32), axis=0, keepdims=True)
        key_place = (iota((keys, count), 0) + start).astype(F32)
        key_seg = jnp.sum((key_place >= end_row).astype(F32), axis=1, keepdims=True)
        same = key_seg == jnp.concatenate([query_seg] * JOINT, axis=1)
        rows = slice(block * queries, (block + 1) * queries)
        yield rows, slice(start, start + keys), same


def softmax_of(key_rows, stacked, same):
    scores = jnp.where(same, dot_nt(key_rows, stacked), MASK_FILL)
    raised = jnp.exp(scores - jnp.max(scores, axis=0, keepdims=True))
    return raised * (1.0 / jnp.sum(raised, axis=0, keepdims=True))


def forward_body(
    capacity,
    groups,
    me_ref,
    len_ref,
    task_ref,
    routes_ref,
    table_ref,
    tok_ref,
    wqkv_ref,
    bias_ref,
    wout_ref,
    obias_ref,
    gains_ref,
    shifts_ref,
    *refs,
):
    qkv_out, att_out, hid_out, one_out = refs[:4]
    slot_out = refs[4 : 4 + groups]
    qkv, att, hid, one, two, stage, sem = refs[4 + groups :]
    tok_count, width = tok_ref.shape
    copies = Copies(sem)
    for step in range(tok_count // ROWS):
        rows = slice(step * ROWS, (step + 1) * ROWS)
        hat, _ = centred_of(tok_ref[rows, :].astype(F32))
        normed = (hat * gains_ref[0:1, :] + shifts_ref[0:1, :]).astype(BF)
        one[rows, :] = normed
        wide = dot(normed, wqkv_ref[...])
        queries = (wide[:, :width] + bias_ref[0:1, :]).astype(BF)
        qkv[rows, :width] = queries * jnp.asarray(HD**-0.5, BF)
        qkv[rows, width : 2 * width] = wide[:, width : 2 * width].astype(BF)
        qkv[rows, 2 * width :] = (wide[:, 2 * width :] + bias_ref[1:2, :]).astype(BF)
    copies.start(one, one_out)
    copies.start(qkv, qkv_out)
    for rows, keys, same in windows(len_ref, tok_count, REACH):
        for first in range(0, width, LANES):
            lanes = slice(first, first + LANES)
            key_rows = qkv[keys, width + first : width + first + LANES]
            value_rows = qkv[keys, 2 * width + first : 2 * width + first + LANES]
            probs = softmax_of(key_rows, split_heads(qkv[rows, lanes]), same).astype(BF)
            att[rows, lanes] = join_heads(dot_tn(probs, value_rows)).astype(BF)
    copies.start(att, att_out)
    for step in range(tok_count // ROWS):
        rows = slice(step * ROWS, (step + 1) * ROWS)
        hidden = tok_ref[rows, :].astype(F32) + dot(att[rows, :], wout_ref[...]) + obias_ref[...]
        hid[rows, :] = hidden
        hat, _ = centred_of(hidden)
        two[rows, :] = (hat * gains_ref[1:2, :] + shifts_ref[1:2, :]).astype(BF)
    copies.start(hid, hid_out)
    tables = routing(len_ref, task_ref, routes_ref, table_ref, me_ref[0])
    for k, picked in fill_slots(tables, two[...], capacity, groups, False):
        stage[k] = picked.astype(BF)
        copies.start(stage.at[k], slot_out[k])
    copies.wait()


def forward(
    capacity,
    groups,
    me,
    lengths,
    seg_task,
    routes,
    gate_table,
    tokens,
    w_qkv,
    bias_qv,
    w_out,
    out_bias,
    gains,
    shifts,
    after,
):
    tok_count, width = tokens.shape
    whole = [
        ((tok_count, 3 * width), BF),
        ((tok_count, width), BF),
        ((tok_count, width), F32),
        ((tok_count, width), BF),
    ]
    (qkv, att, hid, one, *slots), mark = run(
        "forward",
        functools.partial(forward_body, capacity, groups),
        (
            me,
            lengths,
            seg_task,
            routes,
            gate_table,
            tokens,
            w_qkv,
            bias_qv,
            w_out,
            out_bias.reshape(1, width),
            gains,
            shifts,
        ),
        [SCALARS] + [WHOLE] * 11,
        [jax.ShapeDtypeStruct(*kind) for kind in whole]
        + [jax.ShapeDtypeStruct((capacity, width), BF)] * groups,
        [ANYWHERE] * (4 + groups),
        [pltpu.VMEM(*kind) for kind in whole]
        + [
            pltpu.VMEM((tok_count, width), BF),
            pltpu.VMEM((groups, capacity, width), BF),
            pltpu.SemaphoreType.DMA((4 + groups,)),
        ],
        after,
    )
    return qkv, att, hid, one, slots, mark


GELU_A = 0.7978845608028654
GELU_B = 0.044715


def gelu_both(values):
    square = values * values
    inner = values * (GELU_A + (GELU_A * GELU_B) * square)
    half = 0.5 * jnp.tanh(inner) + 0.5
    active = values * half
    slope = half + active * (1.0 - half) * (2.0 * GELU_A + (6.0 * GELU_A * GELU_B) * square)
    return active, slope


def pieces_of(total, size):
    return [slice(i, min(i + size, total)) for i in range(0, total, size)]


def expert_body(ids, planes, me_ref, *refs):
    refs = list(refs)
    take = lambda count: [refs.pop(0) for _ in range(count)]
    blocks = len(ids)
    x_in, (g_in,), parts = take(blocks), take(1), take(planes)
    dx_out = take(blocks)
    act_out, pre_out, xt_out, gt_out = take(4)
    xs, gs, w_in, w_down, act, pre, xt, gt, dx, sem = refs
    cap, width = x_in[0].shape
    hid = parts[0].shape[1]
    rows = blocks * cap
    me = me_ref[0]
    copies = Copies(sem)
    for i, k in enumerate(ids):
        copies.start(x_in[i], xs.at[pl.ds(i * cap, cap)])
        copies.start(g_in.at[me ^ k], gs.at[pl.ds(i * cap, cap)])
    rows_there, copies.open = copies.open, []
    parts_there = []
    for c in range(planes):
        lanes = pl.ds(c * hid, hid)
        copies.start(parts[c].at[pl.ds(0, width)], w_in.at[:, lanes])
        copies.start(parts[c].at[pl.ds(width, width)], w_down.at[:, lanes])
        parts_there.append(copies.open)
        copies.open = []
    for copy in rows_there:
        copy.wait()
    for c in range(planes):
        for copy in parts_there[c]:
            copy.wait()
        lanes = slice(c * hid, (c + 1) * hid)
        for spot in pieces_of(rows, 3 * cap):
            active, slope = gelu_both(dot(xs[spot, :], w_in[:, lanes]))
            act[spot, lanes] = active.astype(BF)
            pre[spot, lanes] = (dot(gs[spot, :], w_down[:, lanes]) * slope).astype(BF)
        copies.start(act.at[:, pl.ds(c * hid, hid)], act_out.at[:, pl.ds(c * hid, hid)])
        copies.start(pre.at[:, pl.ds(c * hid, hid)], pre_out.at[:, pl.ds(c * hid, hid)])
        if c == 0:
            xt[...] = xs[...].T
            copies.start(xt, xt_out)
            gt[...] = gs[...].T
            copies.start(gt, gt_out)
    for i, spot in enumerate(pieces_of(rows, 3 * cap)):
        dx[spot, :] = dot_nt(pre[spot, :], w_in[...]).astype(BF)
        for j in range(spot.start // cap, spot.stop // cap):
            copies.start(dx.at[pl.ds(j * cap, cap)], dx_out[j])
    copies.wait()


def expert_rows(ids, me, x_blocks, g_rows, parts, after):
    blocks, planes = len(ids), len(parts)
    cap, width = x_blocks[0].shape
    hid = parts[0].shape[1]
    rows = blocks * cap
    units, turned = (rows, planes * hid), (width, rows)
    result, mark = run(
        "expert_rows",
        functools.partial(expert_body, ids, planes),
        (me, *x_blocks, g_rows, *parts),
        [SCALARS] + [ANYWHERE] * (blocks + 1 + planes),
        [jax.ShapeDtypeStruct((cap, width), BF)] * blocks
        + [jax.ShapeDtypeStruct(units, BF)] * 2
        + [jax.ShapeDtypeStruct(turned, BF)] * 2,
        [ANYWHERE] * (blocks + 4),
        [
            pltpu.VMEM((rows, width), BF),
            pltpu.VMEM((rows, width), BF),
            pltpu.VMEM((width, planes * hid), BF),
            pltpu.VMEM((width, planes * hid), BF),
            pltpu.VMEM(units, BF),
            pltpu.VMEM(units, BF),
            pltpu.VMEM(turned, BF),
            pltpu.VMEM(turned, BF),
            pltpu.VMEM((rows, width), BF),
            pltpu.SemaphoreType.DMA((3 * blocks + 4 * planes + 2,)),
        ],
        after,
    )
    return result[:blocks], result[blocks:], mark


def output_body(calls, planes, me_ref, *refs):
    act_in, parts = refs[: len(calls)], refs[len(calls) : len(calls) + planes]
    out_ref, act, w_down, stage, sem = refs[len(calls) + planes :]
    _, capacity, width = out_ref.shape
    hid = parts[0].shape[1]
    copies = Copies(sem)
    for c, part in enumerate(parts):
        copies.start(part.at[pl.ds(width, width)], w_down.at[:, pl.ds(c * hid, hid)])
    there, copies.open = copies.open, []
    there_rows, spot = [], 0
    for ids, units in zip(calls, act_in):
        size = len(ids) * capacity
        there_rows.append(copies.start(units, act.at[pl.ds(spot, size)]))
        spot += size
    copies.open = []
    for copy in there:
        copy.wait()
    spot = 0
    for ids, copy in zip(calls, there_rows):
        copy.wait()
        size = len(ids) * capacity
        stage[spot : spot + size, :] = dot_nt(act[spot : spot + size, :], w_down[...]).astype(BF)
        for k in ids:
            copies.start(stage.at[pl.ds(spot, capacity)], out_ref.at[me_ref[0] ^ k])
            spot += capacity
    copies.wait()


def expert_outputs(calls, groups, capacity, me, act, parts, after):
    planes = len(parts)
    width, hid = parts[0].shape[0] // 2, parts[0].shape[1]
    (out,), mark = run(
        "expert_outputs",
        functools.partial(output_body, calls, planes),
        (me, *act, *parts),
        [SCALARS] + [ANYWHERE] * (len(act) + planes),
        [jax.ShapeDtypeStruct((groups, capacity, width), BF)],
        [ANYWHERE],
        [
            pltpu.VMEM((groups * capacity, planes * hid), BF),
            pltpu.VMEM((width, planes * hid), BF),
            pltpu.VMEM((groups * capacity, width), BF),
            pltpu.SemaphoreType.DMA((planes + len(calls) + groups,)),
        ],
        after,
    )
    return out, mark


def weight_body(which, calls, *refs):
    act_in, pre_in, xt_in, gt_in = (refs[i * calls : (i + 1) * calls] for i in range(4))
    out_refs = refs[4 * calls : 4 * calls + len(which)]
    act, pre, xt, gt, stage, sem = refs[4 * calls + len(which) :]
    width, hid = xt.shape[0], act.shape[2]
    spots, total = [], 0
    for turned in xt_in:
        spots.append(pl.ds(total, turned.shape[1]))
        total += turned.shape[1]
    copies = Copies(sem)
    there = []

    def work(n):
        for copy in there[n]:
            copy.wait()
        for i, (turned, units) in enumerate(((xt, pre), (gt, act))):
            spot = pl.ds(i * width, width)
            stage[n, spot, :] = dot(turned[...], units[n % 2]).astype(stage.dtype)
            copies.start(stage.at[n, spot], out_refs[n].at[spot])

    for n, c in enumerate(which):
        lanes = pl.ds(c * hid, hid)
        done, copies.open = copies.open, []
        for i, spot in enumerate(spots):
            if n == 0:
                copies.start(xt_in[i], xt.at[:, spot])
                copies.start(gt_in[i], gt.at[:, spot])
            copies.start(pre_in[i].at[:, lanes], pre.at[n % 2, spot])
            copies.start(act_in[i].at[:, lanes], act.at[n % 2, spot])
        there.append(copies.open)
        copies.open = done
        if n:
            work(n - 1)
    work(len(which) - 1)
    copies.wait()


def weight_grads(which, planes, dtype, act, pre, xt, gt, after):
    calls = len(act)
    width, rows = xt[0].shape[0], sum(turned.shape[1] for turned in xt)
    hid = act[0].shape[1] // planes
    return run(
        "weight_grads",
        functools.partial(weight_body, which, calls),
        (*act, *pre, *xt, *gt),
        [ANYWHERE] * (4 * calls),
        [jax.ShapeDtypeStruct((2 * width, hid), dtype)] * len(which),
        [ANYWHERE] * len(which),
        [
            pltpu.VMEM((2, rows, hid), BF),
            pltpu.VMEM((2, rows, hid), BF),
            pltpu.VMEM((width, rows), BF),
            pltpu.VMEM((width, rows), BF),
            pltpu.VMEM((len(which), 2 * width, hid), dtype),
            pltpu.SemaphoreType.DMA((2 * calls * (len(which) + 1) + 2 * len(which),)),
        ],
        after,
    )


def token_slots(tables, tok_count, capacity):
    len_row, _, start_row, _, far_rows, gate_rows, add_rows = tables
    count = len_row.shape[1]
    place = iota((tok_count, count), 0).astype(F32)
    inside = (place >= start_row) & (place < start_row + len_row)
    columns = []
    for far, add in zip(far_rows, add_rows):
        kept = inside & (place + add < capacity)
        columns.append(over_lanes(kept, place + (add + far * capacity + 1.0)) - 1.0)
    gates = [over_lanes(inside, row) for row in gate_rows]
    return columns, gates, inside


def backward_body(
    groups,
    capacity,
    me_ref,
    len_ref,
    task_ref,
    routes_ref,
    table_ref,
    cot_ref,
    wout_ref,
    gains_ref,
    hid_in,
    att_in,
    qkv_in,
    one_in,
    *refs,
):
    back_in = refs[:groups]
    keep_ref, send_ref, grad_out, dqkv_out = refs[groups : groups + 4]
    back, side, hid, att, qkv, one, grad_all, low, gatt, dqkv, total, sem = refs[groups + 4 :]
    copies = Copies(sem)
    for i, ref in enumerate(back_in):
        copies.start(ref, back.at[pl.ds(i * capacity, capacity)])
    copies.start(hid_in, hid)
    first, copies.open = copies.open, []
    att_there = copies.start(att_in, att)
    qkv_there = copies.start(qkv_in, qkv)
    one_there = copies.start(one_in, one)
    copies.open = []
    tok_count, width = cot_ref.shape
    me = me_ref[0]
    tables = routing(len_ref, task_ref, routes_ref, table_ref, me)
    columns, _, _ = token_slots(tables, tok_count, capacity)
    for i, column in enumerate(columns):
        side[:, i : i + 1] = column.astype(jnp.int32)
    for copy in first:
        copy.wait()
    sums = [jnp.zeros((1, width), F32)] * 3
    for step in range(tok_count // ROWS):
        rows = slice(step * ROWS, (step + 1) * ROWS)
        slots = iota((ROWS, groups * capacity), 1)
        hit = (slots == side[rows, 0:1]) | (slots == side[rows, 1:2])
        grad_two = dot(one_hot(hit), back[...])
        hat, scale = centred_of(hid[rows, :])
        grad = cot_ref[rows, :].astype(F32) + norm_back(grad_two, hat, scale, gains_ref[1:2, :])
        grad_all[rows, :] = grad
        for i, part in enumerate((grad_two * hat, grad_two, grad)):
            sums[i] = sums[i] + jnp.sum(part, axis=0, keepdims=True)
        low[rows, :] = grad.astype(BF)
        gatt[rows, :] = dot_nt(low[rows, :], wout_ref[...]).astype(BF)
    copies.start(grad_all, grad_out)
    att_there.wait()
    total[:, 3 * width : 4 * width] = dot_tn(att[...], low[...])

    qkv_there.wait()
    open_sums = [({}, {}) for _ in range(width // LANES)]
    bias_sums = {}
    spans = list(windows(len_ref, tok_count, 2 * REACH))
    for index, (rows, keys, same) in enumerate(spans):
        next_key = spans[index + 1][1].start if index + 1 < len(spans) else tok_count
        for group, lane in enumerate(range(0, width, LANES)):
            lanes = slice(lane, lane + LANES)
            key_lanes = slice(width + lane, width + lane + LANES)
            value_lanes = slice(2 * width + lane, 2 * width + lane + LANES)
            stacked, grads = split_heads(qkv[rows, lanes]), split_heads(gatt[rows, lanes])
            key_rows, value_rows = qkv[keys, key_lanes], qkv[keys, value_lanes]
            probs = softmax_of(key_rows, stacked, same)
            grad_probs = dot_nt(value_rows, grads)
            inner = jnp.sum(probs * grad_probs, axis=0, keepdims=True)
            grad_scores = (probs * (grad_probs - inner)).astype(BF)
            grad_values = dot(probs.astype(BF), grads)
            grad_keys = dot(grad_scores, stacked)
            grad_queries = join_heads(dot_tn(grad_scores, key_rows)) * HD**-0.5
            dqkv[rows, lanes] = grad_queries.astype(BF)
            for held, fresh, target in zip(
                open_sums[group], (grad_keys, grad_values), (key_lanes, value_lanes)
            ):
                for i in range(0, fresh.shape[0], REACH):
                    place = keys.start + i
                    part = fresh[i : i + REACH]
                    held[place] = held[place] + part if place in held else part
                for place in [place for place in held if place < next_key]:
                    dqkv[place : place + REACH, target] = held.pop(place).astype(BF)
    copies.start(dqkv, dqkv_out)
    ones = jnp.ones((8, tok_count), BF)
    bias = [dot(ones, dqkv[:, :width])[0:1], dot(ones, dqkv[:, 2 * width :])[0:1]]
    short = jnp.concatenate(sums + bias + [jnp.zeros((SMALL - 5, width), F32)], axis=0)
    total[:, 4 * width :] = short.T
    one_there.wait()
    total[:, : 3 * width] = dot_tn(one[...], dqkv[...])
    half, rows, _ = keep_ref.shape
    for j in range(half):
        for bit, ref in enumerate((keep_ref, send_ref)):
            owner = me ^ (2 * j + bit)
            ref[j] = total[pl.ds(pl.multiple_of(owner * rows, rows), rows), :].astype(BF)
    copies.wait()


def backward(
    capacity,
    me,
    lengths,
    seg_task,
    routes,
    gate_table,
    cotangent,
    w_out,
    gains,
    hidden,
    attended,
    qkv,
    one,
    back,
    after,
):
    tok_count, width = cotangent.shape
    groups = len(back)
    columns = 4 * width + SMALL
    pieces = jax.ShapeDtypeStruct((groups // 2, width // groups, columns), BF)
    (keep, send, grad, dqkv), mark = run(
        "backward",
        functools.partial(backward_body, groups, capacity),
        (
            me,
            lengths,
            seg_task,
            routes,
            gate_table,
            cotangent,
            w_out,
            gains,
            hidden,
            attended,
            qkv,
            one,
            *back,
        ),
        [SCALARS] + [WHOLE] * 7 + [ANYWHERE] * (4 + groups),
        [
            pieces,
            pieces,
            jax.ShapeDtypeStruct((tok_count, width), F32),
            jax.ShapeDtypeStruct((tok_count, 3 * width), BF),
        ],
        [WHOLE, WHOLE, ANYWHERE, ANYWHERE],
        [
            pltpu.VMEM((groups * capacity, width), BF),
            pltpu.VMEM((tok_count, 2), jnp.int32),
            pltpu.VMEM((tok_count, width), F32),
            pltpu.VMEM((tok_count, width), BF),
            pltpu.VMEM((tok_count, 3 * width), BF),
            pltpu.VMEM((tok_count, width), BF),
            pltpu.VMEM((tok_count, width), F32),
            pltpu.VMEM((tok_count, width), BF),
            pltpu.VMEM((tok_count, width), BF),
            pltpu.VMEM((tok_count, 3 * width), BF),
            pltpu.VMEM((width, columns), F32),
            pltpu.SemaphoreType.DMA((groups + 6,)),
        ],
        after,
    )
    return keep, send, grad, dqkv, mark


def last_body(dqkv_ref, wqkv_ref, tok_ref, grad_ref, gains_ref, out_ref, small_ref):
    tok_count, width = tok_ref.shape
    sums = [jnp.zeros((1, width), F32)] * 2
    for step in range(tok_count // ROWS):
        rows = slice(step * ROWS, (step + 1) * ROWS)
        grad_one = dot_nt(dqkv_ref[rows, :], wqkv_ref[...])
        hat, scale = centred_of(tok_ref[rows, :].astype(F32))
        back = norm_back(grad_one, hat, scale, gains_ref[0:1, :])
        out_ref[rows, :] = (grad_ref[rows, :] + back).astype(BF)
        for i, part in enumerate((grad_one * hat, grad_one)):
            sums[i] = sums[i] + jnp.sum(part, axis=0, keepdims=True)
    small_ref[...] = jnp.concatenate(sums, axis=0)


def last_back(dqkv, w_qkv, tokens, grad_hidden, gains, after):
    tok_count, width = tokens.shape
    (out, small), mark = run(
        "last_back",
        last_body,
        (dqkv, w_qkv, tokens, grad_hidden, gains),
        [WHOLE] * 5,
        [jax.ShapeDtypeStruct((tok_count, width), BF), jax.ShapeDtypeStruct((2, width), F32)],
        [WHOLE] * 2,
        (),
        after,
    )
    return out, small, mark


def finish_body(
    len_ref,
    task_ref,
    routes_ref,
    table_ref,
    cot_ref,
    hid_ref,
    back_in,
    small_ref,
    out_ref,
    short_ref,
    back,
    side_ref,
    sem,
):
    groups, capacity, _ = back_in.shape
    copies = Copies(sem)
    for i in range(groups):
        copies.start(back_in.at[i], back.at[pl.ds(i * capacity, capacity)])
    tok_count, width = cot_ref.shape
    tables = routing(len_ref, task_ref, routes_ref, table_ref, 0)
    columns, gates, inside = token_slots(tables, tok_count, capacity)
    task_col = over_lanes(inside, task_ref[...].astype(F32))
    for i, column in enumerate(columns + gates + [task_col]):
        side_ref[:, i : i + 1] = column
    copies.wait()
    gate_sums = [jnp.zeros((1, 128), F32)] * 2
    for step in range(tok_count // ROWS):
        rows = slice(step * ROWS, (step + 1) * ROWS)
        slots = iota((ROWS, groups * capacity), 1)
        side = side_ref[rows, :]
        cot = cot_ref[rows, :].astype(F32)
        mixed = hid_ref[rows, :]
        inner = jnp.zeros((ROWS, 1), F32)
        parts = []
        for r in range(2):
            hit = slots == side[:, r : r + 1].astype(jnp.int32)
            picked = dot(one_hot(hit), back[...])
            gate = side[:, 2 + r : 3 + r]
            mixed = mixed + gate * picked
            grad = jnp.sum(cot * picked, axis=1, keepdims=True)
            parts.append((gate, grad))
            inner = inner + gate * grad
        out_ref[rows, :] = mixed.astype(BF)
        task = iota((ROWS, 128), 1) == side[:, 4:5].astype(jnp.int32)
        for r, (gate, grad) in enumerate(parts):
            gate_sums[r] = gate_sums[r] + over_rows(task, gate * (grad - inner))
    wide = width // 128
    for i in range(2):
        for j in range(wide):
            short_ref[i * wide + j : i * wide + j + 1, :] = small_ref[
                i : i + 1, j * 128 : (j + 1) * 128
            ]
    short_ref[2 * wide : 2 * wide + 2, :] = jnp.concatenate(gate_sums, axis=0)


def finish(lengths, seg_task, routes, gate_table, cotangent, hidden, back, small, after):
    tok_count, width = cotangent.shape
    groups, capacity, _ = back.shape
    (out, gate), mark = run(
        "finish",
        finish_body,
        (lengths, seg_task, routes, gate_table, cotangent, hidden, back, small),
        [WHOLE] * 6 + [ANYWHERE, WHOLE],
        [
            jax.ShapeDtypeStruct((tok_count, width), BF),
            jax.ShapeDtypeStruct((2 * width // 128 + 2, 128), F32),
        ],
        [WHOLE] * 2,
        [
            pltpu.VMEM((groups * capacity, width), BF),
            pltpu.VMEM((tok_count, 8), F32),
            pltpu.SemaphoreType.DMA((groups,)),
        ],
        after,
    )
    return out, gate, mark


def swap(block, axis, distance):
    count = lax.axis_size(axis)
    return lax.ppermute(block, axis, [(s, s ^ distance) for s in range(count)])


def turn(block, axis, distance):
    count = lax.axis_size(axis)
    return lax.ppermute(block, axis, [(s, (s + distance) % count) for s in range(count)])


def powers(count):
    return [1 << i for i in range(count.bit_length() - 1)]


def add_pairs(keep, came, after):
    count, rows, columns = keep.shape

    def body(keep_ref, came_ref, *out_refs):
        for j, out_ref in enumerate(out_refs):
            out_ref[...] = (keep_ref[j].astype(F32) + came_ref[j].astype(F32)).astype(BF)

    return run(
        "add_pairs",
        body,
        (keep, came),
        [WHOLE] * 2,
        [jax.ShapeDtypeStruct((rows, columns), BF)] * count,
        [WHOLE] * count,
        (),
        after,
    )


def add_all(blocks, after):
    def body(*refs):
        total = refs[0][...].astype(F32)
        for ref in refs[1:-1]:
            total = total + ref[...].astype(F32)
        refs[-1][...] = total.astype(BF)

    (out,), mark = run(
        "add_all",
        body,
        blocks,
        [WHOLE] * len(blocks),
        [jax.ShapeDtypeStruct(blocks[0].shape, BF)],
        [WHOLE],
        (),
        after,
    )
    return out, mark


def add_part(came, own, after):
    def body(came_ref, own_ref, out_ref):
        out_ref[...] = (came_ref[...].astype(F32) + own_ref[...].astype(F32)).astype(BF)

    size = came.shape
    (out,), mark = run(
        "add_part",
        body,
        (came, own),
        [WHOLE] * 2,
        [jax.ShapeDtypeStruct(size, BF)],
        [WHOLE],
        (),
        after,
    )
    return out, mark


def last_part(came, own, after):
    width, hid = own.shape[0] // 2, own.shape[1]

    def body(*refs):
        *came_refs, own_ref, in_ref, down_ref = refs

        def total(spot):
            sums = own_ref[spot, :]
            for ref in came_refs:
                sums = sums + ref[spot, :].astype(F32)
            return sums

        in_ref[0] = total(slice(0, width))
        down_ref[0] = total(slice(width, 2 * width)).T

    return run(
        "last_part",
        body,
        (*came, own),
        [WHOLE] * (len(came) + 1),
        [jax.ShapeDtypeStruct((1, width, hid), F32), jax.ShapeDtypeStruct((1, hid, width), F32)],
        [WHOLE] * 2,
        (),
        after,
    )


def assemble(me, pieces, short, tasks, after):
    rows, columns = pieces[0].shape
    count = len(pieces)
    width = count * rows
    wide = width // 128

    def body(me_ref, short_ref, *refs):
        qkv_ref, bias_ref, out_ref, obias_ref, gains_ref, shifts_ref, gate_ref, small = refs[count:]
        for k, piece in enumerate(refs[:count]):
            owner = me_ref[0] ^ k
            spot = pl.ds(pl.multiple_of(owner * rows, rows), rows)
            qkv_ref[spot, :] = piece[:, : 3 * width].astype(F32)
            out_ref[spot, :] = piece[:, 3 * width : 4 * width].astype(F32)
            small[spot, :] = piece[:, 4 * width :].astype(F32)
        turned = small[...].T
        for i, ref in enumerate((gains_ref, shifts_ref)):
            parts = [short_ref[j : j + 1, :] for j in range(i * wide, (i + 1) * wide)]
            ref[0:1, :] = jnp.concatenate(parts, axis=1)
            ref[1:2, :] = turned[i : i + 1]
        obias_ref[...] = turned[2:3]
        bias_ref[...] = turned[3:5]
        gate_ref[...] = short_ref[2 * wide : 2 * wide + 2, :tasks]

    pair = jax.ShapeDtypeStruct((2, width), F32)
    return run(
        "assemble",
        body,
        (me, short, *pieces),
        [SCALARS] + [WHOLE] * (count + 1),
        [
            jax.ShapeDtypeStruct((width, 3 * width), F32),
            pair,
            jax.ShapeDtypeStruct((width, width), F32),
            jax.ShapeDtypeStruct((1, width), F32),
            pair,
            pair,
            jax.ShapeDtypeStruct((2, tasks), F32),
        ],
        [WHOLE] * 7,
        [pltpu.VMEM((width, columns - 4 * width), F32)],
        after,
    )


def add_small(block, axis, distance, mark, after=()):
    def body(block_ref, sent_ref, out_ref):
        out_ref[...] = block_ref[...] + sent_ref[...]

    (block,), mark = run(
        "add_small",
        body,
        (block, swap(block, axis, distance)),
        [WHOLE] * 2,
        [jax.ShapeDtypeStruct(block.shape, F32)],
        [WHOLE],
        (),
        (mark, *after),
    )
    return block, mark


def working_order(groups, capacity):
    unit = 128 // math.gcd(128, capacity)
    near = max(2, unit)
    order = sorted(range(near, groups), key=lambda k: (-k.bit_count(), k))
    half = (groups - near) // 2 // unit * unit
    return [list(range(near))[::-1], order[:half], order[half:]]


def shards(
    tokens,
    cotangent,
    w_qkv,
    bias_qv,
    w_out,
    out_bias,
    norm_gains,
    norm_shifts,
    gate_table,
    w_in,
    w_down,
    lengths,
    seg_task,
    routes,
):
    tok_count, width = tokens.shape
    groups = lax.axis_size("expert")
    planes = lax.axis_size("hidden")
    top_count = routes.shape[1]
    capacity = 3 * top_count * tok_count // (2 * groups * w_in.shape[0])
    me = lax.axis_index("expert").astype(jnp.int32).reshape(1)
    route_args = (lengths, seg_task, routes.T, gate_table.T)

    own, mark = join_weights(w_in, w_down)
    above = [own]
    above.append(turn(above[0], "hidden", 1))
    below = above[:1]
    for _ in range((planes - 1) // 2):
        below.append(turn(below[-1], "hidden", -1))

    grad_slots, mark = dispatch_grads(capacity, groups, *route_args, cotangent, (mark,))
    grad_rows = lax.all_to_all(grad_slots, "expert", split_axis=0, concat_axis=0, tiled=True)

    qkv, attended, hidden, one, slots, mark = forward(
        capacity,
        groups,
        me,
        *route_args,
        tokens,
        w_qkv,
        bias_qv,
        w_out,
        out_bias,
        norm_gains,
        norm_shifts,
        (mark,),
    )

    calls = working_order(groups, capacity)
    rows, dx_back, kept = {0: slots[0]}, {}, []
    for ids in calls:
        for k in ids:
            if k:
                rows[k] = swap(slots[k], "expert", k)
    above[1] = hold(above[1], (mark, *below[1:2], *[rows[k] for k in calls[1][:1]]))
    for _ in range(planes // 2 - 1):
        above.append(turn(above[-1], "hidden", 1))
    parts = above + below[:0:-1]

    for ids in calls:
        dxs, rest, mark = expert_rows(ids, me, [rows[k] for k in ids], grad_rows, parts, (mark,))
        kept.append(rest)
        for k, dx in zip(ids, dxs):
            dx_back[k] = swap(dx, "expert", k) if k else dx
    kept = [list(part) for part in zip(*kept)]

    middle = planes // 2
    rising, falling = list(range(middle, planes)), list(range(middle - 1, 0, -1))
    which = sorted(rising + falling, key=lambda c: abs(2 * c - planes))
    fresh, mark = weight_grads(which, planes, BF, *kept, (mark,))
    partial = dict(zip(which, fresh))
    risen = turn(partial[rising[0]], "hidden", 1)
    fallen = [turn(partial[falling[0]], "hidden", -1)] if falling else []
    out_rows, mark = expert_outputs(
        calls, groups, capacity, me, kept[0], parts, (mark,)
    )
    out_back = lax.all_to_all(out_rows, "expert", split_axis=0, concat_axis=0, tiled=True)

    keep, send, grad_hidden, dqkv, mark = backward(
        capacity,
        me,
        *route_args,
        cotangent,
        w_out,
        norm_gains,
        hidden,
        attended,
        qkv,
        one,
        [dx_back[k] for k in range(groups)],
        (mark,),
    )
    sent = swap(send, "expert", 1)
    for c in rising[1:]:
        part, mark = add_part(risen, partial[c], (mark,))
        risen = turn(part, "hidden", 1)
    for c in falling[1:]:
        part, mark = add_part(fallen[0], partial[c], (mark,))
        fallen = [turn(part, "hidden", -1)]
    mine, mark = add_pairs(keep, sent, (mark,))
    sent = [swap(mine[j], "expert", 2 * j) for j in range(1, groups // 2)]
    (whole,), mark = weight_grads(
        [0], planes, F32, *kept, (mark,)
    )
    input_grad, small_one, mark = last_back(dqkv, w_qkv, tokens, grad_hidden, norm_gains, (mark, *fallen)
    )
    total, mark = add_all([mine[0], *sent], (mark,))
    hops = powers(planes)
    for step, distance in enumerate(hops):
        sent = swap(total, "hidden", distance)
        if step == 0:
            layer_out, short, mark = finish(
                *route_args, cotangent, hidden, out_back, small_one, (mark,)
            )
        if step == len(hops) - 1:
            for near in powers(groups):
                short, mark = add_small(short, "expert", near, mark)
        total, mark = add_all([total, sent], (mark,))
    even = [total] + [swap(total, "expert", 2 * j) for j in range(1, groups // 2)]
    for distance in hops:
        short, mark = add_small(short, "hidden", distance, mark)
    (grad_w_in, grad_w_down), mark = last_part([risen, *fallen], whole, (mark,))
    odd = [swap(piece, "expert", 1) for piece in even]
    results, mark = assemble(
        me, [piece for pair in zip(even, odd) for piece in pair], short, gate_table.shape[0], (mark,)
    )
    grad_qkv, grad_bias_qv, grad_w_out, grad_out_bias, grad_gains, grad_shifts, grad_gate = results
    return (
        layer_out,
        input_grad,
        grad_qkv,
        grad_bias_qv,
        grad_w_out,
        grad_out_bias[0],
        grad_gains,
        grad_shifts,
        grad_gate.T,
        grad_w_in,
        grad_w_down,
    )


def solution(mesh):
    split = P(("expert", "hidden"), None)
    return jax.shard_map(
        shards,
        mesh=mesh,
        in_specs=(
            split,
            split,
            P(),
            P(),
            P(),
            P(),
            P(),
            P(),
            P(),
            P("expert", None, "hidden"),
            P("expert", "hidden", None),
            split,
            split,
            P(),
        ),
        out_specs=(
            split,
            split,
            P(),
            P(),
            P(),
            P(),
            P(),
            P(),
            P(),
            P("expert", None, "hidden"),
            P("expert", "hidden", None),
        ),
        check_vma=False,
    )
```

```python
import functools
import math

import jax
import jax.numpy as jnp
from jax import lax
from jax.experimental import pallas as pl
from jax.experimental.pallas import tpu as pltpu
from jax.sharding import PartitionSpec as P

HEADS = 8
HD = 64
NORM_EPS = 1e-05
MASK_FILL = -1000000000.0

BF = jnp.bfloat16
F32 = jnp.float32
MIB = 1 << 20

ROWS = 256
REACH = 64
JOINT = 4
LANES = JOINT * HD
SMALL = 128


def iota(shape, dim):
    return lax.broadcasted_iota(jnp.int32, shape, dim)


def dot(left, right):
    return jnp.dot(left, right, preferred_element_type=F32)


def dot_nt(left, right):
    return lax.dot_general(left, right, (((1,), (1,)), ((), ())), preferred_element_type=F32)


def dot_tn(left, right):
    return lax.dot_general(left, right, (((0,), (0,)), ((), ())), preferred_element_type=F32)


def over_lanes(mask, values):
    return jnp.sum(jnp.where(mask, values, 0.0), axis=1, keepdims=True)


def over_rows(mask, values):
    return jnp.sum(jnp.where(mask, values, 0.0), axis=0, keepdims=True)


def to_column(row):
    count = row.shape[1]
    return over_lanes(iota((count, count), 0) == iota((count, count), 1), row)


def one_hot(mask):
    return mask.astype(F32).astype(BF)


WHOLE = pl.BlockSpec(memory_space=pltpu.VMEM)
SCALARS = pl.BlockSpec(memory_space=pltpu.SMEM)
ANYWHERE = pl.BlockSpec(memory_space=pl.ANY)


SCALE = 0.4
MICROS = {
    "dispatch_grads": 1,
    "forward": 1,
    "hold": 50,
    "expert_rows": 17,
    "weight_grads": 9,
    "expert_outputs": 11,
    "backward": 23,
    "last_back": 6,
    "finish": 12,
}
OTHER = 2


def run(name, body, args, in_specs, out_shape, out_specs, scratch=(), after=(), aliases=None):
    count, extra = len(args), len(after)

    def ordered(*refs):
        outs = refs[count + extra :]
        mark, rest = outs[len(out_shape)], outs[: len(out_shape)] + outs[len(out_shape) + 1 :]
        mark[...] = jnp.zeros_like(mark)
        body(*refs[:count], *rest)

    *results, mark = pl.pallas_call(
        ordered,
        out_shape=[*out_shape, jax.ShapeDtypeStruct((8, 128), F32)],
        in_specs=[*in_specs, *[ANYWHERE] * extra],
        out_specs=[*out_specs, WHOLE],
        scratch_shapes=list(scratch),
        input_output_aliases=aliases or {},
        compiler_params=pltpu.CompilerParams(vmem_limit_bytes=56 * MIB),
        cost_estimate=pl.CostEstimate(flops=int(1.15e9 * SCALE * MICROS.get(name, OTHER)), bytes_accessed=1 << 10, transcendentals=0),
        name=name,
    )(*args, *after)
    return results, mark


def join_weights(w_in, w_down):
    _, width, hid = w_in.shape

    def body(in_ref, down_ref, out_ref):
        out_ref[:width, :] = in_ref[0]
        out_ref[width:, :] = down_ref[0].T

    (out,), mark = run(
        "join_weights",
        body,
        (w_in, w_down),
        [WHOLE] * 2,
        [jax.ShapeDtypeStruct((2 * width, hid), BF)],
        [WHOLE],
    )
    return out, mark


def hold(block, after):
    (block,), _ = run(
        "hold",
        lambda *refs: None,
        (block,),
        [ANYWHERE],
        [jax.ShapeDtypeStruct(block.shape, block.dtype)],
        [ANYWHERE],
        (),
        after,
        {0: 0},
    )
    return block


class Copies:
    def __init__(self, sem):
        self.sem, self.count, self.open = sem, 0, []

    def start(self, source, target):
        copy = pltpu.make_async_copy(source, target, self.sem.at[self.count])
        copy.start()
        self.count += 1
        self.open.append(copy)
        return copy

    def wait(self):
        for copy in self.open:
            copy.wait()
        self.open = []


def centred_of(values):
    centred = values - jnp.mean(values, axis=-1, keepdims=True)
    spread = jnp.mean(centred * centred, axis=-1, keepdims=True)
    scale = lax.rsqrt(spread + NORM_EPS)
    return centred * scale, scale


def norm_back(grad, hat, scale, gain):
    scaled = grad * gain
    return scale * (
        scaled
        - jnp.mean(scaled, axis=-1, keepdims=True)
        - hat * jnp.mean(scaled * hat, axis=-1, keepdims=True)
    )


def sentence_bounds(lengths_ref):
    len_row = lengths_ref[...].astype(F32)
    count = len_row.shape[1]
    len_col = to_column(len_row)
    start_col = over_lanes(iota((count, count), 1) < iota((count, count), 0), len_row)
    start_row = over_rows(iota((count, count), 0) < iota((count, count), 1), len_col)
    return (len_row, len_col, start_row, start_col)


def routing(lengths_ref, task_ref, routes_ref, table_ref, me):
    len_row, len_col, start_row, start_col = sentence_bounds(lengths_ref)
    count = len_row.shape[1]
    tasks = routes_ref.shape[1]
    hit = iota((tasks, count), 0) == task_ref[...]
    expert_rows = [
        over_rows(hit, to_column(routes_ref[r : r + 1, :].astype(F32))) for r in range(2)
    ]
    logit_rows = [over_rows(hit, to_column(table_ref[r : r + 1, :])) for r in range(2)]
    peak = jnp.maximum(logit_rows[0], logit_rows[1])
    raised = [jnp.exp(row - peak) for row in logit_rows]
    gate_rows = [row / (raised[0] + raised[1]) for row in raised]
    expert_cols = [to_column(row) for row in expert_rows]
    earlier = iota((count, count), 0) < iota((count, count), 1)
    add_rows, far_rows = [], []
    for row in expert_rows:
        same = (expert_cols[0] == row) | (expert_cols[1] == row)
        add_rows.append(over_rows(earlier & same, len_col) - start_row)
        far_rows.append((row.astype(jnp.int32) ^ me).astype(F32))
    return (len_row, len_col, start_row, start_col, far_rows, gate_rows, add_rows)


def fill_slots(tables, data, capacity, groups, weighted):
    len_row, len_col, start_row, start_col, far_rows, gate_rows, add_rows = tables
    tok_count, count = data.shape[0], len_row.shape[1]
    place = iota((count, tok_count), 1).astype(F32)
    inside = (place >= start_col) & (place < start_col + len_col)
    token_place = iota((1, tok_count), 1).astype(F32)
    far = [over_rows(inside, to_column(row)) for row in far_rows]
    position = [token_place + over_rows(inside, to_column(row)) for row in add_rows]
    slots = iota((capacity, tok_count), 0)
    slot_column = iota((capacity, count), 0).astype(F32)
    for k in range(groups):
        slot = jnp.where(far[0] == k, position[0], jnp.where(far[1] == k, position[1], -1.0))
        picked = dot(one_hot(slots == slot.astype(jnp.int32)), data)
        if weighted:
            first, second = far_rows[0] == k, far_rows[1] == k
            base = jnp.where(first, add_rows[0], add_rows[1]) + start_row
            gate = jnp.where(first, gate_rows[0], jnp.where(second, gate_rows[1], 0.0))
            picked = picked * over_lanes((slot_column >= base) & (slot_column < base + len_row), gate)
        yield k, picked


def dispatch_body(len_ref, task_ref, routes_ref, table_ref, data_ref, out_ref, stage, sem):
    groups, capacity, _ = out_ref.shape
    copies = Copies(sem)
    tables = routing(len_ref, task_ref, routes_ref, table_ref, 0)
    for k, picked in fill_slots(tables, data_ref[...], capacity, groups, True):
        stage[k] = picked.astype(BF)
        copies.start(stage.at[k], out_ref.at[k])
    copies.wait()


def dispatch_grads(capacity, groups, lengths, seg_task, routes, gate_table, cotangent, after):
    slots = (groups, capacity, cotangent.shape[1])
    (out,), mark = run(
        "dispatch_grads",
        dispatch_body,
        (lengths, seg_task, routes, gate_table, cotangent),
        [WHOLE] * 5,
        [jax.ShapeDtypeStruct(slots, BF)],
        [ANYWHERE],
        [pltpu.VMEM(slots, BF), pltpu.SemaphoreType.DMA((groups,))],
        after,
    )
    return out, mark


def split_heads(block):
    head = iota(block.shape, 1) // HD
    zero = jnp.zeros_like(block)
    return jnp.concatenate([jnp.where(head == h, block, zero) for h in range(JOINT)], axis=0)


def join_heads(stacked):
    rows = stacked.shape[0] // JOINT
    head = iota((rows, stacked.shape[1]), 1) // HD
    out = stacked[:rows]
    for h in range(1, JOINT):
        out = jnp.where(head == h, stacked[h * rows : (h + 1) * rows], out)
    return out


def windows(lengths_ref, tok_count, queries):
    len_row, len_col, start_row, start_col = sentence_bounds(lengths_ref)
    end_row, end_col = start_row + len_row, start_col + len_col
    count = len_row.shape[1]
    keys = queries + 2 * REACH
    for block in range(tok_count // queries):
        start = min(max(block * queries - REACH, 0), tok_count - keys)
        query_place = (iota((count, queries), 1) + block * queries).astype(F32)
        query_seg = jnp.sum((query_place >= end_col).astype(F32), axis=0, keepdims=True)
        key_place = (iota((keys, count), 0) + start).astype(F32)
        key_seg = jnp.sum((key_place >= end_row).astype(F32), axis=1, keepdims=True)
        same = key_seg == jnp.concatenate([query_seg] * JOINT, axis=1)
        rows = slice(block * queries, (block + 1) * queries)
        yield rows, slice(start, start + keys), same


def softmax_of(key_rows, stacked, same):
    scores = jnp.where(same, dot_nt(key_rows, stacked), MASK_FILL)
    raised = jnp.exp(scores - jnp.max(scores, axis=0, keepdims=True))
    return raised * (1.0 / jnp.sum(raised, axis=0, keepdims=True))


def forward_body(
    capacity,
    groups,
    me_ref,
    len_ref,
    task_ref,
    routes_ref,
    table_ref,
    tok_ref,
    wqkv_ref,
    bias_ref,
    wout_ref,
    obias_ref,
    gains_ref,
    shifts_ref,
    *refs,
):
    qkv_out, att_out, hid_out, one_out = refs[:4]
    slot_out = refs[4 : 4 + groups]
    qkv, att, hid, one, two, stage, sem = refs[4 + groups :]
    tok_count, width = tok_ref.shape
    copies = Copies(sem)
    for step in range(tok_count // ROWS):
        rows = slice(step * ROWS, (step + 1) * ROWS)
        hat, _ = centred_of(tok_ref[rows, :].astype(F32))
        normed = (hat * gains_ref[0:1, :] + shifts_ref[0:1, :]).astype(BF)
        one[rows, :] = normed
        wide = dot(normed, wqkv_ref[...])
        queries = (wide[:, :width] + bias_ref[0:1, :]).astype(BF)
        qkv[rows, :width] = queries * jnp.asarray(HD**-0.5, BF)
        qkv[rows, width : 2 * width] = wide[:, width : 2 * width].astype(BF)
        qkv[rows, 2 * width :] = (wide[:, 2 * width :] + bias_ref[1:2, :]).astype(BF)
    copies.start(one, one_out)
    copies.start(qkv, qkv_out)
    for rows, keys, same in windows(len_ref, tok_count, REACH):
        for first in range(0, width, LANES):
            lanes = slice(first, first + LANES)
            key_rows = qkv[keys, width + first : width + first + LANES]
            value_rows = qkv[keys, 2 * width + first : 2 * width + first + LANES]
            probs = softmax_of(key_rows, split_heads(qkv[rows, lanes]), same).astype(BF)
            att[rows, lanes] = join_heads(dot_tn(probs, value_rows)).astype(BF)
    copies.start(att, att_out)
    for step in range(tok_count // ROWS):
        rows = slice(step * ROWS, (step + 1) * ROWS)
        hidden = tok_ref[rows, :].astype(F32) + dot(att[rows, :], wout_ref[...]) + obias_ref[...]
        hid[rows, :] = hidden
        hat, _ = centred_of(hidden)
        two[rows, :] = (hat * gains_ref[1:2, :] + shifts_ref[1:2, :]).astype(BF)
    copies.start(hid, hid_out)
    tables = routing(len_ref, task_ref, routes_ref, table_ref, me_ref[0])
    for k, picked in fill_slots(tables, two[...], capacity, groups, False):
        stage[k] = picked.astype(BF)
        copies.start(stage.at[k], slot_out[k])
    copies.wait()


def forward(
    capacity,
    groups,
    me,
    lengths,
    seg_task,
    routes,
    gate_table,
    tokens,
    w_qkv,
    bias_qv,
    w_out,
    out_bias,
    gains,
    shifts,
    after,
):
    tok_count, width = tokens.shape
    whole = [
        ((tok_count, 3 * width), BF),
        ((tok_count, width), BF),
        ((tok_count, width), F32),
        ((tok_count, width), BF),
    ]
    (qkv, att, hid, one, *slots), mark = run(
        "forward",
        functools.partial(forward_body, capacity, groups),
        (
            me,
            lengths,
            seg_task,
            routes,
            gate_table,
            tokens,
            w_qkv,
            bias_qv,
            w_out,
            out_bias.reshape(1, width),
            gains,
            shifts,
        ),
        [SCALARS] + [WHOLE] * 11,
        [jax.ShapeDtypeStruct(*kind) for kind in whole]
        + [jax.ShapeDtypeStruct((capacity, width), BF)] * groups,
        [ANYWHERE] * (4 + groups),
        [pltpu.VMEM(*kind) for kind in whole]
        + [
            pltpu.VMEM((tok_count, width), BF),
            pltpu.VMEM((groups, capacity, width), BF),
            pltpu.SemaphoreType.DMA((4 + groups,)),
        ],
        after,
    )
    return qkv, att, hid, one, slots, mark


GELU_A = 0.7978845608028654
GELU_B = 0.044715


def gelu_both(values):
    square = values * values
    inner = values * (GELU_A + (GELU_A * GELU_B) * square)
    half = 0.5 * jnp.tanh(inner) + 0.5
    active = values * half
    slope = half + active * (1.0 - half) * (2.0 * GELU_A + (6.0 * GELU_A * GELU_B) * square)
    return active, slope


def pieces_of(total, size):
    return [slice(i, min(i + size, total)) for i in range(0, total, size)]


def expert_body(ids, planes, me_ref, *refs):
    refs = list(refs)
    take = lambda count: [refs.pop(0) for _ in range(count)]
    blocks = len(ids)
    x_in, (g_in,), parts = take(blocks), take(1), take(planes)
    dx_out = take(blocks)
    act_out, pre_out, xt_out, gt_out = take(4)
    xs, gs, w_in, w_down, act, pre, xt, gt, dx, sem = refs
    cap, width = x_in[0].shape
    hid = parts[0].shape[1]
    rows = blocks * cap
    me = me_ref[0]
    copies = Copies(sem)
    for i, k in enumerate(ids):
        copies.start(x_in[i], xs.at[pl.ds(i * cap, cap)])
        copies.start(g_in.at[me ^ k], gs.at[pl.ds(i * cap, cap)])
    rows_there, copies.open = copies.open, []
    parts_there = []
    for c in range(planes):
        lanes = pl.ds(c * hid, hid)
        copies.start(parts[c].at[pl.ds(0, width)], w_in.at[:, lanes])
        copies.start(parts[c].at[pl.ds(width, width)], w_down.at[:, lanes])
        parts_there.append(copies.open)
        copies.open = []
    for copy in rows_there:
        copy.wait()
    for c in range(planes):
        for copy in parts_there[c]:
            copy.wait()
        lanes = slice(c * hid, (c + 1) * hid)
        for spot in pieces_of(rows, 3 * cap):
            active, slope = gelu_both(dot(xs[spot, :], w_in[:, lanes]))
            act[spot, lanes] = active.astype(BF)
            pre[spot, lanes] = (dot(gs[spot, :], w_down[:, lanes]) * slope).astype(BF)
        copies.start(act.at[:, pl.ds(c * hid, hid)], act_out.at[:, pl.ds(c * hid, hid)])
        copies.start(pre.at[:, pl.ds(c * hid, hid)], pre_out.at[:, pl.ds(c * hid, hid)])
        if c == 0:
            xt[...] = xs[...].T
            copies.start(xt, xt_out)
            gt[...] = gs[...].T
            copies.start(gt, gt_out)
    for i, spot in enumerate(pieces_of(rows, 3 * cap)):
        dx[spot, :] = dot_nt(pre[spot, :], w_in[...]).astype(BF)
        for j in range(spot.start // cap, spot.stop // cap):
            copies.start(dx.at[pl.ds(j * cap, cap)], dx_out[j])
    copies.wait()


def expert_rows(ids, me, x_blocks, g_rows, parts, after):
    blocks, planes = len(ids), len(parts)
    cap, width = x_blocks[0].shape
    hid = parts[0].shape[1]
    rows = blocks * cap
    units, turned = (rows, planes * hid), (width, rows)
    result, mark = run(
        "expert_rows",
        functools.partial(expert_body, ids, planes),
        (me, *x_blocks, g_rows, *parts),
        [SCALARS] + [ANYWHERE] * (blocks + 1 + planes),
        [jax.ShapeDtypeStruct((cap, width), BF)] * blocks
        + [jax.ShapeDtypeStruct(units, BF)] * 2
        + [jax.ShapeDtypeStruct(turned, BF)] * 2,
        [ANYWHERE] * (blocks + 4),
        [
            pltpu.VMEM((rows, width), BF),
            pltpu.VMEM((rows, width), BF),
            pltpu.VMEM((width, planes * hid), BF),
            pltpu.VMEM((width, planes * hid), BF),
            pltpu.VMEM(units, BF),
            pltpu.VMEM(units, BF),
            pltpu.VMEM(turned, BF),
            pltpu.VMEM(turned, BF),
            pltpu.VMEM((rows, width), BF),
            pltpu.SemaphoreType.DMA((3 * blocks + 4 * planes + 2,)),
        ],
        after,
    )
    return result[:blocks], result[blocks:], mark


def output_body(calls, planes, me_ref, *refs):
    act_in, parts = refs[: len(calls)], refs[len(calls) : len(calls) + planes]
    out_ref, act, w_down, stage, sem = refs[len(calls) + planes :]
    _, capacity, width = out_ref.shape
    hid = parts[0].shape[1]
    copies = Copies(sem)
    for c, part in enumerate(parts):
        copies.start(part.at[pl.ds(width, width)], w_down.at[:, pl.ds(c * hid, hid)])
    there, copies.open = copies.open, []
    there_rows, spot = [], 0
    for ids, units in zip(calls, act_in):
        size = len(ids) * capacity
        there_rows.append(copies.start(units, act.at[pl.ds(spot, size)]))
        spot += size
    copies.open = []
    for copy in there:
        copy.wait()
    spot = 0
    for ids, copy in zip(calls, there_rows):
        copy.wait()
        size = len(ids) * capacity
        stage[spot : spot + size, :] = dot_nt(act[spot : spot + size, :], w_down[...]).astype(BF)
        for k in ids:
            copies.start(stage.at[pl.ds(spot, capacity)], out_ref.at[me_ref[0] ^ k])
            spot += capacity
    copies.wait()


def expert_outputs(calls, groups, capacity, me, act, parts, after):
    planes = len(parts)
    width, hid = parts[0].shape[0] // 2, parts[0].shape[1]
    (out,), mark = run(
        "expert_outputs",
        functools.partial(output_body, calls, planes),
        (me, *act, *parts),
        [SCALARS] + [ANYWHERE] * (len(act) + planes),
        [jax.ShapeDtypeStruct((groups, capacity, width), BF)],
        [ANYWHERE],
        [
            pltpu.VMEM((groups * capacity, planes * hid), BF),
            pltpu.VMEM((width, planes * hid), BF),
            pltpu.VMEM((groups * capacity, width), BF),
            pltpu.SemaphoreType.DMA((planes + len(calls) + groups,)),
        ],
        after,
    )
    return out, mark


def weight_body(which, calls, *refs):
    act_in, pre_in, xt_in, gt_in = (refs[i * calls : (i + 1) * calls] for i in range(4))
    out_refs = refs[4 * calls : 4 * calls + len(which)]
    act, pre, xt, gt, stage, sem = refs[4 * calls + len(which) :]
    width, hid = xt.shape[0], act.shape[2]
    spots, total = [], 0
    for turned in xt_in:
        spots.append(pl.ds(total, turned.shape[1]))
        total += turned.shape[1]
    copies = Copies(sem)
    there, leaving = {}, []

    def fetch(n, kind):
        if n >= len(which):
            return
        lanes = pl.ds(which[n] * hid, hid)
        copies.open = []
        for i, spot in enumerate(spots):
            if n == 0:
                copies.start((xt_in, gt_in)[kind][i], (xt, gt)[kind].at[:, spot])
            source, target = ((pre_in, pre), (act_in, act))[kind]
            copies.start(source[i].at[:, lanes], target.at[n % 2, spot])
        there[n, kind], copies.open = copies.open, []

    fetch(0, 0)
    fetch(0, 1)
    for n in range(len(which)):
        for kind, (turned, units) in enumerate(((xt, pre), (gt, act))):
            for copy in there[n, kind]:
                copy.wait()
            fetch(n + 1, kind)
            spot = pl.ds(kind * width, width)
            stage[n, spot, :] = dot(turned[...], units[n % 2]).astype(stage.dtype)
            leaving.append(copies.start(stage.at[n, spot], out_refs[n].at[spot]))
    for copy in leaving:
        copy.wait()


def weight_grads(which, planes, dtype, act, pre, xt, gt, after):
    calls = len(act)
    width, rows = xt[0].shape[0], sum(turned.shape[1] for turned in xt)
    hid = act[0].shape[1] // planes
    return run(
        "weight_grads",
        functools.partial(weight_body, which, calls),
        (*act, *pre, *xt, *gt),
        [ANYWHERE] * (4 * calls),
        [jax.ShapeDtypeStruct((2 * width, hid), dtype)] * len(which),
        [ANYWHERE] * len(which),
        [
            pltpu.VMEM((2, rows, hid), BF),
            pltpu.VMEM((2, rows, hid), BF),
            pltpu.VMEM((width, rows), BF),
            pltpu.VMEM((width, rows), BF),
            pltpu.VMEM((len(which), 2 * width, hid), dtype),
            pltpu.SemaphoreType.DMA((2 * calls * (len(which) + 1) + 2 * len(which),)),
        ],
        after,
    )


def token_slots(tables, tok_count, capacity):
    len_row, _, start_row, _, far_rows, gate_rows, add_rows = tables
    count = len_row.shape[1]
    place = iota((tok_count, count), 0).astype(F32)
    inside = (place >= start_row) & (place < start_row + len_row)
    columns = []
    for far, add in zip(far_rows, add_rows):
        kept = inside & (place + add < capacity)
        columns.append(over_lanes(kept, place + (add + far * capacity + 1.0)) - 1.0)
    gates = [over_lanes(inside, row) for row in gate_rows]
    return columns, gates, inside


def backward_body(
    groups,
    capacity,
    me_ref,
    len_ref,
    task_ref,
    routes_ref,
    table_ref,
    cot_ref,
    wout_ref,
    gains_ref,
    hid_in,
    att_in,
    qkv_in,
    one_in,
    *refs,
):
    back_in = refs[:groups]
    keep_ref, send_ref, grad_out, dqkv_out = refs[groups : groups + 4]
    back, side, hid, att, qkv, one, grad_all, low, gatt, dqkv, total, sem = refs[groups + 4 :]
    copies = Copies(sem)
    for i, ref in enumerate(back_in):
        copies.start(ref, back.at[pl.ds(i * capacity, capacity)])
    copies.start(hid_in, hid)
    first, copies.open = copies.open, []
    att_there = copies.start(att_in, att)
    qkv_there = copies.start(qkv_in, qkv)
    one_there = copies.start(one_in, one)
    copies.open = []
    tok_count, width = cot_ref.shape
    me = me_ref[0]
    tables = routing(len_ref, task_ref, routes_ref, table_ref, me)
    columns, _, _ = token_slots(tables, tok_count, capacity)
    for i, column in enumerate(columns):
        side[:, i : i + 1] = column.astype(jnp.int32)
    for copy in first:
        copy.wait()
    sums = [jnp.zeros((1, width), F32)] * 3
    for step in range(tok_count // ROWS):
        rows = slice(step * ROWS, (step + 1) * ROWS)
        slots = iota((ROWS, groups * capacity), 1)
        hit = (slots == side[rows, 0:1]) | (slots == side[rows, 1:2])
        grad_two = dot(one_hot(hit), back[...])
        hat, scale = centred_of(hid[rows, :])
        grad = cot_ref[rows, :].astype(F32) + norm_back(grad_two, hat, scale, gains_ref[1:2, :])
        grad_all[rows, :] = grad
        for i, part in enumerate((grad_two * hat, grad_two, grad)):
            sums[i] = sums[i] + jnp.sum(part, axis=0, keepdims=True)
        low[rows, :] = grad.astype(BF)
        gatt[rows, :] = dot_nt(low[rows, :], wout_ref[...]).astype(BF)
    copies.start(grad_all, grad_out)
    att_there.wait()
    total[:, 3 * width : 4 * width] = dot_tn(att[...], low[...])

    qkv_there.wait()
    open_sums = [({}, {}) for _ in range(width // LANES)]
    bias_sums = {}
    spans = list(windows(len_ref, tok_count, 2 * REACH))
    for index, (rows, keys, same) in enumerate(spans):
        next_key = spans[index + 1][1].start if index + 1 < len(spans) else tok_count
        for group, lane in enumerate(range(0, width, LANES)):
            lanes = slice(lane, lane + LANES)
            key_lanes = slice(width + lane, width + lane + LANES)
            value_lanes = slice(2 * width + lane, 2 * width + lane + LANES)
            stacked, grads = split_heads(qkv[rows, lanes]), split_heads(gatt[rows, lanes])
            key_rows, value_rows = qkv[keys, key_lanes], qkv[keys, value_lanes]
            probs = softmax_of(key_rows, stacked, same)
            grad_probs = dot_nt(value_rows, grads)
            inner = jnp.sum(probs * grad_probs, axis=0, keepdims=True)
            grad_scores = (probs * (grad_probs - inner)).astype(BF)
            grad_values = dot(probs.astype(BF), grads)
            grad_keys = dot(grad_scores, stacked)
            grad_queries = join_heads(dot_tn(grad_scores, key_rows)) * HD**-0.5
            dqkv[rows, lanes] = grad_queries.astype(BF)
            for held, fresh, target in zip(
                open_sums[group], (grad_keys, grad_values), (key_lanes, value_lanes)
            ):
                for i in range(0, fresh.shape[0], REACH):
                    place = keys.start + i
                    part = fresh[i : i + REACH]
                    held[place] = held[place] + part if place in held else part
                for place in [place for place in held if place < next_key]:
                    dqkv[place : place + REACH, target] = held.pop(place).astype(BF)
    copies.start(dqkv, dqkv_out)
    ones = jnp.ones((8, tok_count), BF)
    bias = [dot(ones, dqkv[:, :width])[0:1], dot(ones, dqkv[:, 2 * width :])[0:1]]
    short = jnp.concatenate(sums + bias + [jnp.zeros((SMALL - 5, width), F32)], axis=0)
    total[:, 4 * width :] = short.T
    one_there.wait()
    total[:, : 3 * width] = dot_tn(one[...], dqkv[...])
    half, rows, _ = keep_ref.shape
    for j in range(half):
        for bit, ref in enumerate((keep_ref, send_ref)):
            owner = me ^ (2 * j + bit)
            ref[j] = total[pl.ds(pl.multiple_of(owner * rows, rows), rows), :].astype(BF)
    copies.wait()


def backward(
    capacity,
    me,
    lengths,
    seg_task,
    routes,
    gate_table,
    cotangent,
    w_out,
    gains,
    hidden,
    attended,
    qkv,
    one,
    back,
    after,
):
    tok_count, width = cotangent.shape
    groups = len(back)
    columns = 4 * width + SMALL
    pieces = jax.ShapeDtypeStruct((groups // 2, width // groups, columns), BF)
    (keep, send, grad, dqkv), mark = run(
        "backward",
        functools.partial(backward_body, groups, capacity),
        (
            me,
            lengths,
            seg_task,
            routes,
            gate_table,
            cotangent,
            w_out,
            gains,
            hidden,
            attended,
            qkv,
            one,
            *back,
        ),
        [SCALARS] + [WHOLE] * 7 + [ANYWHERE] * (4 + groups),
        [
            pieces,
            pieces,
            jax.ShapeDtypeStruct((tok_count, width), F32),
            jax.ShapeDtypeStruct((tok_count, 3 * width), BF),
        ],
        [WHOLE, WHOLE, ANYWHERE, ANYWHERE],
        [
            pltpu.VMEM((groups * capacity, width), BF),
            pltpu.VMEM((tok_count, 2), jnp.int32),
            pltpu.VMEM((tok_count, width), F32),
            pltpu.VMEM((tok_count, width), BF),
            pltpu.VMEM((tok_count, 3 * width), BF),
            pltpu.VMEM((tok_count, width), BF),
            pltpu.VMEM((tok_count, width), F32),
            pltpu.VMEM((tok_count, width), BF),
            pltpu.VMEM((tok_count, width), BF),
            pltpu.VMEM((tok_count, 3 * width), BF),
            pltpu.VMEM((width, columns), F32),
            pltpu.SemaphoreType.DMA((groups + 6,)),
        ],
        after,
    )
    return keep, send, grad, dqkv, mark


def last_body(dqkv_ref, wqkv_ref, tok_ref, grad_ref, gains_ref, out_ref, small_ref):
    tok_count, width = tok_ref.shape
    sums = [jnp.zeros((1, width), F32)] * 2
    for step in range(tok_count // ROWS):
        rows = slice(step * ROWS, (step + 1) * ROWS)
        grad_one = dot_nt(dqkv_ref[rows, :], wqkv_ref[...])
        hat, scale = centred_of(tok_ref[rows, :].astype(F32))
        back = norm_back(grad_one, hat, scale, gains_ref[0:1, :])
        out_ref[rows, :] = (grad_ref[rows, :] + back).astype(BF)
        for i, part in enumerate((grad_one * hat, grad_one)):
            sums[i] = sums[i] + jnp.sum(part, axis=0, keepdims=True)
    small_ref[...] = jnp.concatenate(sums, axis=0)


def last_back(dqkv, w_qkv, tokens, grad_hidden, gains, after):
    tok_count, width = tokens.shape
    (out, small), mark = run(
        "last_back",
        last_body,
        (dqkv, w_qkv, tokens, grad_hidden, gains),
        [WHOLE] * 5,
        [jax.ShapeDtypeStruct((tok_count, width), BF), jax.ShapeDtypeStruct((2, width), F32)],
        [WHOLE] * 2,
        (),
        after,
    )
    return out, small, mark


def finish_body(
    len_ref,
    task_ref,
    routes_ref,
    table_ref,
    cot_ref,
    hid_ref,
    back_in,
    small_ref,
    out_ref,
    short_ref,
    back,
    side_ref,
    sem,
):
    groups, capacity, _ = back_in.shape
    copies = Copies(sem)
    for i in range(groups):
        copies.start(back_in.at[i], back.at[pl.ds(i * capacity, capacity)])
    tok_count, width = cot_ref.shape
    tables = routing(len_ref, task_ref, routes_ref, table_ref, 0)
    columns, gates, inside = token_slots(tables, tok_count, capacity)
    task_col = over_lanes(inside, task_ref[...].astype(F32))
    for i, column in enumerate(columns + gates + [task_col]):
        side_ref[:, i : i + 1] = column
    copies.wait()
    gate_sums = [jnp.zeros((1, 128), F32)] * 2
    for step in range(tok_count // ROWS):
        rows = slice(step * ROWS, (step + 1) * ROWS)
        slots = iota((ROWS, groups * capacity), 1)
        side = side_ref[rows, :]
        cot = cot_ref[rows, :].astype(F32)
        mixed = hid_ref[rows, :]
        inner = jnp.zeros((ROWS, 1), F32)
        parts = []
        for r in range(2):
            hit = slots == side[:, r : r + 1].astype(jnp.int32)
            picked = dot(one_hot(hit), back[...])
            gate = side[:, 2 + r : 3 + r]
            mixed = mixed + gate * picked
            grad = jnp.sum(cot * picked, axis=1, keepdims=True)
            parts.append((gate, grad))
            inner = inner + gate * grad
        out_ref[rows, :] = mixed.astype(BF)
        task = iota((ROWS, 128), 1) == side[:, 4:5].astype(jnp.int32)
        for r, (gate, grad) in enumerate(parts):
            gate_sums[r] = gate_sums[r] + over_rows(task, gate * (grad - inner))
    wide = width // 128
    for i in range(2):
        for j in range(wide):
            short_ref[i * wide + j : i * wide + j + 1, :] = small_ref[
                i : i + 1, j * 128 : (j + 1) * 128
            ]
    short_ref[2 * wide : 2 * wide + 2, :] = jnp.concatenate(gate_sums, axis=0)


def finish(lengths, seg_task, routes, gate_table, cotangent, hidden, back, small, after):
    tok_count, width = cotangent.shape
    groups, capacity, _ = back.shape
    (out, gate), mark = run(
        "finish",
        finish_body,
        (lengths, seg_task, routes, gate_table, cotangent, hidden, back, small),
        [WHOLE] * 6 + [ANYWHERE, WHOLE],
        [
            jax.ShapeDtypeStruct((tok_count, width), BF),
            jax.ShapeDtypeStruct((2 * width // 128 + 2, 128), F32),
        ],
        [WHOLE] * 2,
        [
            pltpu.VMEM((groups * capacity, width), BF),
            pltpu.VMEM((tok_count, 8), F32),
            pltpu.SemaphoreType.DMA((groups,)),
        ],
        after,
    )
    return out, gate, mark


def swap(block, axis, distance):
    count = lax.axis_size(axis)
    return lax.ppermute(block, axis, [(s, s ^ distance) for s in range(count)])


def turn(block, axis, distance):
    count = lax.axis_size(axis)
    return lax.ppermute(block, axis, [(s, (s + distance) % count) for s in range(count)])


def powers(count):
    return [1 << i for i in range(count.bit_length() - 1)]


def add_pairs(keep, came, after):
    count, rows, columns = keep.shape

    def body(keep_ref, came_ref, *out_refs):
        for j, out_ref in enumerate(out_refs):
            out_ref[...] = (keep_ref[j].astype(F32) + came_ref[j].astype(F32)).astype(BF)

    return run(
        "add_pairs",
        body,
        (keep, came),
        [WHOLE] * 2,
        [jax.ShapeDtypeStruct((rows, columns), BF)] * count,
        [WHOLE] * count,
        (),
        after,
    )


def add_all(blocks, after):
    def body(*refs):
        total = refs[0][...].astype(F32)
        for ref in refs[1:-1]:
            total = total + ref[...].astype(F32)
        refs[-1][...] = total.astype(BF)

    (out,), mark = run(
        "add_all",
        body,
        blocks,
        [WHOLE] * len(blocks),
        [jax.ShapeDtypeStruct(blocks[0].shape, BF)],
        [WHOLE],
        (),
        after,
    )
    return out, mark


def add_part(came, own, after):
    def body(came_ref, own_ref, out_ref):
        out_ref[...] = (came_ref[...].astype(F32) + own_ref[...].astype(F32)).astype(BF)

    size = came.shape
    (out,), mark = run(
        "add_part",
        body,
        (came, own),
        [WHOLE] * 2,
        [jax.ShapeDtypeStruct(size, BF)],
        [WHOLE],
        (),
        after,
    )
    return out, mark


def last_part(came, own, after):
    width, hid = own.shape[0] // 2, own.shape[1]

    def body(*refs):
        *came_refs, own_ref, in_ref, down_ref = refs

        def total(spot):
            sums = own_ref[spot, :]
            for ref in came_refs:
                sums = sums + ref[spot, :].astype(F32)
            return sums

        in_ref[0] = total(slice(0, width))
        down_ref[0] = total(slice(width, 2 * width)).T

    return run(
        "last_part",
        body,
        (*came, own),
        [WHOLE] * (len(came) + 1),
        [jax.ShapeDtypeStruct((1, width, hid), F32), jax.ShapeDtypeStruct((1, hid, width), F32)],
        [WHOLE] * 2,
        (),
        after,
    )


def assemble(me, pieces, short, tasks, after):
    rows, columns = pieces[0].shape
    count = len(pieces)
    width = count * rows
    wide = width // 128

    def body(me_ref, short_ref, *refs):
        qkv_ref, bias_ref, out_ref, obias_ref, gains_ref, shifts_ref, gate_ref, small = refs[count:]
        for k, piece in enumerate(refs[:count]):
            owner = me_ref[0] ^ k
            spot = pl.ds(pl.multiple_of(owner * rows, rows), rows)
            qkv_ref[spot, :] = piece[:, : 3 * width].astype(F32)
            out_ref[spot, :] = piece[:, 3 * width : 4 * width].astype(F32)
            small[spot, :] = piece[:, 4 * width :].astype(F32)
        turned = small[...].T
        for i, ref in enumerate((gains_ref, shifts_ref)):
            parts = [short_ref[j : j + 1, :] for j in range(i * wide, (i + 1) * wide)]
            ref[0:1, :] = jnp.concatenate(parts, axis=1)
            ref[1:2, :] = turned[i : i + 1]
        obias_ref[...] = turned[2:3]
        bias_ref[...] = turned[3:5]
        gate_ref[...] = short_ref[2 * wide : 2 * wide + 2, :tasks]

    pair = jax.ShapeDtypeStruct((2, width), F32)
    return run(
        "assemble",
        body,
        (me, short, *pieces),
        [SCALARS] + [WHOLE] * (count + 1),
        [
            jax.ShapeDtypeStruct((width, 3 * width), F32),
            pair,
            jax.ShapeDtypeStruct((width, width), F32),
            jax.ShapeDtypeStruct((1, width), F32),
            pair,
            pair,
            jax.ShapeDtypeStruct((2, tasks), F32),
        ],
        [WHOLE] * 7,
        [pltpu.VMEM((width, columns - 4 * width), F32)],
        after,
    )


def add_small(block, axis, distance, mark, after=()):
    def body(block_ref, sent_ref, out_ref):
        out_ref[...] = block_ref[...] + sent_ref[...]

    (block,), mark = run(
        "add_small",
        body,
        (block, swap(block, axis, distance)),
        [WHOLE] * 2,
        [jax.ShapeDtypeStruct(block.shape, F32)],
        [WHOLE],
        (),
        (mark, *after),
    )
    return block, mark


def working_order(groups, capacity):
    unit = 128 // math.gcd(128, capacity)
    near = max(2, unit)
    order = sorted(range(near, groups), key=lambda k: (-k.bit_count(), k))
    half = (groups - near) // 2 // unit * unit
    return [list(range(near))[::-1] + order[:half], order[half:]]


def shards(
    tokens,
    cotangent,
    w_qkv,
    bias_qv,
    w_out,
    out_bias,
    norm_gains,
    norm_shifts,
    gate_table,
    w_in,
    w_down,
    lengths,
    seg_task,
    routes,
):
    tok_count, width = tokens.shape
    groups = lax.axis_size("expert")
    planes = lax.axis_size("hidden")
    top_count = routes.shape[1]
    capacity = 3 * top_count * tok_count // (2 * groups * w_in.shape[0])
    me = lax.axis_index("expert").astype(jnp.int32).reshape(1)
    route_args = (lengths, seg_task, routes.T, gate_table.T)

    own, mark = join_weights(w_in, w_down)
    above = [own]
    above.append(turn(above[0], "hidden", 1))
    below = above[:1]
    for _ in range((planes - 1) // 2):
        below.append(turn(below[-1], "hidden", -1))

    grad_slots, mark = dispatch_grads(capacity, groups, *route_args, cotangent, (mark,))
    grad_rows = lax.all_to_all(grad_slots, "expert", split_axis=0, concat_axis=0, tiled=True)

    qkv, attended, hidden, one, slots, mark = forward(
        capacity,
        groups,
        me,
        *route_args,
        tokens,
        w_qkv,
        bias_qv,
        w_out,
        out_bias,
        norm_gains,
        norm_shifts,
        (mark,),
    )

    calls = working_order(groups, capacity)
    rows, dx_back, kept = {0: slots[0]}, {}, []
    for ids in calls:
        for k in ids:
            if k:
                rows[k] = swap(slots[k], "expert", k)
    above[1] = hold(above[1], (mark, *below[1:2], rows[max(rows, key=int.bit_count)]))
    for _ in range(planes // 2 - 1):
        above.append(turn(above[-1], "hidden", 1))
    parts = above + below[:0:-1]

    for ids in calls:
        dxs, rest, mark = expert_rows(ids, me, [rows[k] for k in ids], grad_rows, parts, (mark,))
        kept.append(rest)
        for k, dx in zip(ids, dxs):
            dx_back[k] = swap(dx, "expert", k) if k else dx
    kept = [list(part) for part in zip(*kept)]

    middle = planes // 2
    rising, falling = list(range(middle, planes)), list(range(middle - 1, 0, -1))
    which = sorted(rising + falling, key=lambda c: abs(2 * c - planes))
    fresh, mark = weight_grads(which, planes, BF, *kept, (mark,))
    partial = dict(zip(which, fresh))
    risen = turn(partial[rising[0]], "hidden", 1)
    fallen = [turn(partial[falling[0]], "hidden", -1)] if falling else []
    out_rows, mark = expert_outputs(
        calls, groups, capacity, me, kept[0], parts, (mark,)
    )
    out_back = lax.all_to_all(out_rows, "expert", split_axis=0, concat_axis=0, tiled=True)

    keep, send, grad_hidden, dqkv, mark = backward(
        capacity,
        me,
        *route_args,
        cotangent,
        w_out,
        norm_gains,
        hidden,
        attended,
        qkv,
        one,
        [dx_back[k] for k in range(groups)],
        (mark,),
    )
    sent = swap(send, "expert", 1)
    for c in rising[1:]:
        part, mark = add_part(risen, partial[c], (mark,))
        risen = turn(part, "hidden", 1)
    for c in falling[1:]:
        part, mark = add_part(fallen[0], partial[c], (mark,))
        fallen = [turn(part, "hidden", -1)]
    mine, mark = add_pairs(keep, sent, (mark,))
    sent = [swap(mine[j], "expert", 2 * j) for j in range(1, groups // 2)]
    (whole,), mark = weight_grads(
        [0], planes, F32, *kept, (mark,)
    )
    input_grad, small_one, mark = last_back(dqkv, w_qkv, tokens, grad_hidden, norm_gains, (mark, *fallen)
    )
    total, mark = add_all([mine[0], *sent], (mark,))
    hops = powers(planes)
    for step, distance in enumerate(hops):
        sent = swap(total, "hidden", distance)
        if step == 0:
            layer_out, short, mark = finish(
                *route_args, cotangent, hidden, out_back, small_one, (mark,)
            )
        if step == len(hops) - 1:
            for near in powers(groups):
                short, mark = add_small(short, "expert", near, mark)
        total, mark = add_all([total, sent], (mark,))
    even = [total] + [swap(total, "expert", 2 * j) for j in range(1, groups // 2)]
    for distance in hops:
        short, mark = add_small(short, "hidden", distance, mark)
    (grad_w_in, grad_w_down), mark = last_part([risen, *fallen], whole, (mark,))
    odd = [swap(piece, "expert", 1) for piece in even]
    results, mark = assemble(
        me, [piece for pair in zip(even, odd) for piece in pair], short, gate_table.shape[0], (mark,)
    )
    grad_qkv, grad_bias_qv, grad_w_out, grad_out_bias, grad_gains, grad_shifts, grad_gate = results
    return (
        layer_out,
        input_grad,
        grad_qkv,
        grad_bias_qv,
        grad_w_out,
        grad_out_bias[0],
        grad_gains,
        grad_shifts,
        grad_gate.T,
        grad_w_in,
        grad_w_down,
    )


def solution(mesh):
    split = P(("expert", "hidden"), None)
    return jax.shard_map(
        shards,
        mesh=mesh,
        in_specs=(
            split,
            split,
            P(),
            P(),
            P(),
            P(),
            P(),
            P(),
            P(),
            P("expert", None, "hidden"),
            P("expert", "hidden", None),
            split,
            split,
            P(),
        ),
        out_specs=(
            split,
            split,
            P(),
            P(),
            P(),
            P(),
            P(),
            P(),
            P(),
            P("expert", None, "hidden"),
            P("expert", "hidden", None),
        ),
        check_vma=False,
    )
```

```python
import functools
import math

import jax
import jax.numpy as jnp
from jax import lax
from jax.experimental import pallas as pl
from jax.experimental.pallas import tpu as pltpu
from jax.sharding import PartitionSpec as P

HEADS = 8
HD = 64
NORM_EPS = 1e-05
MASK_FILL = -1000000000.0

BF = jnp.bfloat16
F32 = jnp.float32
MIB = 1 << 20

ROWS = 256
REACH = 64
JOINT = 4
LANES = JOINT * HD
SMALL = 128


def iota(shape, dim):
    return lax.broadcasted_iota(jnp.int32, shape, dim)


def dot(left, right):
    return jnp.dot(left, right, preferred_element_type=F32)


def dot_nt(left, right):
    return lax.dot_general(left, right, (((1,), (1,)), ((), ())), preferred_element_type=F32)


def dot_tn(left, right):
    return lax.dot_general(left, right, (((0,), (0,)), ((), ())), preferred_element_type=F32)


def over_lanes(mask, values):
    return jnp.sum(jnp.where(mask, values, 0.0), axis=1, keepdims=True)


def over_rows(mask, values):
    return jnp.sum(jnp.where(mask, values, 0.0), axis=0, keepdims=True)


def to_column(row):
    count = row.shape[1]
    return over_lanes(iota((count, count), 0) == iota((count, count), 1), row)


def one_hot(mask):
    return mask.astype(F32).astype(BF)


WHOLE = pl.BlockSpec(memory_space=pltpu.VMEM)
SCALARS = pl.BlockSpec(memory_space=pltpu.SMEM)
ANYWHERE = pl.BlockSpec(memory_space=pl.ANY)


SCALE = 0.4
MICROS = {
    "dispatch_grads": 1,
    "forward": 1,
    "hold": 50,
    "expert_rows": 17,
    "weight_grads": 9,
    "expert_outputs": 11,
    "backward": 23,
    "last_back": 6,
    "finish": 12,
}
OTHER = 2


def run(name, body, args, in_specs, out_shape, out_specs, scratch=(), after=(), aliases=None):
    count, extra = len(args), len(after)

    def ordered(*refs):
        outs = refs[count + extra :]
        mark, rest = outs[len(out_shape)], outs[: len(out_shape)] + outs[len(out_shape) + 1 :]
        mark[...] = jnp.zeros_like(mark)
        body(*refs[:count], *rest)

    *results, mark = pl.pallas_call(
        ordered,
        out_shape=[*out_shape, jax.ShapeDtypeStruct((8, 128), F32)],
        in_specs=[*in_specs, *[ANYWHERE] * extra],
        out_specs=[*out_specs, WHOLE],
        scratch_shapes=list(scratch),
        input_output_aliases=aliases or {},
        compiler_params=pltpu.CompilerParams(vmem_limit_bytes=56 * MIB),
        cost_estimate=pl.CostEstimate(flops=int(1.15e9 * SCALE * MICROS.get(name, OTHER)), bytes_accessed=1 << 10, transcendentals=0),
        name=name,
    )(*args, *after)
    return results, mark


def join_weights(w_in, w_down):
    _, width, hid = w_in.shape

    def body(in_ref, down_ref, out_ref):
        out_ref[:width, :] = in_ref[0]
        out_ref[width:, :] = down_ref[0].T

    (out,), mark = run(
        "join_weights",
        body,
        (w_in, w_down),
        [WHOLE] * 2,
        [jax.ShapeDtypeStruct((2 * width, hid), BF)],
        [WHOLE],
    )
    return out, mark


def hold(block, after):
    (block,), _ = run(
        "hold",
        lambda *refs: None,
        (block,),
        [ANYWHERE],
        [jax.ShapeDtypeStruct(block.shape, block.dtype)],
        [ANYWHERE],
        (),
        after,
        {0: 0},
    )
    return block


class Copies:
    def __init__(self, sem):
        self.sem, self.count, self.open = sem, 0, []

    def start(self, source, target):
        copy = pltpu.make_async_copy(source, target, self.sem.at[self.count])
        copy.start()
        self.count += 1
        self.open.append(copy)
        return copy

    def wait(self):
        for copy in self.open:
            copy.wait()
        self.open = []


def centred_of(values):
    centred = values - jnp.mean(values, axis=-1, keepdims=True)
    spread = jnp.mean(centred * centred, axis=-1, keepdims=True)
    scale = lax.rsqrt(spread + NORM_EPS)
    return centred * scale, scale


def norm_back(grad, hat, scale, gain):
    scaled = grad * gain
    return scale * (
        scaled
        - jnp.mean(scaled, axis=-1, keepdims=True)
        - hat * jnp.mean(scaled * hat, axis=-1, keepdims=True)
    )


def sentence_bounds(lengths_ref):
    len_row = lengths_ref[...].astype(F32)
    count = len_row.shape[1]
    len_col = to_column(len_row)
    start_col = over_lanes(iota((count, count), 1) < iota((count, count), 0), len_row)
    start_row = over_rows(iota((count, count), 0) < iota((count, count), 1), len_col)
    return (len_row, len_col, start_row, start_col)


def routing(lengths_ref, task_ref, routes_ref, table_ref, me):
    len_row, len_col, start_row, start_col = sentence_bounds(lengths_ref)
    count = len_row.shape[1]
    tasks = routes_ref.shape[1]
    hit = iota((tasks, count), 0) == task_ref[...]
    expert_rows = [
        over_rows(hit, to_column(routes_ref[r : r + 1, :].astype(F32))) for r in range(2)
    ]
    logit_rows = [over_rows(hit, to_column(table_ref[r : r + 1, :])) for r in range(2)]
    peak = jnp.maximum(logit_rows[0], logit_rows[1])
    raised = [jnp.exp(row - peak) for row in logit_rows]
    gate_rows = [row / (raised[0] + raised[1]) for row in raised]
    expert_cols = [to_column(row) for row in expert_rows]
    earlier = iota((count, count), 0) < iota((count, count), 1)
    add_rows, far_rows = [], []
    for row in expert_rows:
        same = (expert_cols[0] == row) | (expert_cols[1] == row)
        add_rows.append(over_rows(earlier & same, len_col) - start_row)
        far_rows.append((row.astype(jnp.int32) ^ me).astype(F32))
    return (len_row, len_col, start_row, start_col, far_rows, gate_rows, add_rows)


def fill_slots(tables, data, capacity, groups, weighted):
    len_row, len_col, start_row, start_col, far_rows, gate_rows, add_rows = tables
    tok_count, count = data.shape[0], len_row.shape[1]
    place = iota((count, tok_count), 1).astype(F32)
    inside = (place >= start_col) & (place < start_col + len_col)
    token_place = iota((1, tok_count), 1).astype(F32)
    far = [over_rows(inside, to_column(row)) for row in far_rows]
    position = [token_place + over_rows(inside, to_column(row)) for row in add_rows]
    slots = iota((capacity, tok_count), 0)
    slot_column = iota((capacity, count), 0).astype(F32)
    for k in range(groups):
        slot = jnp.where(far[0] == k, position[0], jnp.where(far[1] == k, position[1], -1.0))
        picked = dot(one_hot(slots == slot.astype(jnp.int32)), data)
        if weighted:
            first, second = far_rows[0] == k, far_rows[1] == k
            base = jnp.where(first, add_rows[0], add_rows[1]) + start_row
            gate = jnp.where(first, gate_rows[0], jnp.where(second, gate_rows[1], 0.0))
            picked = picked * over_lanes((slot_column >= base) & (slot_column < base + len_row), gate)
        yield k, picked


def dispatch_body(len_ref, task_ref, routes_ref, table_ref, data_ref, out_ref, stage, sem):
    groups, capacity, _ = out_ref.shape
    copies = Copies(sem)
    tables = routing(len_ref, task_ref, routes_ref, table_ref, 0)
    for k, picked in fill_slots(tables, data_ref[...], capacity, groups, True):
        stage[k] = picked.astype(BF)
        copies.start(stage.at[k], out_ref.at[k])
    copies.wait()


def dispatch_grads(capacity, groups, lengths, seg_task, routes, gate_table, cotangent, after):
    slots = (groups, capacity, cotangent.shape[1])
    (out,), mark = run(
        "dispatch_grads",
        dispatch_body,
        (lengths, seg_task, routes, gate_table, cotangent),
        [WHOLE] * 5,
        [jax.ShapeDtypeStruct(slots, BF)],
        [ANYWHERE],
        [pltpu.VMEM(slots, BF), pltpu.SemaphoreType.DMA((groups,))],
        after,
    )
    return out, mark


def split_heads(block):
    head = iota(block.shape, 1) // HD
    zero = jnp.zeros_like(block)
    return jnp.concatenate([jnp.where(head == h, block, zero) for h in range(JOINT)], axis=0)


def join_heads(stacked):
    rows = stacked.shape[0] // JOINT
    head = iota((rows, stacked.shape[1]), 1) // HD
    out = stacked[:rows]
    for h in range(1, JOINT):
        out = jnp.where(head == h, stacked[h * rows : (h + 1) * rows], out)
    return out


def windows(lengths_ref, tok_count, queries):
    len_row, len_col, start_row, start_col = sentence_bounds(lengths_ref)
    end_row, end_col = start_row + len_row, start_col + len_col
    count = len_row.shape[1]
    keys = queries + 2 * REACH
    for block in range(tok_count // queries):
        start = min(max(block * queries - REACH, 0), tok_count - keys)
        query_place = (iota((count, queries), 1) + block * queries).astype(F32)
        query_seg = jnp.sum((query_place >= end_col).astype(F32), axis=0, keepdims=True)
        key_place = (iota((keys, count), 0) + start).astype(F32)
        key_seg = jnp.sum((key_place >= end_row).astype(F32), axis=1, keepdims=True)
        same = key_seg == jnp.concatenate([query_seg] * JOINT, axis=1)
        rows = slice(block * queries, (block + 1) * queries)
        yield rows, slice(start, start + keys), same


def softmax_of(key_rows, stacked, same):
    scores = jnp.where(same, dot_nt(key_rows, stacked), MASK_FILL)
    raised = jnp.exp(scores - jnp.max(scores, axis=0, keepdims=True))
    return raised * (1.0 / jnp.sum(raised, axis=0, keepdims=True))


def forward_body(
    capacity,
    groups,
    me_ref,
    len_ref,
    task_ref,
    routes_ref,
    table_ref,
    tok_ref,
    wqkv_ref,
    bias_ref,
    wout_ref,
    obias_ref,
    gains_ref,
    shifts_ref,
    *refs,
):
    qkv_out, att_out, hid_out, one_out = refs[:4]
    slot_out = refs[4 : 4 + groups]
    qkv, att, hid, one, two, stage, sem = refs[4 + groups :]
    tok_count, width = tok_ref.shape
    copies = Copies(sem)
    for step in range(tok_count // ROWS):
        rows = slice(step * ROWS, (step + 1) * ROWS)
        hat, _ = centred_of(tok_ref[rows, :].astype(F32))
        normed = (hat * gains_ref[0:1, :] + shifts_ref[0:1, :]).astype(BF)
        one[rows, :] = normed
        wide = dot(normed, wqkv_ref[...])
        queries = (wide[:, :width] + bias_ref[0:1, :]).astype(BF)
        qkv[rows, :width] = queries * jnp.asarray(HD**-0.5, BF)
        qkv[rows, width : 2 * width] = wide[:, width : 2 * width].astype(BF)
        qkv[rows, 2 * width :] = (wide[:, 2 * width :] + bias_ref[1:2, :]).astype(BF)
    copies.start(one, one_out)
    copies.start(qkv, qkv_out)
    for rows, keys, same in windows(len_ref, tok_count, REACH):
        for first in range(0, width, LANES):
            lanes = slice(first, first + LANES)
            key_rows = qkv[keys, width + first : width + first + LANES]
            value_rows = qkv[keys, 2 * width + first : 2 * width + first + LANES]
            probs = softmax_of(key_rows, split_heads(qkv[rows, lanes]), same).astype(BF)
            att[rows, lanes] = join_heads(dot_tn(probs, value_rows)).astype(BF)
    copies.start(att, att_out)
    for step in range(tok_count // ROWS):
        rows = slice(step * ROWS, (step + 1) * ROWS)
        hidden = tok_ref[rows, :].astype(F32) + dot(att[rows, :], wout_ref[...]) + obias_ref[...]
        hid[rows, :] = hidden
        hat, _ = centred_of(hidden)
        two[rows, :] = (hat * gains_ref[1:2, :] + shifts_ref[1:2, :]).astype(BF)
    copies.start(hid, hid_out)
    tables = routing(len_ref, task_ref, routes_ref, table_ref, me_ref[0])
    for k, picked in fill_slots(tables, two[...], capacity, groups, False):
        stage[k] = picked.astype(BF)
        copies.start(stage.at[k], slot_out[k])
    copies.wait()


def forward(
    capacity,
    groups,
    me,
    lengths,
    seg_task,
    routes,
    gate_table,
    tokens,
    w_qkv,
    bias_qv,
    w_out,
    out_bias,
    gains,
    shifts,
    after,
):
    tok_count, width = tokens.shape
    whole = [
        ((tok_count, 3 * width), BF),
        ((tok_count, width), BF),
        ((tok_count, width), F32),
        ((tok_count, width), BF),
    ]
    (qkv, att, hid, one, *slots), mark = run(
        "forward",
        functools.partial(forward_body, capacity, groups),
        (
            me,
            lengths,
            seg_task,
            routes,
            gate_table,
            tokens,
            w_qkv,
            bias_qv,
            w_out,
            out_bias.reshape(1, width),
            gains,
            shifts,
        ),
        [SCALARS] + [WHOLE] * 11,
        [jax.ShapeDtypeStruct(*kind) for kind in whole]
        + [jax.ShapeDtypeStruct((capacity, width), BF)] * groups,
        [ANYWHERE] * (4 + groups),
        [pltpu.VMEM(*kind) for kind in whole]
        + [
            pltpu.VMEM((tok_count, width), BF),
            pltpu.VMEM((groups, capacity, width), BF),
            pltpu.SemaphoreType.DMA((4 + groups,)),
        ],
        after,
    )
    return qkv, att, hid, one, slots, mark


GELU_A = 0.7978845608028654
GELU_B = 0.044715


def gelu_both(values):
    square = values * values
    inner = values * (GELU_A + (GELU_A * GELU_B) * square)
    half = 0.5 * jnp.tanh(inner) + 0.5
    active = values * half
    slope = half + active * (1.0 - half) * (2.0 * GELU_A + (6.0 * GELU_A * GELU_B) * square)
    return active, slope


def pieces_of(total, size):
    return [slice(i, min(i + size, total)) for i in range(0, total, size)]


def expert_body(ids, planes, me_ref, *refs):
    refs = list(refs)
    take = lambda count: [refs.pop(0) for _ in range(count)]
    blocks = len(ids)
    x_in, (g_in,), parts = take(blocks), take(1), take(planes)
    dx_out = take(blocks)
    act_out, pre_out, xt_out, gt_out = take(4)
    xs, gs, w_in, w_down, act, pre, xt, gt, dx, sem = refs
    cap, width = x_in[0].shape
    hid = parts[0].shape[1]
    rows = blocks * cap
    me = me_ref[0]
    copies = Copies(sem)
    for i, k in enumerate(ids):
        copies.start(x_in[i], xs.at[pl.ds(i * cap, cap)])
        copies.start(g_in.at[me ^ k], gs.at[pl.ds(i * cap, cap)])
    rows_there, copies.open = copies.open, []
    parts_there = []
    for c in range(planes):
        lanes = pl.ds(c * hid, hid)
        copies.start(parts[c].at[pl.ds(0, width)], w_in.at[:, lanes])
        copies.start(parts[c].at[pl.ds(width, width)], w_down.at[:, lanes])
        parts_there.append(copies.open)
        copies.open = []
    for copy in rows_there:
        copy.wait()
    for c in range(planes):
        for copy in parts_there[c]:
            copy.wait()
        lanes = slice(c * hid, (c + 1) * hid)
        for spot in pieces_of(rows, 3 * cap):
            active, slope = gelu_both(dot(xs[spot, :], w_in[:, lanes]))
            act[spot, lanes] = active.astype(BF)
            pre[spot, lanes] = (dot(gs[spot, :], w_down[:, lanes]) * slope).astype(BF)
        copies.start(act.at[:, pl.ds(c * hid, hid)], act_out.at[:, pl.ds(c * hid, hid)])
        copies.start(pre.at[:, pl.ds(c * hid, hid)], pre_out.at[:, pl.ds(c * hid, hid)])
        if c == 0:
            xt[...] = xs[...].T
            copies.start(xt, xt_out)
            gt[...] = gs[...].T
            copies.start(gt, gt_out)
    for i, spot in enumerate(pieces_of(rows, 3 * cap)):
        dx[spot, :] = dot_nt(pre[spot, :], w_in[...]).astype(BF)
        for j in range(spot.start // cap, spot.stop // cap):
            copies.start(dx.at[pl.ds(j * cap, cap)], dx_out[j])
    copies.wait()


def expert_rows(ids, me, x_blocks, g_rows, parts, after):
    blocks, planes = len(ids), len(parts)
    cap, width = x_blocks[0].shape
    hid = parts[0].shape[1]
    rows = blocks * cap
    units, turned = (rows, planes * hid), (width, rows)
    result, mark = run(
        "expert_rows",
        functools.partial(expert_body, ids, planes),
        (me, *x_blocks, g_rows, *parts),
        [SCALARS] + [ANYWHERE] * (blocks + 1 + planes),
        [jax.ShapeDtypeStruct((cap, width), BF)] * blocks
        + [jax.ShapeDtypeStruct(units, BF)] * 2
        + [jax.ShapeDtypeStruct(turned, BF)] * 2,
        [ANYWHERE] * (blocks + 4),
        [
            pltpu.VMEM((rows, width), BF),
            pltpu.VMEM((rows, width), BF),
            pltpu.VMEM((width, planes * hid), BF),
            pltpu.VMEM((width, planes * hid), BF),
            pltpu.VMEM(units, BF),
            pltpu.VMEM(units, BF),
            pltpu.VMEM(turned, BF),
            pltpu.VMEM(turned, BF),
            pltpu.VMEM((rows, width), BF),
            pltpu.SemaphoreType.DMA((3 * blocks + 4 * planes + 2,)),
        ],
        after,
    )
    return result[:blocks], result[blocks:], mark


def output_body(calls, planes, me_ref, *refs):
    act_in, parts = refs[: len(calls)], refs[len(calls) : len(calls) + planes]
    out_ref, act, w_down, stage, sem = refs[len(calls) + planes :]
    _, capacity, width = out_ref.shape
    hid = parts[0].shape[1]
    copies = Copies(sem)
    for c, part in enumerate(parts):
        copies.start(part.at[pl.ds(width, width)], w_down.at[:, pl.ds(c * hid, hid)])
    there, copies.open = copies.open, []
    there_rows, spot = [], 0
    for ids, units in zip(calls, act_in):
        size = len(ids) * capacity
        there_rows.append(copies.start(units, act.at[pl.ds(spot, size)]))
        spot += size
    copies.open = []
    for copy in there:
        copy.wait()
    spot = 0
    for ids, copy in zip(calls, there_rows):
        copy.wait()
        size = len(ids) * capacity
        stage[spot : spot + size, :] = dot_nt(act[spot : spot + size, :], w_down[...]).astype(BF)
        for k in ids:
            copies.start(stage.at[pl.ds(spot, capacity)], out_ref.at[me_ref[0] ^ k])
            spot += capacity
    copies.wait()


def expert_outputs(calls, groups, capacity, me, act, parts, after):
    planes = len(parts)
    width, hid = parts[0].shape[0] // 2, parts[0].shape[1]
    (out,), mark = run(
        "expert_outputs",
        functools.partial(output_body, calls, planes),
        (me, *act, *parts),
        [SCALARS] + [ANYWHERE] * (len(act) + planes),
        [jax.ShapeDtypeStruct((groups, capacity, width), BF)],
        [ANYWHERE],
        [
            pltpu.VMEM((groups * capacity, planes * hid), BF),
            pltpu.VMEM((width, planes * hid), BF),
            pltpu.VMEM((groups * capacity, width), BF),
            pltpu.SemaphoreType.DMA((planes + len(calls) + groups,)),
        ],
        after,
    )
    return out, mark


def weight_body(which, calls, *refs):
    act_in, pre_in, xt_in, gt_in = (refs[i * calls : (i + 1) * calls] for i in range(4))
    out_refs = refs[4 * calls : 4 * calls + len(which)]
    act, pre, xt, gt, stage, sem = refs[4 * calls + len(which) :]
    width, hid = xt.shape[0], act.shape[2]
    spots, total = [], 0
    for turned in xt_in:
        spots.append(pl.ds(total, turned.shape[1]))
        total += turned.shape[1]
    copies = Copies(sem)
    there, leaving = {}, []

    def fetch(n, kind):
        if n >= len(which):
            return
        lanes = pl.ds(which[n] * hid, hid)
        copies.open = []
        for i, spot in enumerate(spots):
            if n == 0:
                copies.start((xt_in, gt_in)[kind][i], (xt, gt)[kind].at[:, spot])
            source, target = ((pre_in, pre), (act_in, act))[kind]
            copies.start(source[i].at[:, lanes], target.at[n % 2, spot])
        there[n, kind], copies.open = copies.open, []

    fetch(0, 0)
    fetch(0, 1)
    for n in range(len(which)):
        for kind, (turned, units) in enumerate(((xt, pre), (gt, act))):
            for copy in there[n, kind]:
                copy.wait()
            fetch(n + 1, kind)
            spot = pl.ds(kind * width, width)
            stage[n, spot, :] = dot(turned[...], units[n % 2]).astype(stage.dtype)
            leaving.append(copies.start(stage.at[n, spot], out_refs[n].at[spot]))
    for copy in leaving:
        copy.wait()


def weight_grads(which, planes, dtype, act, pre, xt, gt, after):
    calls = len(act)
    width, rows = xt[0].shape[0], sum(turned.shape[1] for turned in xt)
    hid = act[0].shape[1] // planes
    return run(
        "weight_grads",
        functools.partial(weight_body, which, calls),
        (*act, *pre, *xt, *gt),
        [ANYWHERE] * (4 * calls),
        [jax.ShapeDtypeStruct((2 * width, hid), dtype)] * len(which),
        [ANYWHERE] * len(which),
        [
            pltpu.VMEM((2, rows, hid), BF),
            pltpu.VMEM((2, rows, hid), BF),
            pltpu.VMEM((width, rows), BF),
            pltpu.VMEM((width, rows), BF),
            pltpu.VMEM((len(which), 2 * width, hid), dtype),
            pltpu.SemaphoreType.DMA((2 * calls * (len(which) + 1) + 2 * len(which),)),
        ],
        after,
    )


def token_slots(tables, tok_count, capacity):
    len_row, _, start_row, _, far_rows, gate_rows, add_rows = tables
    count = len_row.shape[1]
    place = iota((tok_count, count), 0).astype(F32)
    inside = (place >= start_row) & (place < start_row + len_row)
    columns = []
    for far, add in zip(far_rows, add_rows):
        kept = inside & (place + add < capacity)
        columns.append(over_lanes(kept, place + (add + far * capacity + 1.0)) - 1.0)
    gates = [over_lanes(inside, row) for row in gate_rows]
    return columns, gates, inside


def backward_body(
    groups,
    capacity,
    me_ref,
    len_ref,
    task_ref,
    routes_ref,
    table_ref,
    cot_ref,
    wout_ref,
    gains_ref,
    hid_in,
    att_in,
    qkv_in,
    one_in,
    *refs,
):
    back_in = refs[:groups]
    keep_ref, send_ref, grad_out, dqkv_out = refs[groups : groups + 4]
    back, side, hid, att, qkv, one, grad_all, low, gatt, dqkv, total, sem = refs[groups + 4 :]
    copies = Copies(sem)
    for i, ref in enumerate(back_in):
        copies.start(ref, back.at[pl.ds(i * capacity, capacity)])
    copies.start(hid_in, hid)
    first, copies.open = copies.open, []
    att_there = copies.start(att_in, att)
    qkv_there = copies.start(qkv_in, qkv)
    one_there = copies.start(one_in, one)
    copies.open = []
    tok_count, width = cot_ref.shape
    me = me_ref[0]
    tables = routing(len_ref, task_ref, routes_ref, table_ref, me)
    columns, _, _ = token_slots(tables, tok_count, capacity)
    for i, column in enumerate(columns):
        side[:, i : i + 1] = column.astype(jnp.int32)
    for copy in first:
        copy.wait()
    sums = [jnp.zeros((1, width), F32)] * 3
    for step in range(tok_count // ROWS):
        rows = slice(step * ROWS, (step + 1) * ROWS)
        slots = iota((ROWS, groups * capacity), 1)
        hit = (slots == side[rows, 0:1]) | (slots == side[rows, 1:2])
        grad_two = dot(one_hot(hit), back[...])
        hat, scale = centred_of(hid[rows, :])
        grad = cot_ref[rows, :].astype(F32) + norm_back(grad_two, hat, scale, gains_ref[1:2, :])
        grad_all[rows, :] = grad
        for i, part in enumerate((grad_two * hat, grad_two, grad)):
            sums[i] = sums[i] + jnp.sum(part, axis=0, keepdims=True)
        low[rows, :] = grad.astype(BF)
        gatt[rows, :] = dot_nt(low[rows, :], wout_ref[...]).astype(BF)
    copies.start(grad_all, grad_out)
    att_there.wait()
    total[:, 3 * width : 4 * width] = dot_tn(att[...], low[...])

    qkv_there.wait()
    open_sums = [({}, {}) for _ in range(width // LANES)]
    bias_sums = {}
    spans = list(windows(len_ref, tok_count, 2 * REACH))
    for index, (rows, keys, same) in enumerate(spans):
        next_key = spans[index + 1][1].start if index + 1 < len(spans) else tok_count
        for group, lane in enumerate(range(0, width, LANES)):
            lanes = slice(lane, lane + LANES)
            key_lanes = slice(width + lane, width + lane + LANES)
            value_lanes = slice(2 * width + lane, 2 * width + lane + LANES)
            stacked, grads = split_heads(qkv[rows, lanes]), split_heads(gatt[rows, lanes])
            key_rows, value_rows = qkv[keys, key_lanes], qkv[keys, value_lanes]
            probs = softmax_of(key_rows, stacked, same)
            grad_probs = dot_nt(value_rows, grads)
            inner = jnp.sum(probs * grad_probs, axis=0, keepdims=True)
            grad_scores = (probs * (grad_probs - inner)).astype(BF)
            grad_values = dot(probs.astype(BF), grads)
            grad_keys = dot(grad_scores, stacked)
            grad_queries = join_heads(dot_tn(grad_scores, key_rows)) * HD**-0.5
            dqkv[rows, lanes] = grad_queries.astype(BF)
            for held, fresh, target in zip(
                open_sums[group], (grad_keys, grad_values), (key_lanes, value_lanes)
            ):
                for i in range(0, fresh.shape[0], REACH):
                    place = keys.start + i
                    part = fresh[i : i + REACH]
                    held[place] = held[place] + part if place in held else part
                for place in [place for place in held if place < next_key]:
                    dqkv[place : place + REACH, target] = held.pop(place).astype(BF)
    copies.start(dqkv, dqkv_out)
    ones = jnp.ones((8, tok_count), BF)
    bias = [dot(ones, dqkv[:, :width])[0:1], dot(ones, dqkv[:, 2 * width :])[0:1]]
    short = jnp.concatenate(sums + bias + [jnp.zeros((SMALL - 5, width), F32)], axis=0)
    total[:, 4 * width :] = short.T
    one_there.wait()
    total[:, : 3 * width] = dot_tn(one[...], dqkv[...])
    half, rows, _ = keep_ref.shape
    for j in range(half):
        for bit, ref in enumerate((keep_ref, send_ref)):
            owner = me ^ (2 * j + bit)
            ref[j] = total[pl.ds(pl.multiple_of(owner * rows, rows), rows), :].astype(BF)
    copies.wait()


def backward(
    capacity,
    me,
    lengths,
    seg_task,
    routes,
    gate_table,
    cotangent,
    w_out,
    gains,
    hidden,
    attended,
    qkv,
    one,
    back,
    after,
):
    tok_count, width = cotangent.shape
    groups = len(back)
    columns = 4 * width + SMALL
    pieces = jax.ShapeDtypeStruct((groups // 2, width // groups, columns), BF)
    (keep, send, grad, dqkv), mark = run(
        "backward",
        functools.partial(backward_body, groups, capacity),
        (
            me,
            lengths,
            seg_task,
            routes,
            gate_table,
            cotangent,
            w_out,
            gains,
            hidden,
            attended,
            qkv,
            one,
            *back,
        ),
        [SCALARS] + [WHOLE] * 7 + [ANYWHERE] * (4 + groups),
        [
            pieces,
            pieces,
            jax.ShapeDtypeStruct((tok_count, width), F32),
            jax.ShapeDtypeStruct((tok_count, 3 * width), BF),
        ],
        [WHOLE, WHOLE, ANYWHERE, ANYWHERE],
        [
            pltpu.VMEM((groups * capacity, width), BF),
            pltpu.VMEM((tok_count, 2), jnp.int32),
            pltpu.VMEM((tok_count, width), F32),
            pltpu.VMEM((tok_count, width), BF),
            pltpu.VMEM((tok_count, 3 * width), BF),
            pltpu.VMEM((tok_count, width), BF),
            pltpu.VMEM((tok_count, width), F32),
            pltpu.VMEM((tok_count, width), BF),
            pltpu.VMEM((tok_count, width), BF),
            pltpu.VMEM((tok_count, 3 * width), BF),
            pltpu.VMEM((width, columns), F32),
            pltpu.SemaphoreType.DMA((groups + 6,)),
        ],
        after,
    )
    return keep, send, grad, dqkv, mark


def last_body(dqkv_ref, wqkv_ref, tok_ref, grad_ref, gains_ref, out_ref, small_ref):
    tok_count, width = tok_ref.shape
    sums = [jnp.zeros((1, width), F32)] * 2
    for step in range(tok_count // ROWS):
        rows = slice(step * ROWS, (step + 1) * ROWS)
        grad_one = dot_nt(dqkv_ref[rows, :], wqkv_ref[...])
        hat, scale = centred_of(tok_ref[rows, :].astype(F32))
        back = norm_back(grad_one, hat, scale, gains_ref[0:1, :])
        out_ref[rows, :] = (grad_ref[rows, :] + back).astype(BF)
        for i, part in enumerate((grad_one * hat, grad_one)):
            sums[i] = sums[i] + jnp.sum(part, axis=0, keepdims=True)
    small_ref[...] = jnp.concatenate(sums, axis=0)


def last_back(dqkv, w_qkv, tokens, grad_hidden, gains, after):
    tok_count, width = tokens.shape
    (out, small), mark = run(
        "last_back",
        last_body,
        (dqkv, w_qkv, tokens, grad_hidden, gains),
        [WHOLE] * 5,
        [jax.ShapeDtypeStruct((tok_count, width), BF), jax.ShapeDtypeStruct((2, width), F32)],
        [WHOLE] * 2,
        (),
        after,
    )
    return out, small, mark


def finish_body(
    len_ref,
    task_ref,
    routes_ref,
    table_ref,
    cot_ref,
    hid_ref,
    back_in,
    small_ref,
    out_ref,
    short_ref,
    back,
    side_ref,
    sem,
):
    groups, capacity, _ = back_in.shape
    copies = Copies(sem)
    for i in range(groups):
        copies.start(back_in.at[i], back.at[pl.ds(i * capacity, capacity)])
    tok_count, width = cot_ref.shape
    tables = routing(len_ref, task_ref, routes_ref, table_ref, 0)
    columns, gates, inside = token_slots(tables, tok_count, capacity)
    task_col = over_lanes(inside, task_ref[...].astype(F32))
    for i, column in enumerate(columns + gates + [task_col]):
        side_ref[:, i : i + 1] = column
    copies.wait()
    gate_sums = [jnp.zeros((1, 128), F32)] * 2
    for step in range(tok_count // ROWS):
        rows = slice(step * ROWS, (step + 1) * ROWS)
        slots = iota((ROWS, groups * capacity), 1)
        side = side_ref[rows, :]
        cot = cot_ref[rows, :].astype(F32)
        mixed = hid_ref[rows, :]
        inner = jnp.zeros((ROWS, 1), F32)
        parts = []
        for r in range(2):
            hit = slots == side[:, r : r + 1].astype(jnp.int32)
            picked = dot(one_hot(hit), back[...])
            gate = side[:, 2 + r : 3 + r]
            mixed = mixed + gate * picked
            grad = jnp.sum(cot * picked, axis=1, keepdims=True)
            parts.append((gate, grad))
            inner = inner + gate * grad
        out_ref[rows, :] = mixed.astype(BF)
        task = iota((ROWS, 128), 1) == side[:, 4:5].astype(jnp.int32)
        for r, (gate, grad) in enumerate(parts):
            gate_sums[r] = gate_sums[r] + over_rows(task, gate * (grad - inner))
    wide = width // 128
    for i in range(2):
        for j in range(wide):
            short_ref[i * wide + j : i * wide + j + 1, :] = small_ref[
                i : i + 1, j * 128 : (j + 1) * 128
            ]
    short_ref[2 * wide : 2 * wide + 2, :] = jnp.concatenate(gate_sums, axis=0)


def finish(lengths, seg_task, routes, gate_table, cotangent, hidden, back, small, after):
    tok_count, width = cotangent.shape
    groups, capacity, _ = back.shape
    (out, gate), mark = run(
        "finish",
        finish_body,
        (lengths, seg_task, routes, gate_table, cotangent, hidden, back, small),
        [WHOLE] * 6 + [ANYWHERE, WHOLE],
        [
            jax.ShapeDtypeStruct((tok_count, width), BF),
            jax.ShapeDtypeStruct((2 * width // 128 + 2, 128), F32),
        ],
        [WHOLE] * 2,
        [
            pltpu.VMEM((groups * capacity, width), BF),
            pltpu.VMEM((tok_count, 8), F32),
            pltpu.SemaphoreType.DMA((groups,)),
        ],
        after,
    )
    return out, gate, mark


def swap(block, axis, distance):
    count = lax.axis_size(axis)
    return lax.ppermute(block, axis, [(s, s ^ distance) for s in range(count)])


def turn(block, axis, distance):
    count = lax.axis_size(axis)
    return lax.ppermute(block, axis, [(s, (s + distance) % count) for s in range(count)])


def powers(count):
    return [1 << i for i in range(count.bit_length() - 1)]


def add_pairs(keep, came, after):
    count, rows, columns = keep.shape

    def body(keep_ref, came_ref, *out_refs):
        for j, out_ref in enumerate(out_refs):
            out_ref[...] = (keep_ref[j].astype(F32) + came_ref[j].astype(F32)).astype(BF)

    return run(
        "add_pairs",
        body,
        (keep, came),
        [WHOLE] * 2,
        [jax.ShapeDtypeStruct((rows, columns), BF)] * count,
        [WHOLE] * count,
        (),
        after,
    )


def add_all(blocks, after):
    def body(*refs):
        total = refs[0][...].astype(F32)
        for ref in refs[1:-1]:
            total = total + ref[...].astype(F32)
        refs[-1][...] = total.astype(BF)

    (out,), mark = run(
        "add_all",
        body,
        blocks,
        [WHOLE] * len(blocks),
        [jax.ShapeDtypeStruct(blocks[0].shape, BF)],
        [WHOLE],
        (),
        after,
    )
    return out, mark


def add_part(came, own, after):
    def body(came_ref, own_ref, out_ref):
        out_ref[...] = (came_ref[...].astype(F32) + own_ref[...].astype(F32)).astype(BF)

    size = came.shape
    (out,), mark = run(
        "add_part",
        body,
        (came, own),
        [WHOLE] * 2,
        [jax.ShapeDtypeStruct(size, BF)],
        [WHOLE],
        (),
        after,
    )
    return out, mark


def last_part(came, own, after):
    width, hid = own.shape[0] // 2, own.shape[1]

    def body(*refs):
        *came_refs, own_ref, in_ref, down_ref = refs

        def total(spot):
            sums = own_ref[spot, :]
            for ref in came_refs:
                sums = sums + ref[spot, :].astype(F32)
            return sums

        in_ref[0] = total(slice(0, width))
        down_ref[0] = total(slice(width, 2 * width)).T

    return run(
        "last_part",
        body,
        (*came, own),
        [WHOLE] * (len(came) + 1),
        [jax.ShapeDtypeStruct((1, width, hid), F32), jax.ShapeDtypeStruct((1, hid, width), F32)],
        [WHOLE] * 2,
        (),
        after,
    )


def assemble(me, pieces, short, tasks, after):
    rows, columns = pieces[0].shape
    count = len(pieces)
    width = count * rows
    wide = width // 128

    def body(me_ref, short_ref, *refs):
        qkv_ref, bias_ref, out_ref, obias_ref, gains_ref, shifts_ref, gate_ref, small = refs[count:]
        for k, piece in enumerate(refs[:count]):
            owner = me_ref[0] ^ k
            spot = pl.ds(pl.multiple_of(owner * rows, rows), rows)
            qkv_ref[spot, :] = piece[:, : 3 * width].astype(F32)
            out_ref[spot, :] = piece[:, 3 * width : 4 * width].astype(F32)
            small[spot, :] = piece[:, 4 * width :].astype(F32)
        turned = small[...].T
        for i, ref in enumerate((gains_ref, shifts_ref)):
            parts = [short_ref[j : j + 1, :] for j in range(i * wide, (i + 1) * wide)]
            ref[0:1, :] = jnp.concatenate(parts, axis=1)
            ref[1:2, :] = turned[i : i + 1]
        obias_ref[...] = turned[2:3]
        bias_ref[...] = turned[3:5]
        gate_ref[...] = short_ref[2 * wide : 2 * wide + 2, :tasks]

    pair = jax.ShapeDtypeStruct((2, width), F32)
    return run(
        "assemble",
        body,
        (me, short, *pieces),
        [SCALARS] + [WHOLE] * (count + 1),
        [
            jax.ShapeDtypeStruct((width, 3 * width), F32),
            pair,
            jax.ShapeDtypeStruct((width, width), F32),
            jax.ShapeDtypeStruct((1, width), F32),
            pair,
            pair,
            jax.ShapeDtypeStruct((2, tasks), F32),
        ],
        [WHOLE] * 7,
        [pltpu.VMEM((width, columns - 4 * width), F32)],
        after,
    )


def add_small(block, axis, distance, mark, after=()):
    def body(block_ref, sent_ref, out_ref):
        out_ref[...] = block_ref[...] + sent_ref[...]

    (block,), mark = run(
        "add_small",
        body,
        (block, swap(block, axis, distance)),
        [WHOLE] * 2,
        [jax.ShapeDtypeStruct(block.shape, F32)],
        [WHOLE],
        (),
        (mark, *after),
    )
    return block, mark


def working_order(groups, capacity):
    unit = 128 // math.gcd(128, capacity)
    near = max(2, unit)
    order = sorted(range(near, groups), key=lambda k: (-k.bit_count(), k))
    half = (groups - near) // 2 // unit * unit
    return [list(range(near))[::-1] + order[:half], order[half:]]


def shards(
    tokens,
    cotangent,
    w_qkv,
    bias_qv,
    w_out,
    out_bias,
    norm_gains,
    norm_shifts,
    gate_table,
    w_in,
    w_down,
    lengths,
    seg_task,
    routes,
):
    tok_count, width = tokens.shape
    groups = lax.axis_size("expert")
    planes = lax.axis_size("hidden")
    top_count = routes.shape[1]
    capacity = 3 * top_count * tok_count // (2 * groups * w_in.shape[0])
    me = lax.axis_index("expert").astype(jnp.int32).reshape(1)
    route_args = (lengths, seg_task, routes.T, gate_table.T)

    own, mark = join_weights(w_in, w_down)
    above = [own]
    above.append(turn(above[0], "hidden", 1))
    below = above[:1]
    for _ in range((planes - 1) // 2):
        below.append(turn(below[-1], "hidden", -1))

    grad_slots, mark = dispatch_grads(capacity, groups, *route_args, cotangent, (mark,))
    grad_rows = lax.all_to_all(grad_slots, "expert", split_axis=0, concat_axis=0, tiled=True)

    qkv, attended, hidden, one, slots, mark = forward(
        capacity,
        groups,
        me,
        *route_args,
        tokens,
        w_qkv,
        bias_qv,
        w_out,
        out_bias,
        norm_gains,
        norm_shifts,
        (mark,),
    )

    calls = working_order(groups, capacity)
    rows, dx_back, kept = {0: slots[0]}, {}, []
    for ids in calls:
        for k in ids:
            if k:
                rows[k] = swap(slots[k], "expert", k)
    above[1] = hold(above[1], (mark, *below[1:2], rows[max(rows, key=int.bit_count)]))
    for _ in range(planes // 2 - 1):
        above.append(turn(above[-1], "hidden", 1))
    parts = above + below[:0:-1]

    for ids in calls:
        dxs, rest, mark = expert_rows(ids, me, [rows[k] for k in ids], grad_rows, parts, (mark,))
        kept.append(rest)
        for k, dx in zip(ids, dxs):
            dx_back[k] = swap(dx, "expert", k) if k else dx
    kept = [list(part) for part in zip(*kept)]

    middle = planes // 2
    rising, falling = list(range(middle, planes)), list(range(middle - 1, 0, -1))
    which = sorted(rising + falling, key=lambda c: abs(2 * c - planes))
    fresh, mark = weight_grads(which, planes, BF, *kept, (mark,))
    partial = dict(zip(which, fresh))
    risen = turn(partial[rising[0]], "hidden", 1)
    fallen = [turn(partial[falling[0]], "hidden", -1)] if falling else []
    out_rows, mark = expert_outputs(
        calls, groups, capacity, me, kept[0], parts, (mark,)
    )
    out_back = lax.all_to_all(out_rows, "expert", split_axis=0, concat_axis=0, tiled=True)

    keep, send, grad_hidden, dqkv, mark = backward(
        capacity,
        me,
        *route_args,
        cotangent,
        w_out,
        norm_gains,
        hidden,
        attended,
        qkv,
        one,
        [dx_back[k] for k in range(groups)],
        (mark,),
    )
    sent = swap(send, "expert", 1)
    for c in rising[1:]:
        part, mark = add_part(risen, partial[c], (mark,))
        risen = turn(part, "hidden", 1)
    for c in falling[1:]:
        part, mark = add_part(fallen[0], partial[c], (mark,))
        fallen = [turn(part, "hidden", -1)]
    mine, mark = add_pairs(keep, sent, (mark,))
    sent = [swap(mine[j], "expert", 2 * j) for j in range(1, groups // 2)]
    (whole,), mark = weight_grads(
        [0], planes, F32, *kept, (mark,)
    )
    input_grad, small_one, mark = last_back(dqkv, w_qkv, tokens, grad_hidden, norm_gains, (mark, *fallen)
    )
    total, mark = add_all([mine[0], *sent], (mark,))
    hops = powers(planes)[::-1]
    for step, distance in enumerate(hops):
        sent = swap(total, "hidden", distance)
        if step == 0:
            layer_out, short, mark = finish(
                *route_args, cotangent, hidden, out_back, small_one, (mark,)
            )
        if step == len(hops) - 1:
            for near in powers(groups):
                short, mark = add_small(short, "expert", near, mark)
        total, mark = add_all([total, sent], (mark,))
    even = [total] + [swap(total, "expert", 2 * j) for j in range(1, groups // 2)]
    for distance in hops:
        short, mark = add_small(short, "hidden", distance, mark)
    (grad_w_in, grad_w_down), mark = last_part([risen, *fallen], whole, (mark,))
    odd = [swap(piece, "expert", 1) for piece in even]
    results, mark = assemble(
        me, [piece for pair in zip(even, odd) for piece in pair], short, gate_table.shape[0], (mark,)
    )
    grad_qkv, grad_bias_qv, grad_w_out, grad_out_bias, grad_gains, grad_shifts, grad_gate = results
    return (
        layer_out,
        input_grad,
        grad_qkv,
        grad_bias_qv,
        grad_w_out,
        grad_out_bias[0],
        grad_gains,
        grad_shifts,
        grad_gate.T,
        grad_w_in,
        grad_w_down,
    )


def solution(mesh):
    split = P(("expert", "hidden"), None)
    return jax.shard_map(
        shards,
        mesh=mesh,
        in_specs=(
            split,
            split,
            P(),
            P(),
            P(),
            P(),
            P(),
            P(),
            P(),
            P("expert", None, "hidden"),
            P("expert", "hidden", None),
            split,
            split,
            P(),
        ),
        out_specs=(
            split,
            split,
            P(),
            P(),
            P(),
            P(),
            P(),
            P(),
            P(),
            P("expert", None, "hidden"),
            P("expert", "hidden", None),
        ),
        check_vma=False,
    )
```
